256 devices in a mesh: gx: 8 (over z), gy: 32 (over y, x, core).
Axes of the slice: x: 4, y: 4, z: 8, core: 2. Of those that a mesh axis runs over, the one named last changes fastest.
Arguments:
- bin_population: int32 [256, 1024], P('gy', 'gx'), may hold values from 1 to 16
- local_coordinates: float32 [3, 16, 256, 1024], P(None, None, 'gy', 'gx'), may hold values from 0 to 1
- field_tilt: float32 [2, 16, 256, 1024], P(None, None, 'gy', 'gx'), may hold values from -3.140625 to 3.140625
- body_weights: float32 [16, 256, 1024], P(None, 'gy', 'gx'), may hold values from 0.5 to 2
- thermal_conductance: float32 [16, 256, 1024], P(None, 'gy', 'gx'), may hold values from 1 to 6
- heat_storage: float32 [16, 256, 1024], P(None, 'gy', 'gx'), may hold values from 0.6 to 1.2
- thermal_level: float32 [16, 256, 1024], P(None, 'gy', 'gx'), may hold values from 0.5 to 4
- motion_vectors: float32 [3, 16, 256, 1024], P(None, None, 'gy', 'gx'), may hold values from -0.2 to 0.2
Outputs:
- heated: float32 [16, 256, 1024], P(None, 'gy', 'gx')
- moved: float32 [3, 16, 256, 1024], P(None, None, 'gy', 'gx')
The draws below stay inside these ranges and needn't reach their ends.
Inputs may be any that keep to these rules, and one draw needn't show every extreme that they name: Slots 0 to bin_population - 1 of a cell hold particles, the others are empty.
All inputs are finite; a program needn't handle non-finite values.
Results may differ from the reference program's by a relative error of at most 0.0001.
Values sent between devices are 32-bit elements; how exact they have to be, the bound alone decides.
A program may use at most 64 MiB of HBM per device.

```python
import math
import jax
import jax.numpy as jnp
from jax import lax

BODIES_PER_BIN = 16
CY = 8
SECTIONS = 4
GRID_HEIGHT = 256
GRID_WIDTH = 1024


def set_ends(array, key, smallest, high):
    shape = array.shape
    spot = [jax.random.randint(jax.random.fold_in(key, axis), (), 0, shape[axis]) for axis in range(len(shape))]
    array = array.at[tuple(spot)].set(smallest)
    longest = shape.index(max(shape))
    spot[longest] = (spot[longest] + 1) % shape[longest]
    return array.at[tuple(spot)].set(high)


def levels(stream_key, shape, cuts, least, largest):
    def one(dim, parts):
        steps = jax.random.uniform(jax.random.fold_in(jax.random.fold_in(stream_key, 6), dim), (parts,), jnp.float32, least / len(cuts), largest / len(cuts))
        return jnp.repeat(jnp.exp(steps), shape[dim] // parts).reshape((-1,) + (1,) * (len(shape) - dim - 1))

    loudness = one(*cuts[0])
    for cut in cuts[1:]:
        loudness = loudness * one(*cut)
    return loudness


def setup_inputs(seed: int = 0) -> dict:
    splits = jax.random.split(jax.random.key(seed), 9)
    bin_population = set_ends(jax.random.randint(splits[0], (GRID_HEIGHT, GRID_WIDTH), 1, BODIES_PER_BIN + 1), jax.random.fold_in(splits[0], 1), 1, BODIES_PER_BIN).astype(jnp.int32)
    local_coordinates = jnp.clip(1.0 * jax.random.uniform(splits[1], (3, BODIES_PER_BIN, GRID_HEIGHT, GRID_WIDTH), jnp.float32) ** levels(splits[1], (3, BODIES_PER_BIN, GRID_HEIGHT, GRID_WIDTH), ((2, 32), (3, 8)), -0.2, 0.2), 0.0, 1.0)
    field_tilt = jnp.clip(jax.random.uniform(splits[2], (2, BODIES_PER_BIN, GRID_HEIGHT, GRID_WIDTH), jnp.float32, -3.140625, 3.140625), -3.140625, 3.140625)
    body_weights = jnp.clip(jnp.exp(math.log(2.0) - 1.3862944 * jax.random.uniform(splits[3], (BODIES_PER_BIN, GRID_HEIGHT, GRID_WIDTH), jnp.float32) ** levels(splits[3], (BODIES_PER_BIN, GRID_HEIGHT, GRID_WIDTH), ((1, 32), (2, 8)), -0.2, 0.2)), 0.5, 2.0)
    thermal_conductance = jnp.clip(jnp.exp(math.log(6.0) - 1.7917595 * jax.random.uniform(splits[4], (BODIES_PER_BIN, GRID_HEIGHT, GRID_WIDTH), jnp.float32) ** levels(splits[4], (BODIES_PER_BIN, GRID_HEIGHT, GRID_WIDTH), ((1, 32), (2, 8)), -0.2, 0.2)), 1.0, 6.0)
    heat_storage = jnp.clip(jnp.exp(math.log(1.2) - 0.6931472 * jax.random.uniform(splits[5], (BODIES_PER_BIN, GRID_HEIGHT, GRID_WIDTH), jnp.float32) ** levels(splits[5], (BODIES_PER_BIN, GRID_HEIGHT, GRID_WIDTH), ((1, 32), (2, 8)), -0.2, 0.2)), 0.6, 1.2)
    thermal_level = jnp.clip(jnp.exp(math.log(4.0) - 2.0794415 * jax.random.uniform(splits[6], (BODIES_PER_BIN, GRID_HEIGHT, GRID_WIDTH), jnp.float32) ** levels(splits[6], (BODIES_PER_BIN, GRID_HEIGHT, GRID_WIDTH), ((1, 32), (2, 8)), -0.2, 0.2)), 0.5, 4.0)
    motion_vectors = jnp.clip(jax.random.uniform(splits[7], (3, BODIES_PER_BIN, GRID_HEIGHT, GRID_WIDTH), jnp.float32, -0.2, 0.2) * levels(splits[7], (3, BODIES_PER_BIN, GRID_HEIGHT, GRID_WIDTH), ((2, 32), (3, 8)), -0.4, 0.0), -0.2, 0.2)
    return dict(bin_population=bin_population, local_coordinates=local_coordinates, field_tilt=field_tilt, body_weights=body_weights, thermal_conductance=thermal_conductance, heat_storage=heat_storage, thermal_level=thermal_level, motion_vectors=motion_vectors)


ISO_PART = 0.1
HEAT_RATIO = 5.0 / 3.0
COURANT = 0.3
VISCOSITY = 0.5

def rkl_table(section_total):
    weight = 4.0 / (section_total * section_total + section_total - 2)
    series = [1.0 / 3.0, 1.0 / 3.0, 1.0 / 3.0]
    for section_no in range(3, section_total + 1):
        series.append((section_no * section_no + section_no - 2) / (2.0 * section_no * (section_no + 1)))
    first_tilde_weight = series[1] * weight
    coef_rows = []
    for section_no in range(2, section_total + 1):
        recursion_weight_m = (2 * section_no - 1) / section_no * series[section_no] / series[section_no - 1]
        recursion_weight_n = -(section_no - 1) / section_no * series[section_no] / series[section_no - 2]
        coef_rows.append((recursion_weight_m, recursion_weight_n, recursion_weight_m * weight, -(1.0 - series[section_no - 1]) * recursion_weight_m * weight))
    return (first_tilde_weight, coef_rows)

def expand(static):
    polar_ang = static[6]
    azimuth = static[7]
    return [static[0], static[1], static[2], static[3], static[4], static[5], jnp.sin(polar_ang) * jnp.cos(azimuth), jnp.sin(polar_ang) * jnp.sin(azimuth), jnp.cos(polar_ang)]

def separation(own_side, far_side, step_y, step_x):
    sep_x = own_side[0][:, None] - far_side[0][None, :] - float(step_x)
    sep_y = own_side[1][:, None] - far_side[1][None, :] - float(step_y)
    sep_z = own_side[2][:, None] - far_side[2][None, :]
    return (sep_x, sep_y, sep_z)

def neighbour_sum(own_side, padded, pair_term):
    rows_here = own_side[0].shape[-2]
    cols_here = own_side[0].shape[-1]
    totals = None
    for step_y in (-1, 0, 1):
        for step_x in (-1, 0, 1):
            far_side = [quantity[:, 1 + step_y:1 + step_y + rows_here, 1 + step_x:1 + step_x + cols_here] for quantity in padded]
            summands = pair_term(own_side, far_side, separation(own_side, far_side, step_y, step_x))
            summands = [lax.optimization_barrier(jnp.sum(addend, axis=1)) for addend in summands]
            totals = summands if totals is None else [running + addend for running, addend in zip(totals, summands)]
    return totals

def conduction_pair(own_side, far_side, displace):
    dist_sq = displace[0] * displace[0] + displace[1] * displace[1] + displace[2] * displace[2]
    kernel = jnp.maximum(1.0 - dist_sq, 0.0) ** 3
    along_own = own_side[6][:, None] * displace[0] + own_side[7][:, None] * displace[1] + own_side[8][:, None] * displace[2]
    along_far = far_side[6][None] * displace[0] + far_side[7][None] * displace[1] + far_side[8][None] * displace[2]
    conduct = own_side[3][:, None] * far_side[3][None] * kernel * (ISO_PART + 0.5 * (along_own * along_own + along_far * along_far))
    conduct = conduct * (0.5 * (own_side[5][:, None] + far_side[5][None]))
    return [conduct * (far_side[9][None] - own_side[9][:, None])]

def density_pair(own_side, far_side, displace):
    dist_sq = displace[0] * displace[0] + displace[1] * displace[1] + displace[2] * displace[2]
    kernel = jnp.maximum(1.0 - dist_sq, 0.0) ** 3
    return [far_side[3][None] * far_side[4][None] * kernel]

def kick_pair(own_side, far_side, displace):
    dist_sq = displace[0] * displace[0] + displace[1] * displace[1] + displace[2] * displace[2]
    soften = jnp.maximum(1.0 - dist_sq, 0.0)
    kernel = soften * soften * soften
    weight_pair = own_side[3][:, None] * far_side[3][None] * far_side[4][None]
    push = 6.0 * weight_pair * (own_side[9][:, None] + far_side[9][None]) * soften * soften
    drag = VISCOSITY * weight_pair * kernel * own_side[10][:, None] * far_side[10][None]
    return [push * displace[axis_no] + drag * (far_side[11 + axis_no][None] - own_side[11 + axis_no][:, None]) for axis_no in range(3)]

def blockwise(own_list, padded_list, pair_term):
    rows_all = own_list[0].shape[1]
    block_count = rows_all // CY

    def one_block(block_no):
        begin = block_no * CY
        own_part = [lax.dynamic_slice_in_dim(quantity, begin, CY, 1) for quantity in own_list]
        far_part = [lax.dynamic_slice_in_dim(quantity, begin, CY + 2, 1) for quantity in padded_list]
        return jnp.stack(neighbour_sum(own_part, far_part, pair_term), 0)
    stacked = lax.map(one_block, jnp.arange(block_count, dtype=jnp.int32))
    merged = jnp.transpose(stacked, (1, 2, 0, 3, 4))
    merged = merged.reshape(merged.shape[0], merged.shape[1], rows_all, merged.shape[4])
    return [merged[number] for number in range(merged.shape[0])]

def padding(quantity):
    return jnp.pad(quantity, ((0, 0), (1, 1), (1, 1)))

def reference(bin_population, local_coordinates, field_tilt, body_weights, thermal_conductance, heat_storage, thermal_level, motion_vectors):
    slots = local_coordinates.shape[1]
    live = (lax.broadcasted_iota(jnp.int32, (slots,) + bin_population.shape, 0) < bin_population[None]).astype(jnp.float32)
    static = jnp.concatenate([local_coordinates, live[None], body_weights[None], thermal_conductance[None], field_tilt], axis=0)
    own_static = expand(static)
    far_static = expand(jnp.pad(static, ((0, 0), (0, 0), (1, 1), (1, 1))))
    wave_velocity_bound = jnp.sqrt(HEAT_RATIO * (HEAT_RATIO - 1.0) * thermal_level) + jnp.sqrt(motion_vectors[0] * motion_vectors[0] + motion_vectors[1] * motion_vectors[1] + motion_vectors[2] * motion_vectors[2])
    fastest = jnp.max(live * wave_velocity_bound)
    integration_interval = COURANT / fastest

    def conductive_laplacian(field):
        summed = blockwise(own_static + [field], far_static + [padding(field)], conduction_pair)[0]
        return summed / heat_storage
    first_tilde_weight, coef_rows = rkl_table(SECTIONS)
    starting_derivative = conductive_laplacian(thermal_level)
    previous_iterate = thermal_level
    current_iterate = thermal_level + first_tilde_weight * integration_interval * starting_derivative
    for recursion_weight_m, recursion_weight_n, tilde_recursion_weight, tilde_gamma_weight in coef_rows:
        time_derivative = conductive_laplacian(current_iterate)
        next_iterate = recursion_weight_m * current_iterate + recursion_weight_n * previous_iterate + (1.0 - recursion_weight_m - recursion_weight_n) * thermal_level + tilde_recursion_weight * integration_interval * time_derivative + tilde_gamma_weight * integration_interval * starting_derivative
        previous_iterate = current_iterate
        current_iterate = next_iterate
    heated = current_iterate
    dense_sum = blockwise(own_static, far_static, density_pair)[0]
    density = 1.0 - live + live * dense_sum
    inv_rho = 1.0 / density
    press_term = (HEAT_RATIO - 1.0) * density * heated * inv_rho * inv_rho
    own_moving = [press_term, inv_rho, motion_vectors[0], motion_vectors[1], motion_vectors[2]]
    accel = blockwise(own_static + own_moving, far_static + [padding(quantity) for quantity in own_moving], kick_pair)
    moved = motion_vectors + integration_interval * jnp.stack(accel, 0)
    return (heated, moved)
```

```python
import functools

import jax
import jax.numpy as jnp
from jax import lax
from jax.experimental import pallas as pl
from jax.experimental.pallas import tpu as pltpu
from jax.sharding import PartitionSpec as P

SECTIONS = 4
ISO_PART = 0.1
HEAT_RATIO = 5.0 / 3.0
COURANT = 0.3
ROOT_HALF = 0.5**0.5
MESH = pl.DeviceIdType.MESH

SLOTS = 16
ROWS = 8
COLS = 128
FLAT = SLOTS * ROWS

X, Y, Z, BX, BY, BZ, KA, F, M, VX, VY, VZ = range(12)
QUANTITIES = 12

DIRS = ((0, 1), (1, -1), (1, 0), (1, 1))

CO, KE, WX, WY, WZ = range(5)
SELF_AT = len(DIRS) * SLOTS * SLOTS
ROW_AT = SELF_AT + SLOTS * 8
COL_AT = ROW_AT + 6 * SLOTS * 2
PAIRS = COL_AT + 12

EX_Y1, EX_G, EX_Y2, EX_Y3, EX_P = range(5)
EXCHANGES = ((EX_Y1, 2), (EX_Y2, 1), (EX_Y3, 1), (EX_P, 1))

EMPTY_Z = 10.0
OUTSIDE_Z = 20.0
EDGE_Z = 40.0

SIN = (0.9999999957157406, -0.1666665796974384, 0.008333050613415454, -0.0001980904606136566, 2.605165590448684e-06)
COS = (
    0.9999999997798981,
    -0.4999999935694129,
    0.04166663620835954,
    -0.001388836083517328,
    2.476013513307355e-05,
    -2.605106944029617e-07,
)


def rkl_table(section_total):
    weight = 4.0 / (section_total * section_total + section_total - 2)
    series = [1.0 / 3.0, 1.0 / 3.0, 1.0 / 3.0]
    for j in range(3, section_total + 1):
        series.append((j * j + j - 2) / (2.0 * j * (j + 1)))
    rows = []
    for j in range(2, section_total + 1):
        m = (2 * j - 1) / j * series[j] / series[j - 1]
        n = -(j - 1) / j * series[j] / series[j - 2]
        rows.append((m, n, m * weight, -(1.0 - series[j - 1]) * m * weight))
    return series[1] * weight, rows


def horner(coefs, t):
    total = jnp.full_like(t, coefs[-1])
    for c in coefs[-2::-1]:
        total = total * t + c
    return total


def sin_cos(angle):
    half = 0.5 * angle
    t = half * half
    s = half * horner(SIN, t)
    c = horner(COS, t)
    return 2.0 * s * c, 1.0 - 2.0 * s * s


def pair_terms(i, j):
    dx, dy, dz = i[X] - j[X], i[Y] - j[Y], i[Z] - j[Z]
    s = jnp.maximum(1.0 - (dx * dx + dy * dy + dz * dz), 0.0)
    s2 = s * s
    ke = s2 * s
    own = i[BX] * dx + i[BY] * dy + i[BZ] * dz
    far = j[BX] * dx + j[BY] * dy + j[BZ] * dz
    co = ke * (ISO_PART + (own * own + far * far)) * (i[KA] + j[KA])
    w = s2 * (i[M] * j[M])
    return co, ke, w * dx, w * dy, w * dz


def kernel(
    sizes,
    pop,
    loc,
    tilt,
    mass,
    kappa,
    cap,
    temp,
    mot,
    heated,
    moved,
    own,
    far,
    ycur,
    yprev,
    lap0,
    gfac,
    press,
    sfar,
    acc,
    accj,
    kacc,
    kaccj,
    store,
    rowsend0,
    rowrecv0,
    colsend0,
    colrecv0,
    cbsend,
    cbrecv,
    rowfar,
    colfar,
    colown,
    rsend,
    rrecv,
    vsend,
    vrecv,
    drecv,
    hs,
    cf,
    oc,
    msrc,
    mrecv,
    send_sem,
    recv_sem,
    msend_sem,
    mrecv_sem,
):
    n_gx, n_lo, n_hi = sizes
    n_gy = n_lo * n_hi
    gx = lax.axis_index("gx")
    gy = lax.axis_index("gy")
    left, right = lax.rem(gx + n_gx - 1, n_gx), lax.rem(gx + 1, n_gx)
    up, down = lax.rem(gy + n_gy - 1, n_gy), lax.rem(gy + 1, n_gy)
    lo, hi = lax.rem(gy, n_lo), lax.div(gy, n_lo)

    around = ((gx, up), (gx, down), (left, gy), (right, gy), (left, up), (right, up), (left, down), (right, down))
    stages = (
        [(lax.rem(gx + k, n_gx), gy) for k in range(1, n_gx)],
        [(gx, hi * n_lo + lax.rem(lo + k, n_lo)) for k in range(1, n_lo)],
        [(gx, lax.rem(hi + k, n_hi) * n_lo + lo) for k in range(1, n_hi)],
    )

    barrier = pltpu.get_barrier_semaphore()
    greeted = list(around) + [d for stage in stages for d in stage]
    for device in greeted:
        pl.semaphore_signal(barrier, inc=1, device_id=device, device_id_type=MESH)

    lane = lax.broadcasted_iota(jnp.int32, (ROWS, COLS), 1)
    row = lax.broadcasted_iota(jnp.int32, (ROWS, COLS), 0)
    lane16 = lax.broadcasted_iota(jnp.int32, (SLOTS, COLS), 1)
    zero = jnp.zeros((ROWS, COLS), jnp.float32)

    def at(p):
        start = p * ROWS
        return pl.ds(start if isinstance(p, int) else pl.multiple_of(start, ROWS), ROWS)

    def edge_row(side):
        return pl.ds(0 if side == 0 else ROWS - 1, SLOTS, stride=ROWS)

    def shifted(v):
        low = pltpu.roll(v, ROWS - 1, 0)
        return (pltpu.roll(v, COLS - 1, 1), pltpu.roll(low, 1, 1), low, pltpu.roll(low, COLS - 1, 1))

    def unshifted(a, b, c, d):
        return pltpu.roll(a, 1, 1) + pltpu.roll(pltpu.roll(b, COLS - 1, 1) + c + pltpu.roll(d, 1, 1), 1, 0)

    def gather(v, index):
        return jnp.take_along_axis(v, index, axis=1)

    def packed_columns(tile_of):
        v = tile_of(0)
        for p in range(1, SLOTS):
            mask = (lane == 8 * p) | (lane == 8 * p - 1)
            v = jnp.where(mask, pltpu.roll(tile_of(p), 8 * p, 1), v)
        return v

    group = lane & ~7
    within = (lane & 7) * 8
    own_index = (group, (group + (COLS - 1)) & (COLS - 1))
    far_index = (
        ((within + (COLS - 1)) & (COLS - 1), (within + 63) & (COLS - 1)),
        (within, within + 64),
    )

    def prepare(p, fastest):
        live = p < pop[...]
        sin_p, cos_p = sin_cos(tilt[0, p])
        sin_a, cos_a = sin_cos(tilt[1, p])
        t = temp[p]
        v = [mot[c, p] for c in range(3)]
        values = [
            loc[0, p],
            loc[1, p],
            jnp.where(live, loc[2, p], EMPTY_Z),
            ROOT_HALF * (sin_p * cos_a),
            ROOT_HALF * (sin_p * sin_a),
            ROOT_HALF * cos_p,
            0.5 * kappa[p],
            t,
            mass[p],
        ] + v
        for k in range(QUANTITIES):
            own[k, at(p), :] = values[k]
        speed = jnp.sqrt(HEAT_RATIO * (HEAT_RATIO - 1.0) * t) + jnp.sqrt(v[0] * v[0] + v[1] * v[1] + v[2] * v[2])
        return jnp.maximum(fastest, jnp.where(live, speed, 0.0))

    msrc[0] = lax.fori_loop(0, SLOTS, prepare, zero)

    for side in range(2):
        cb = jnp.zeros((SLOTS, COLS), jnp.float32)
        for k in range(QUANTITIES):
            packed = own[k, edge_row(side), :]
            rowsend0[side, k] = packed
            cb = jnp.where((lane16 == 2 * k) | (lane16 == 2 * k + 1), pltpu.roll(packed, 2 * k + 1, 1), cb)
        cbsend[side] = cb

    def pack_k(k, carry):
        colsend0[k] = packed_columns(lambda p: own[k, at(p), :])
        return carry

    lax.fori_loop(0, QUANTITIES, pack_k, 0)

    def remote(src, dst, s, r, device):
        return pltpu.make_async_remote_copy(
            src_ref=src, dst_ref=dst, send_sem=s, recv_sem=r, device_id=device, device_id_type=MESH
        )

    stage_at = (0, n_gx - 1, n_gx + n_lo - 2)

    def stage_copies(stage):
        return [
            remote(
                msrc.at[stage],
                mrecv.at[stage_at[stage] + k],
                msend_sem.at[stage_at[stage] + k],
                mrecv_sem.at[stage_at[stage] + k],
                device,
            )
            for k, device in enumerate(stages[stage])
        ]

    def stage_start(stage):
        for copy in stage_copies(stage):
            copy.start()

    def stage_finish(stage):
        best = msrc[stage]
        for k, copy in enumerate(stage_copies(stage)):
            copy.wait_recv()
            best = jnp.maximum(best, mrecv[stage_at[stage] + k])
        msrc[stage + 1] = best

    def opening_copies():
        plan = (
            (rowsend0.at[0], rowrecv0.at[1]),
            (rowsend0.at[1], rowrecv0.at[0]),
            (colsend0, colrecv0.at[1]),
            (colsend0, colrecv0.at[0]),
            (cbsend.at[0], cbrecv.at[3]),
            (cbsend.at[0], cbrecv.at[2]),
            (cbsend.at[1], cbrecv.at[1]),
            (cbsend.at[1], cbrecv.at[0]),
        )
        return [
            remote(src, dst, send_sem.at[0, c], recv_sem.at[0, c], around[c]) for c, (src, dst) in enumerate(plan)
        ]

    def section_copies(e):
        first, count = EXCHANGES[e - 1]
        part = pl.ds(first, count)
        plan = (
            (rsend.at[0, part], rrecv.at[1, part]),
            (rsend.at[1, part], rrecv.at[0, part]),
            (vsend.at[part], vrecv.at[1, part]),
            (vsend.at[part], vrecv.at[0, part]),
            (rsend.at[0, part], drecv.at[3, part]),
            (rsend.at[0, part], drecv.at[2, part]),
            (rsend.at[1, part], drecv.at[1, part]),
            (rsend.at[1, part], drecv.at[0, part]),
        )
        return [
            remote(src, dst, send_sem.at[e, c], recv_sem.at[e, c], around[c]) for c, (src, dst) in enumerate(plan)
        ]

    pl.semaphore_wait(barrier, len(greeted))
    for copy in opening_copies():
        copy.start()
    stage_start(0)

    def make_far(p, carry):
        for k in range(QUANTITIES):
            for d, v in enumerate(shifted(own[k, at(p), :])):
                if k == X and DIRS[d][1]:
                    v = v + float(DIRS[d][1])
                if k == Y and DIRS[d][0]:
                    v = v + float(DIRS[d][0])
                if k == Z:
                    out = None
                    for step, index, ends in ((DIRS[d][0], row, ROWS - 1), (DIRS[d][1], lane, COLS - 1)):
                        if step:
                            hit = index == (ends if step > 0 else 0)
                            out = hit if out is None else out | hit
                    v = jnp.where(out, OUTSIDE_Z, v)
                far[d, k, p] = v
        for c in range(2):
            acc[c, at(p), :] = zero
            for d in range(4):
                accj[d, c, p] = zero
        for c in range(3):
            kacc[c, at(p), :] = zero
            for d in range(4):
                kaccj[d, c, p] = zero
        return carry

    lax.fori_loop(0, SLOTS, make_far, 0)

    PASS1 = range(9)

    def put(index, terms):
        for c in range(5):
            store[c, index] = terms[c]

    def first_dirs(n, carry):
        d = lax.div(n, 8)
        p0 = lax.rem(n, 8) * 2
        mine = [[own[k, at(p0 + a), :] for k in PASS1] for a in range(2)]
        ti = [zero, zero]
        ri = [zero, zero]
        for q in range(SLOTS):
            other = [far[d, k, q] for k in PASS1]
            tj, rj = None, None
            for a in range(2):
                terms = pair_terms(mine[a], other)
                put(d * 256 + (p0 + a) * 16 + q, terms)
                t = terms[CO] * (other[F] - mine[a][F])
                ti[a] = ti[a] + t
                ri[a] = ri[a] + terms[KE] * other[M]
                r = terms[KE] * mine[a][M]
                tj = t if tj is None else tj + t
                rj = r if rj is None else rj + r
            accj[d, 0, q] = accj[d, 0, q] - tj
            accj[d, 1, q] = accj[d, 1, q] + rj
        for a in range(2):
            acc[0, at(p0 + a), :] += ti[a]
            acc[1, at(p0 + a), :] += ri[a]
        return carry

    def first_self_some(steps):
        def first_self(p, carry):
            mine = [own[k, at(p), :] for k in PASS1]
            ti, ri = zero, zero
            for step in steps:
                q = lax.rem(p + step, SLOTS)
                other = [own[k, at(q), :] for k in PASS1]
                terms = pair_terms(mine, other)
                put(SELF_AT + p * 8 + (step - 1), terms)
                t = terms[CO] * (other[F] - mine[F])
                ti = ti + t
                ri = ri + terms[KE] * other[M]
                acc[0, at(q), :] += -t
                acc[1, at(q), :] += terms[KE] * mine[M]
            acc[0, at(p), :] += ti
            acc[1, at(p), :] += ri
            return carry

        return first_self

    stage_finish(0)
    stage_start(1)
    lax.fori_loop(0, 16, first_dirs, 0)
    stage_finish(1)
    stage_start(2)
    lax.fori_loop(16, 32, first_dirs, 0)
    lax.fori_loop(0, SLOTS, first_self_some(range(1, 8)), 0)
    lax.fori_loop(0, SLOTS // 2, first_self_some((8,)), 0)
    stage_finish(2)

    for copy in opening_copies():
        copy.wait_recv()

    z_side = (jnp.where(gy == 0, EDGE_Z, 0.0), jnp.where(gy == n_gy - 1, EDGE_Z, 0.0))
    z_end = (jnp.where(gx == 0, EDGE_Z, 0.0), jnp.where(gx == n_gx - 1, EDGE_Z, 0.0))
    z_lane = jnp.where(lane16 == 0, z_end[0], 0.0), jnp.where(lane16 == COLS - 1, z_end[1], 0.0)

    for side in range(2):
        step_y = -1.0 if side == 0 else 1.0
        corner_l, corner_r = cbrecv[side * 2], cbrecv[side * 2 + 1]
        for k in PASS1:
            h = rowrecv0[side, k]
            if k == Y:
                h = h + step_y
            if k == Z:
                h = h + z_side[side]
            cl = pltpu.roll(corner_l, (COLS - 2 * k) % COLS, 1)
            cr = pltpu.roll(corner_r, (COLS - 1 - (2 * k + 1)) % COLS, 1)
            if k == Y:
                cl, cr = cl + step_y, cr + step_y
            if k == Z:
                cl, cr = cl + z_side[side], cr + z_side[side]
            hl = jnp.where(lane16 == 0, cl, pltpu.roll(h, 1, 1))
            hr = jnp.where(lane16 == COLS - 1, cr, pltpu.roll(h, COLS - 1, 1))
            if k == X:
                hl, hr = hl - 1.0, hr + 1.0
            if k == Z:
                hl, hr = hl + z_lane[0], hr + z_lane[1]
            rowfar[side * 3, k] = hl
            rowfar[side * 3 + 1, k] = h
            rowfar[side * 3 + 2, k] = hr
        for k in range(VX, VZ + 1):
            h = rowrecv0[side, k]
            cl = pltpu.roll(corner_l, (COLS - 2 * k) % COLS, 1)
            cr = pltpu.roll(corner_r, (COLS - 1 - (2 * k + 1)) % COLS, 1)
            rowfar[side * 3, k] = jnp.where(lane16 == 0, cl, pltpu.roll(h, 1, 1))
            rowfar[side * 3 + 1, k] = h
            rowfar[side * 3 + 2, k] = jnp.where(lane16 == COLS - 1, cr, pltpu.roll(h, COLS - 1, 1))

    for side in range(2):
        for k in range(QUANTITIES):
            colown[side, k] = gather(colsend0[k], own_index[side])
            for h in range(2):
                v = gather(colrecv0[side, k], far_index[side][h])
                if k == X:
                    v = v + (-1.0 if side == 0 else 1.0)
                if k == Z:
                    v = v + z_end[side]
                before, after = pltpu.roll(v, 1, 0), pltpu.roll(v, ROWS - 1, 0)
                if k == Y:
                    before, after = before - 1.0, after + 1.0
                if k == Z:
                    before = jnp.where(row == 0, OUTSIDE_Z, before)
                    after = jnp.where(row == ROWS - 1, OUTSIDE_Z, after)
                for number, value in enumerate((before, v, after)):
                    colfar[side * 6 + number * 2 + h, k] = value

    def halves(ref_at):
        return [ref_at(pl.ds(a * 8, 8)) for a in range(2)]

    def scatter_rows(target, c, side, total):
        target[c, edge_row(side), :] = target[c, edge_row(side), :] + total

    def group_sum(v):
        v = v + pltpu.roll(v, COLS - 1, 1)
        v = v + pltpu.roll(v, COLS - 2, 1)
        return v + pltpu.roll(v, COLS - 4, 1)

    ends = (lane == 0) | (lane == COLS - 1)

    def scatter_columns(target, c, total_l, total_r):
        u = jnp.where((lane & 7) == 0, group_sum(total_l), 0.0)
        u = jnp.where((lane & 7) == 7, pltpu.roll(group_sum(total_r), COLS - 1, 1), u)
        for p in range(SLOTS):
            target[c, at(p), :] += jnp.where(ends, pltpu.roll(u, (COLS - 8 * p) % COLS, 1), 0.0)

    for side in range(2):

        def first_row(number, totals):
            c = side * 3 + number
            t, r = list(totals[:2]), list(totals[2:])
            mine = [[rowsend0[side, k, pl.ds(a * 8, 8), :] for k in PASS1] for a in range(2)]
            for q in range(SLOTS):
                other = [rowfar[c, k, pl.ds(q, 1), :] for k in PASS1]
                for a in range(2):
                    terms = pair_terms(mine[a], other)
                    put(ROW_AT + (c * 16 + q) * 2 + a, terms)
                    t[a] = t[a] + terms[CO] * (other[F] - mine[a][F])
                    r[a] = r[a] + terms[KE] * other[M]
            return (*t, *r)

        t0, t1, r0, r1 = lax.fori_loop(0, 3, first_row, (zero, zero, zero, zero))
        scatter_rows(acc, 0, side, jnp.concatenate([t0, t1], axis=0))
        scatter_rows(acc, 1, side, jnp.concatenate([r0, r1], axis=0))

    column_totals = []
    for side in range(2):
        mine = [colown[side, k] for k in PASS1]

        def first_column(number, totals):
            c = side * 6 + number
            other = [colfar[c, k] for k in PASS1]
            terms = pair_terms(mine, other)
            put(COL_AT + c, terms)
            return totals[0] + terms[CO] * (other[F] - mine[F]), totals[1] + terms[KE] * other[M]

        column_totals.append(lax.fori_loop(0, 6, first_column, (zero, zero)))
    for c in range(2):
        scatter_columns(acc, c, column_totals[0][c], column_totals[1][c])

    best = msrc[3]
    for shift in (4, 2, 1):
        best = jnp.maximum(best, pltpu.roll(best, shift, 0))
    for shift in (64, 32, 16, 8, 4, 2, 1):
        best = jnp.maximum(best, pltpu.roll(best, shift, 1))
    step_dt = COURANT / best

    def total_of(target, per_dir, c, p):
        return target[c, at(p), :] + unshifted(*(per_dir[d, c, p] for d in range(4)))

    first_weight, coefs = rkl_table(SECTIONS)

    def first_update(p, carry):
        live = p < pop[...]
        start = own[F, at(p), :]
        lap = jnp.where(live, total_of(acc, accj, 0, p) / cap[p], 0.0) * step_dt
        m = own[M, at(p), :]
        density = jnp.where(live, m + total_of(acc, accj, 1, p), 1.0)
        inverse = 1.0 / density
        lap0[p] = lap
        y = start + first_weight * lap
        ycur[at(p), :] = y
        yprev[p] = start
        gfac[0, at(p), :] = ROOT_HALF * m * inverse
        press[1, at(p), :] = 6.0 * (HEAT_RATIO - 1.0) * inverse
        for d, v in enumerate(shifted(y)):
            sfar[0, d, p] = v
        for d, v in enumerate(shifted(gfac[0, at(p), :])):
            sfar[1, d, p] = v
        acc[0, at(p), :] = zero
        for d in range(4):
            accj[d, 0, p] = zero
        return carry

    lax.fori_loop(0, SLOTS, first_update, 0)

    def send(e, sources):
        first, count = EXCHANGES[e - 1]
        for n in range(count):
            tile, edge = sources[n]
            for side in range(2):
                rsend[side, first + n] = edge(side)
            vsend[first + n] = packed_columns(tile)
        for copy in section_copies(e):
            copy.start()

    def receive(e):
        for copy in section_copies(e):
            copy.wait_recv()
        first, count = EXCHANGES[e - 1]
        for n in range(first, first + count):
            for side in range(2):
                h = rrecv[side, n]
                hl, hr = drecv[side * 2, n], drecv[side * 2 + 1, n]
                hs[n, side * 3] = pltpu.roll(jnp.where(lane16 == COLS - 1, hl, h), 1, 1)
                hs[n, side * 3 + 1] = h
                hs[n, side * 3 + 2] = pltpu.roll(jnp.where(lane16 == 0, hr, h), COLS - 1, 1)
                oc[n, side] = gather(vsend[n], own_index[side])
                for half in range(2):
                    v = gather(vrecv[side, n], far_index[side][half])
                    for number, value in enumerate((pltpu.roll(v, 1, 0), v, pltpu.roll(v, ROWS - 1, 0))):
                        cf[n, side * 6 + number * 2 + half] = value

    def flat_source(ref):
        return (lambda p: ref[at(p), :]), (lambda side: ref[edge_row(side), :])

    def section_dirs(n, carry):
        d = lax.div(n, 4)
        p0 = lax.rem(n, 4) * 4
        mine = [ycur[at(p0 + a), :] for a in range(4)]
        ti = [zero] * 4
        for q in range(SLOTS):
            other = sfar[0, d, q]
            tj = None
            for a in range(4):
                t = store[CO, d * 256 + (p0 + a) * 16 + q] * (other - mine[a])
                ti[a] = ti[a] + t
                tj = t if tj is None else tj + t
            accj[d, 0, q] = accj[d, 0, q] - tj
        for a in range(4):
            acc[0, at(p0 + a), :] += ti[a]
        return carry

    def section_self_some(steps):
        def section_self(p, carry):
            mine = ycur[at(p), :]
            ti = zero
            for step in steps:
                q = lax.rem(p + step, SLOTS)
                t = store[CO, SELF_AT + p * 8 + (step - 1)] * (ycur[at(q), :] - mine)
                ti = ti + t
                acc[0, at(q), :] += -t
            acc[0, at(p), :] += ti
            return carry

        return section_self

    def section_inside():
        lax.fori_loop(0, 16, section_dirs, 0)
        lax.fori_loop(0, SLOTS, section_self_some(range(1, 8)), 0)
        lax.fori_loop(0, SLOTS // 2, section_self_some((8,)), 0)

    def section_outside(n):
        for side in range(2):
            mine = [rsend[side, n, pl.ds(a * 8, 8), :] for a in range(2)]
            t = [zero, zero]
            for number in range(3):
                c = side * 3 + number
                for q in range(SLOTS):
                    other = hs[n, c, pl.ds(q, 1), :]
                    for a in range(2):
                        t[a] = t[a] + store[CO, ROW_AT + (c * 16 + q) * 2 + a] * (other - mine[a])
            scatter_rows(acc, 0, side, jnp.concatenate(t, axis=0))
        totals = []
        for side in range(2):
            mine = oc[n, side]
            t = zero
            for number in range(6):
                c = side * 6 + number
                t = t + store[CO, COL_AT + c] * (cf[n, c] - mine)
            totals.append(t)
        scatter_columns(acc, 0, *totals)

    def section_update(coef, last):
        m, n, weight, gamma = coef

        def update(p, carry):
            live = p < pop[...]
            start = own[F, at(p), :]
            lap = jnp.where(live, total_of(acc, accj, 0, p) / cap[p], 0.0) * step_dt
            now = ycur[at(p), :]
            y = m * now + n * yprev[p] + (1.0 - m - n) * start + weight * lap + gamma * lap0[p]
            if last:
                heated[p] = y
                pr = press[1, at(p), :] * y
                press[0, at(p), :] = pr
                for d, v in enumerate(shifted(pr)):
                    sfar[0, d, p] = v
            else:
                yprev[p] = now
                ycur[at(p), :] = y
                for d, v in enumerate(shifted(y)):
                    sfar[0, d, p] = v
                acc[0, at(p), :] = zero
                for d in range(4):
                    accj[d, 0, p] = zero
            return carry

        lax.fori_loop(0, SLOTS, update, 0)

    def drag_dirs(n, carry):
        d = lax.div(n, 8)
        p0 = lax.rem(n, 8) * 2
        g = [gfac[0, at(p0 + a), :] for a in range(2)]
        v = [[own[VX + c, at(p0 + a), :] for c in range(3)] for a in range(2)]
        total = [[zero] * 3 for _ in range(2)]
        for q in range(SLOTS):
            gj = sfar[1, d, q]
            vj = [far[d, VX + c, q] for c in range(3)]
            back = [None] * 3
            for a in range(2):
                w = store[KE, d * 256 + (p0 + a) * 16 + q] * (g[a] * gj)
                for c in range(3):
                    e = w * (vj[c] - v[a][c])
                    total[a][c] = total[a][c] + e
                    back[c] = e if back[c] is None else back[c] + e
            for c in range(3):
                kaccj[d, c, q] = kaccj[d, c, q] - back[c]
        for a in range(2):
            for c in range(3):
                kacc[c, at(p0 + a), :] += total[a][c]
        return carry

    def drag_self_some(steps):
        def drag_self(p, carry):
            g = gfac[0, at(p), :]
            v = [own[VX + c, at(p), :] for c in range(3)]
            total = [zero] * 3
            for step in steps:
                q = lax.rem(p + step, SLOTS)
                w = store[KE, SELF_AT + p * 8 + (step - 1)] * (g * gfac[0, at(q), :])
                for c in range(3):
                    e = w * (own[VX + c, at(q), :] - v[c])
                    total[c] = total[c] + e
                    kacc[c, at(q), :] += -e
            for c in range(3):
                kacc[c, at(p), :] += total[c]
            return carry

        return drag_self

    def drag_outside():
        for side in range(2):
            g = [rsend[side, EX_G, pl.ds(a * 8, 8), :] for a in range(2)]
            v = [[rowsend0[side, VX + c, pl.ds(a * 8, 8), :] for c in range(3)] for a in range(2)]

            def one(number, totals):
                c = side * 3 + number
                total = list(totals)
                for q in range(SLOTS):
                    gj = hs[EX_G, c, pl.ds(q, 1), :]
                    vj = [rowfar[c, VX + x, pl.ds(q, 1), :] for x in range(3)]
                    for a in range(2):
                        w = store[KE, ROW_AT + (c * 16 + q) * 2 + a] * (g[a] * gj)
                        for x in range(3):
                            total[a * 3 + x] = total[a * 3 + x] + w * (vj[x] - v[a][x])
                return tuple(total)

            total = lax.fori_loop(0, 3, one, (zero,) * 6)
            for x in range(3):
                scatter_rows(kacc, x, side, jnp.concatenate([total[x], total[3 + x]], axis=0))
        totals = []
        for side in range(2):
            total = [zero] * 3
            for number in range(6):
                c = side * 6 + number
                w = store[KE, COL_AT + c] * (oc[EX_G, side] * cf[EX_G, c])
                for x in range(3):
                    total[x] = total[x] + w * (colfar[c, VX + x] - colown[side, VX + x])
            totals.append(total)
        for x in range(3):
            scatter_columns(kacc, x, totals[0][x], totals[1][x])

    def push_dirs(n, carry):
        d = lax.div(n, 8)
        p0 = lax.rem(n, 8) * 2
        pi = [press[0, at(p0 + a), :] for a in range(2)]
        total = [[zero] * 3 for _ in range(2)]
        for q in range(SLOTS):
            pj = sfar[0, d, q]
            back = [None] * 3
            for a in range(2):
                both = pi[a] + pj
                for c in range(3):
                    e = both * store[WX + c, d * 256 + (p0 + a) * 16 + q]
                    total[a][c] = total[a][c] + e
                    back[c] = e if back[c] is None else back[c] + e
            for c in range(3):
                kaccj[d, c, q] = kaccj[d, c, q] - back[c]
        for a in range(2):
            for c in range(3):
                kacc[c, at(p0 + a), :] += total[a][c]
        return carry

    def push_self_some(steps):
        def push_self(p, carry):
            pi = press[0, at(p), :]
            total = [zero] * 3
            for step in steps:
                q = lax.rem(p + step, SLOTS)
                both = pi + press[0, at(q), :]
                for c in range(3):
                    e = both * store[WX + c, SELF_AT + p * 8 + (step - 1)]
                    total[c] = total[c] + e
                    kacc[c, at(q), :] += -e
            for c in range(3):
                kacc[c, at(p), :] += total[c]
            return carry

        return push_self

    def push_outside():
        for side in range(2):
            pi = [rsend[side, EX_P, pl.ds(a * 8, 8), :] for a in range(2)]

            def one(number, totals):
                c = side * 3 + number
                total = list(totals)
                for q in range(SLOTS):
                    pj = hs[EX_P, c, pl.ds(q, 1), :]
                    for a in range(2):
                        both = pi[a] + pj
                        for x in range(3):
                            total[a * 3 + x] = (
                                total[a * 3 + x] + both * store[WX + x, ROW_AT + (c * 16 + q) * 2 + a]
                            )
                return tuple(total)

            total = lax.fori_loop(0, 3, one, (zero,) * 6)
            for x in range(3):
                scatter_rows(kacc, x, side, jnp.concatenate([total[x], total[3 + x]], axis=0))
        totals = []
        for side in range(2):
            total = [zero] * 3
            for number in range(6):
                c = side * 6 + number
                both = oc[EX_P, side] + cf[EX_P, c]
                for x in range(3):
                    total[x] = total[x] + both * store[WX + x, COL_AT + c]
            totals.append(total)
        for x in range(3):
            scatter_columns(kacc, x, totals[0][x], totals[1][x])

    send(1, [flat_source(ycur), flat_source(gfac.at[0])])
    section_inside()
    lax.fori_loop(0, SLOTS, drag_self_some(range(1, 8)), 0)
    lax.fori_loop(0, SLOTS // 2, drag_self_some((8,)), 0)
    lax.fori_loop(0, 8, drag_dirs, 0)
    receive(1)
    section_outside(EX_Y1)
    section_update(coefs[0], False)

    send(2, [flat_source(ycur)])
    section_inside()
    lax.fori_loop(8, 20, drag_dirs, 0)
    receive(2)
    section_outside(EX_Y2)
    section_update(coefs[1], False)

    send(3, [flat_source(ycur)])
    section_inside()
    lax.fori_loop(20, 32, drag_dirs, 0)
    drag_outside()
    receive(3)
    section_outside(EX_Y3)
    section_update(coefs[2], True)

    send(4, [flat_source(press.at[0])])
    lax.fori_loop(0, 32, push_dirs, 0)
    lax.fori_loop(0, SLOTS, push_self_some(range(1, 8)), 0)
    lax.fori_loop(0, SLOTS // 2, push_self_some((8,)), 0)
    receive(4)
    push_outside()

    def finish(p, carry):
        live = p < pop[...]
        scale = jnp.where(live, step_dt / own[M, at(p), :], 0.0)
        for c in range(3):
            moved[c, p] = own[VX + c, at(p), :] + scale * total_of(kacc, kaccj, c, p)
        return carry

    lax.fori_loop(0, SLOTS, finish, 0)

    for copy in opening_copies():
        copy.wait_send()
    for e in range(1, 5):
        for copy in section_copies(e):
            copy.wait_send()
    for stage in range(3):
        for copy in stage_copies(stage):
            copy.wait_send()


def body(sizes, *args):
    f32 = jnp.float32
    messages = sum(sizes) - 3
    tile = (SLOTS, ROWS, COLS)
    vmem = pl.BlockSpec(memory_space=pltpu.VMEM)
    scratch = [
        pltpu.VMEM((QUANTITIES, FLAT, COLS), f32),
        pltpu.VMEM((4, QUANTITIES) + tile, f32),
        pltpu.VMEM((FLAT, COLS), f32),
        pltpu.VMEM(tile, f32),
        pltpu.VMEM(tile, f32),
        pltpu.VMEM((1, FLAT, COLS), f32),
        pltpu.VMEM((2, FLAT, COLS), f32),
        pltpu.VMEM((2, 4) + tile, f32),
        pltpu.VMEM((2, FLAT, COLS), f32),
        pltpu.VMEM((4, 2) + tile, f32),
        pltpu.VMEM((3, FLAT, COLS), f32),
        pltpu.VMEM((4, 3) + tile, f32),
        pltpu.VMEM((5, PAIRS, ROWS, COLS), f32),
        pltpu.VMEM((2, QUANTITIES, SLOTS, COLS), f32),
        pltpu.VMEM((2, QUANTITIES, SLOTS, COLS), f32),
        pltpu.VMEM((QUANTITIES, ROWS, COLS), f32),
        pltpu.VMEM((2, QUANTITIES, ROWS, COLS), f32),
        pltpu.VMEM((2, SLOTS, COLS), f32),
        pltpu.VMEM((4, SLOTS, COLS), f32),
        pltpu.VMEM((6, QUANTITIES, SLOTS, COLS), f32),
        pltpu.VMEM((12, QUANTITIES, ROWS, COLS), f32),
        pltpu.VMEM((2, QUANTITIES, ROWS, COLS), f32),
        pltpu.VMEM((2, 5, SLOTS, COLS), f32),
        pltpu.VMEM((2, 5, SLOTS, COLS), f32),
        pltpu.VMEM((5, ROWS, COLS), f32),
        pltpu.VMEM((2, 5, ROWS, COLS), f32),
        pltpu.VMEM((4, 5, SLOTS, COLS), f32),
        pltpu.VMEM((5, 6, SLOTS, COLS), f32),
        pltpu.VMEM((5, 12, ROWS, COLS), f32),
        pltpu.VMEM((5, 2, ROWS, COLS), f32),
        pltpu.VMEM((4, ROWS, COLS), f32),
        pltpu.VMEM((messages, ROWS, COLS), f32),
        pltpu.SemaphoreType.DMA((5, 8)),
        pltpu.SemaphoreType.DMA((5, 8)),
        pltpu.SemaphoreType.DMA((messages,)),
        pltpu.SemaphoreType.DMA((messages,)),
    ]
    return pl.pallas_call(
        functools.partial(kernel, sizes),
        out_shape=(jax.ShapeDtypeStruct(tile, f32), jax.ShapeDtypeStruct((3,) + tile, f32)),
        in_specs=[vmem] * 8,
        out_specs=(vmem, vmem),
        scratch_shapes=scratch,
        compiler_params=pltpu.CompilerParams(
            collective_id=0, has_side_effects=True, vmem_limit_bytes=52 * 1024 * 1024
        ),
        name="sections_and_kick",
    )(*args)


def solution(mesh):
    n_gx, n_gy = mesh.shape["gx"], mesh.shape["gy"]
    n_hi = 4 if n_gy % 4 == 0 and n_gy > 4 else 2
    sizes = (n_gx, n_gy // n_hi, n_hi)
    cells = P("gy", "gx")
    one = P(None, "gy", "gx")
    many = P(None, None, "gy", "gx")
    return jax.shard_map(
        functools.partial(body, sizes),
        mesh=mesh,
        in_specs=(cells, many, many, one, one, one, one, many),
        out_specs=(one, many),
        check_vma=False,
    )
```

```python
import functools

import jax
import jax.numpy as jnp
from jax import lax
from jax.experimental import pallas as pl
from jax.experimental.pallas import tpu as pltpu
from jax.sharding import PartitionSpec as P

SECTIONS = 4
ISO_PART = 0.1
HEAT_RATIO = 5.0 / 3.0
COURANT = 0.3
ROOT_HALF = 0.5**0.5
MESH = pl.DeviceIdType.MESH

SLOTS = 16
ROWS = 8
COLS = 128
FLAT = SLOTS * ROWS

X, Y, Z, BX, BY, BZ, KA, F, M, VX, VY, VZ = range(12)
QUANTITIES = 12

DIRS = ((0, 1), (1, -1), (1, 0), (1, 1))

CO, KE, WX, WY, WZ = range(5)
SELF_AT = len(DIRS) * SLOTS * SLOTS
ROW_AT = SELF_AT + SLOTS * 8
COL_AT = ROW_AT + 6 * SLOTS * 2
PAIRS = COL_AT + 12

ROUNDS = 4
FIELD, DRAG = range(2)

EMPTY_Z = 10.0
OUTSIDE_Z = 20.0
EDGE_Z = 40.0

SIN = (0.9999999957157406, -0.1666665796974384, 0.008333050613415454, -0.0001980904606136566, 2.605165590448684e-06)
COS = (
    0.9999999997798981,
    -0.4999999935694129,
    0.04166663620835954,
    -0.001388836083517328,
    2.476013513307355e-05,
    -2.605106944029617e-07,
)


def section_polynomial(section_total):
    weight = 4.0 / (section_total * section_total + section_total - 2)
    series = [1.0 / 3.0, 1.0 / 3.0, 1.0 / 3.0]
    for j in range(3, section_total + 1):
        series.append((j * j + j - 2) / (2.0 * j * (j + 1)))

    def padded(values):
        return values + [0.0] * (section_total + 1 - len(values))

    before, now = padded([1.0]), padded([1.0, series[1] * weight])
    for j in range(2, section_total + 1):
        m = (2 * j - 1) / j * series[j] / series[j - 1]
        n = -(j - 1) / j * series[j] / series[j - 2]
        after = [m * a + n * b for a, b in zip(now, before)]
        after[0] += 1.0 - m - n
        after[1] -= (1.0 - series[j - 1]) * m * weight
        for k in range(section_total):
            after[k + 1] += m * weight * now[k]
        before, now = now, after
    return now


def horner(coefs, t):
    total = jnp.full_like(t, coefs[-1])
    for c in coefs[-2::-1]:
        total = total * t + c
    return total


def sin_cos(angle):
    half = 0.5 * angle
    t = half * half
    s = half * horner(SIN, t)
    c = horner(COS, t)
    return 2.0 * s * c, 1.0 - 2.0 * s * s


def pair_terms(i, j):
    dx, dy, dz = i[X] - j[X], i[Y] - j[Y], i[Z] - j[Z]
    s = jnp.maximum(1.0 - (dx * dx + dy * dy + dz * dz), 0.0)
    s2 = s * s
    own = i[BX] * dx + i[BY] * dy + i[BZ] * dz
    far = j[BX] * dx + j[BY] * dy + j[BZ] * dz
    co = (s2 * s) * (ISO_PART + (own * own + far * far)) * (i[KA] + j[KA])
    w = s2 * (i[M] * j[M])
    return co, w * s, w * dx, w * dy, w * dz


def kernel(
    sizes,
    pop_in,
    loc_in,
    tilt_in,
    mass_in,
    kappa_in,
    cap_in,
    temp_in,
    mot_in,
    heated,
    moved,
    pop,
    loc,
    tilt,
    mass,
    kappa,
    cap,
    temp,
    mot,
    own,
    far,
    field,
    powers,
    gfac,
    pfac,
    sfar,
    gfar,
    acc,
    accj,
    kacc,
    kaccj,
    store,
    rowsend0,
    rowrecv0,
    colsend0,
    colrecv0,
    cbsend,
    cbrecv,
    rowfar,
    colfar,
    colown,
    coltot,
    rsend,
    rrecv,
    vsend,
    vrecv,
    drecv,
    hs,
    cf,
    oc,
    msrc,
    mrecv,
    send_sem,
    recv_sem,
    msend_sem,
    mrecv_sem,
    load_sem,
):
    loads = [
        pltpu.make_async_copy(src, dst, load_sem.at[number])
        for number, (src, dst) in enumerate(
            (
                (pop_in, pop),
                (loc_in, loc),
                (tilt_in, tilt),
                (mass_in, mass),
                (kappa_in, kappa),
                (cap_in, cap),
                (temp_in, temp),
                (mot_in, mot),
            )
        )
    ]
    for load in loads:
        load.start()

    n_gx, n_lo, n_hi = sizes
    n_gy = n_lo * n_hi
    gx = lax.axis_index("gx")
    gy = lax.axis_index("gy")
    left, right = lax.rem(gx + n_gx - 1, n_gx), lax.rem(gx + 1, n_gx)
    up, down = lax.rem(gy + n_gy - 1, n_gy), lax.rem(gy + 1, n_gy)
    lo, hi = lax.rem(gy, n_lo), lax.div(gy, n_lo)

    around = ((gx, up), (gx, down), (left, gy), (right, gy), (left, up), (right, up), (left, down), (right, down))

    stage_size = (n_gx - 1, n_lo - 1, n_hi - 1)
    stage_at = (0, n_gx - 1, n_gx + n_lo - 2)

    def stage_device(stage, k):
        if stage == 0:
            return (lax.rem(gx + k + 1, n_gx), gy)
        if stage == 1:
            return (gx, hi * n_lo + lax.rem(lo + k + 1, n_lo))
        return (gx, lax.rem(hi + k + 1, n_hi) * n_lo + lo)

    def each(count, fn):
        def run(k, carry):
            fn(k)
            return carry

        lax.fori_loop(0, count, run, 0)

    barrier = pltpu.get_barrier_semaphore()

    def greet(device):
        pl.semaphore_signal(barrier, inc=1, device_id=device, device_id_type=MESH)

    for device in around:
        greet(device)
    for stage in range(3):
        each(stage_size[stage], lambda k, stage=stage: greet(stage_device(stage, k)))

    lane = lax.broadcasted_iota(jnp.int32, (ROWS, COLS), 1)
    row = lax.broadcasted_iota(jnp.int32, (ROWS, COLS), 0)
    lane16 = lax.broadcasted_iota(jnp.int32, (SLOTS, COLS), 1)
    zero = jnp.zeros((ROWS, COLS), jnp.float32)

    def at(p):
        start = p * ROWS
        return pl.ds(start if isinstance(p, int) else pl.multiple_of(start, ROWS), ROWS)

    def edge_row(side):
        return pl.ds(side * (ROWS - 1), SLOTS, stride=ROWS)

    def half(a):
        return pl.ds(a * 8, 8)

    def shifted(v):
        low = pltpu.roll(v, ROWS - 1, 0)
        return (pltpu.roll(v, COLS - 1, 1), pltpu.roll(low, 1, 1), low, pltpu.roll(low, COLS - 1, 1))

    def unshifted(a, b, c, d):
        return pltpu.roll(a, 1, 1) + pltpu.roll(pltpu.roll(b, COLS - 1, 1) + c + pltpu.roll(d, 1, 1), 1, 0)

    def gather(v, index):
        return jnp.take_along_axis(v, index, axis=1)

    def packed_columns(tile_of):
        v = tile_of(0)
        for p in range(1, SLOTS):
            mask = (lane == 8 * p) | (lane == 8 * p - 1)
            v = jnp.where(mask, pltpu.roll(tile_of(p), 8 * p, 1), v)
        return v

    group = lane & ~7
    within = (lane & 7) * 8
    own_index = (group, (group + (COLS - 1)) & (COLS - 1))
    far_index = (
        ((within + (COLS - 1)) & (COLS - 1), (within + 63) & (COLS - 1)),
        (within, within + 64),
    )

    def prepare(p, fastest):
        live = p < pop[...]
        sin_p, cos_p = sin_cos(tilt[0, p])
        sin_a, cos_a = sin_cos(tilt[1, p])
        t = temp[p]
        v = [mot[c, p] for c in range(3)]
        values = [
            loc[0, p],
            loc[1, p],
            jnp.where(live, loc[2, p], EMPTY_Z),
            ROOT_HALF * (sin_p * cos_a),
            ROOT_HALF * (sin_p * sin_a),
            ROOT_HALF * cos_p,
            0.5 * kappa[p],
            t,
            mass[p],
        ] + v
        for k in range(QUANTITIES):
            own[k, at(p), :] = values[k]
        for c in range(2):
            acc[c, at(p), :] = zero
        for c in range(3):
            kacc[c, at(p), :] = zero
        speed = jnp.sqrt(HEAT_RATIO * (HEAT_RATIO - 1.0) * t) + jnp.sqrt(v[0] * v[0] + v[1] * v[1] + v[2] * v[2])
        return jnp.maximum(fastest, jnp.where(live, speed, 0.0))

    for load in loads:
        load.wait()
    msrc[0] = lax.fori_loop(0, SLOTS, prepare, zero)

    def pack(k, cb):
        cb = list(cb)
        for side in range(2):
            packed = own[k, edge_row(side), :]
            rowsend0[side, k] = packed
            mask = (lane16 == 2 * k) | (lane16 == 2 * k + 1)
            cb[side] = jnp.where(mask, pltpu.roll(packed, 2 * k + 1, 1), cb[side])
        colsend0[k] = packed_columns(lambda p: own[k, at(p), :])
        return tuple(cb)

    blank = jnp.zeros((SLOTS, COLS), jnp.float32)
    cbsend[0], cbsend[1] = lax.fori_loop(0, QUANTITIES, pack, (blank, blank))

    def remote(src, dst, s, r, device):
        return pltpu.make_async_remote_copy(
            src_ref=src, dst_ref=dst, send_sem=s, recv_sem=r, device_id=device, device_id_type=MESH
        )

    def stage_copy(stage, k):
        slot = stage_at[stage] + k
        return remote(
            msrc.at[stage], mrecv.at[slot], msend_sem.at[slot], mrecv_sem.at[slot], stage_device(stage, k)
        )

    def stage_start(stage):
        each(stage_size[stage], lambda k: stage_copy(stage, k).start())

    def stage_finish(stage):
        def take(k, best):
            stage_copy(stage, k).wait_recv()
            return jnp.maximum(best, mrecv[stage_at[stage] + k])

        msrc[stage + 1] = lax.fori_loop(0, stage_size[stage], take, msrc[stage])

    def opening_copies():
        plan = (
            (rowsend0.at[0], rowrecv0.at[1]),
            (rowsend0.at[1], rowrecv0.at[0]),
            (colsend0, colrecv0.at[1]),
            (colsend0, colrecv0.at[0]),
            (cbsend.at[0], cbrecv.at[3]),
            (cbsend.at[0], cbrecv.at[2]),
            (cbsend.at[1], cbrecv.at[1]),
            (cbsend.at[1], cbrecv.at[0]),
        )
        return [
            remote(src, dst, send_sem.at[ROUNDS, c], recv_sem.at[ROUNDS, c], around[c])
            for c, (src, dst) in enumerate(plan)
        ]

    def round_copies(e):
        plan = (
            (rsend.at[e, 0], rrecv.at[e, 1]),
            (rsend.at[e, 1], rrecv.at[e, 0]),
            (vsend.at[e], vrecv.at[e, 1]),
            (vsend.at[e], vrecv.at[e, 0]),
            (rsend.at[e, 0], drecv.at[e, 3]),
            (rsend.at[e, 0], drecv.at[e, 2]),
            (rsend.at[e, 1], drecv.at[e, 1]),
            (rsend.at[e, 1], drecv.at[e, 0]),
        )
        return [
            remote(src, dst, send_sem.at[e, c], recv_sem.at[e, c], around[c]) for c, (src, dst) in enumerate(plan)
        ]

    pl.semaphore_wait(barrier, len(around) + sum(stage_size))
    for copy in opening_copies():
        copy.start()
    stage_start(0)

    PASS1 = range(9)

    def put(index, terms):
        for c in range(5):
            store[c, index] = terms[c]

    def first_self(p, carry):
        mine = [own[k, at(p), :] for k in PASS1]
        ti, ri = zero, zero
        for step in range(1, 9):
            q = lax.rem(p + step, SLOTS)
            other = [own[k, at(q), :] for k in PASS1]
            terms = pair_terms(mine, other)
            put(SELF_AT + p * 8 + (step - 1), terms)
            t = terms[CO] * (other[F] - mine[F])
            ti = ti + t
            ri = ri + terms[KE]
            if step < 8:
                acc[0, at(q), :] += -t
                acc[1, at(q), :] += terms[KE]
        acc[0, at(p), :] += ti
        acc[1, at(p), :] += ri
        for k in range(QUANTITIES):
            for d, v in enumerate(shifted(own[k, at(p), :])):
                if k == X and DIRS[d][1]:
                    v = v + float(DIRS[d][1])
                if k == Y and DIRS[d][0]:
                    v = v + float(DIRS[d][0])
                if k == Z:
                    out = None
                    for step, index, last in ((DIRS[d][0], row, ROWS - 1), (DIRS[d][1], lane, COLS - 1)):
                        if step:
                            hit = index == (last if step > 0 else 0)
                            out = hit if out is None else out | hit
                    v = jnp.where(out, OUTSIDE_Z, v)
                far[d, k, p] = v
        for d in range(4):
            for c in range(2):
                accj[d, c, p] = zero
            for c in range(3):
                kaccj[d, c, p] = zero
        return carry

    def first_dirs(n, carry):
        d = lax.div(n, 8)
        p0 = lax.rem(n, 8) * 2
        mine = [[own[k, at(p0 + a), :] for k in PASS1] for a in range(2)]
        ti = [zero, zero]
        ri = [zero, zero]
        for q in range(SLOTS):
            other = [far[d, k, q] for k in PASS1]
            tj, rj = None, None
            for a in range(2):
                terms = pair_terms(mine[a], other)
                put(d * 256 + (p0 + a) * 16 + q, terms)
                t, r = terms[CO] * (other[F] - mine[a][F]), terms[KE]
                ti[a] = ti[a] + t
                ri[a] = ri[a] + r
                tj = t if tj is None else tj + t
                rj = r if rj is None else rj + r
            accj[d, 0, q] = accj[d, 0, q] - tj
            accj[d, 1, q] = accj[d, 1, q] + rj
        for a in range(2):
            acc[0, at(p0 + a), :] += ti[a]
            acc[1, at(p0 + a), :] += ri[a]
        return carry

    lax.fori_loop(0, SLOTS, first_self, 0)
    lax.fori_loop(0, 32, first_dirs, 0)
    stage_finish(0)
    stage_start(1)

    for copy in opening_copies():
        copy.wait_recv()

    def rows_around(k, carry):
        for side in range(2):
            h = rowrecv0[side, k]
            cl = pltpu.roll(cbrecv[side * 2], lax.rem(COLS - 2 * k, COLS), 1)
            cr = pltpu.roll(cbrecv[side * 2 + 1], COLS - 2 - 2 * k, 1)
            rowfar[side * 3, k] = jnp.where(lane16 == 0, cl, pltpu.roll(h, 1, 1))
            rowfar[side * 3 + 1, k] = h
            rowfar[side * 3 + 2, k] = jnp.where(lane16 == COLS - 1, cr, pltpu.roll(h, COLS - 1, 1))
            colown[side, k] = gather(colsend0[k], own_index[side])
            for h in range(2):
                v = gather(colrecv0[side, k], far_index[side][h])
                for number, value in enumerate((pltpu.roll(v, 1, 0), v, pltpu.roll(v, ROWS - 1, 0))):
                    colfar[side * 6 + number * 2 + h, k] = value
        return carry

    lax.fori_loop(0, QUANTITIES, rows_around, 0)

    z_side = (jnp.where(gy == 0, EDGE_Z, 0.0), jnp.where(gy == n_gy - 1, EDGE_Z, 0.0))
    z_end = (jnp.where(gx == 0, EDGE_Z, 0.0), jnp.where(gx == n_gx - 1, EDGE_Z, 0.0))
    z_lane = (
        jnp.where(lane16 == 0, z_end[0], 0.0),
        jnp.zeros((SLOTS, COLS), jnp.float32),
        jnp.where(lane16 == COLS - 1, z_end[1], 0.0),
    )
    for side in range(2):
        for number in range(3):
            c = side * 3 + number
            if number != 1:
                rowfar[c, X] = rowfar[c, X] + float(number - 1)
            rowfar[c, Y] = rowfar[c, Y] + (-1.0 if side == 0 else 1.0)
            rowfar[c, Z] = rowfar[c, Z] + (z_lane[number] + z_side[side])
            for h in range(2):
                c = side * 6 + number * 2 + h
                colfar[c, X] = colfar[c, X] + (-1.0 if side == 0 else 1.0)
                z = colfar[c, Z] + z_end[side]
                if number != 1:
                    colfar[c, Y] = colfar[c, Y] + float(number - 1)
                    z = jnp.where(row == (0 if number == 0 else ROWS - 1), OUTSIDE_Z, z)
                colfar[c, Z] = z

    def scatter_rows(target, c, side, halves):
        target[c, edge_row(side), :] = target[c, edge_row(side), :] + jnp.concatenate(halves, axis=0)

    def group_sum(v):
        v = v + pltpu.roll(v, COLS - 1, 1)
        v = v + pltpu.roll(v, COLS - 2, 1)
        return v + pltpu.roll(v, COLS - 4, 1)

    ends = (lane == 0) | (lane == COLS - 1)

    def scatter_columns(target, count):
        combined = []
        for c in range(count):
            u = jnp.where((lane & 7) == 0, group_sum(coltot[0, c]), 0.0)
            combined.append(jnp.where((lane & 7) == 7, pltpu.roll(group_sum(coltot[1, c]), COLS - 1, 1), u))

        def add(p):
            for c in range(count):
                v = pltpu.roll(combined[c], lax.rem(COLS - 8 * p, COLS), 1)
                target[c, at(p), :] += jnp.where(ends, v, 0.0)

        each(SLOTS, add)

    def rim(target, count, row_mine, row_terms, col_mine, col_terms):
        def one_side(side):
            mine = row_mine(side)

            def one_row(number, totals):
                total = list(totals)
                c = side * 3 + number
                for q in range(SLOTS):
                    add = row_terms(c, q, mine)
                    for a in range(2):
                        for x, e in enumerate(add(a, ROW_AT + (c * 16 + q) * 2 + a)):
                            total[a * count + x] = total[a * count + x] + e
                return tuple(total)

            total = lax.fori_loop(0, 3, one_row, (zero,) * (2 * count))
            for x in range(count):
                scatter_rows(target, x, side, [total[x], total[count + x]])

            mine_col = col_mine(side)

            def one_column(number, totals):
                c = side * 6 + number
                return tuple(t + e for t, e in zip(totals, col_terms(c, mine_col, COL_AT + c)))

            total = lax.fori_loop(0, 6, one_column, (zero,) * count)
            for x in range(count):
                coltot[side, x] = total[x]

        each(2, one_side)
        scatter_columns(target, count)

    def first_terms(mine, other, index):
        terms = pair_terms(mine, other)
        put(index, terms)
        return terms[CO] * (other[F] - mine[F]), terms[KE]

    def first_row(c, q, mine):
        other = [rowfar[c, k, pl.ds(q, 1), :] for k in PASS1]
        return lambda a, index: first_terms(mine[a], other, index)

    rim(
        acc,
        2,
        lambda side: [[rowsend0[side, k, half(a), :] for k in PASS1] for a in range(2)],
        first_row,
        lambda side: [colown[side, k] for k in PASS1],
        lambda c, mine, index: first_terms(mine, [colfar[c, k] for k in PASS1], index),
    )
    stage_finish(1)
    stage_start(2)

    def total_of(target, per_dir, c, p):
        return target[c, at(p), :] + unshifted(*(per_dir[d, c, p] for d in range(4)))

    def set_field(p, value):
        field[at(p), :] = value
        for d, v in enumerate(shifted(value)):
            sfar[d, p] = v
        acc[0, at(p), :] = zero
        for d in range(4):
            accj[d, 0, p] = zero

    def first_update(p):
        live = p < pop[...]
        m = own[M, at(p), :]
        density = jnp.where(live, m + total_of(acc, accj, 1, p) / m, 1.0)
        inverse = 1.0 / density
        g = ROOT_HALF * inverse
        gfac[at(p), :] = g
        for d, v in enumerate(shifted(g)):
            gfar[d, p] = v
        pfac[p] = 6.0 * (HEAT_RATIO - 1.0) * inverse
        u = jnp.where(live, total_of(acc, accj, 0, p) / cap[p], 0.0)
        powers[0, p] = u
        set_field(p, u)

    each(SLOTS, first_update)

    def section_dirs(n, carry):
        d = lax.div(n, 4)
        p0 = lax.rem(n, 4) * 4
        mine = [field[at(p0 + a), :] for a in range(4)]
        ti = [zero] * 4
        for q in range(SLOTS):
            other = sfar[d, q]
            tj = None
            for a in range(4):
                t = store[CO, d * 256 + (p0 + a) * 16 + q] * (other - mine[a])
                ti[a] = ti[a] + t
                tj = t if tj is None else tj + t
            accj[d, 0, q] = accj[d, 0, q] - tj
        for a in range(4):
            acc[0, at(p0 + a), :] += ti[a]
        return carry

    def self_partners(p):
        for step in range(1, 9):
            yield lax.rem(p + step, SLOTS), SELF_AT + p * 8 + (step - 1), False
        for step in range(1, 8):
            q = lax.rem(p + SLOTS - step, SLOTS)
            yield q, SELF_AT + q * 8 + (step - 1), True

    def section_self(p):
        mine = field[at(p), :]
        ti = zero
        for q, index, _ in self_partners(p):
            ti = ti + store[CO, index] * (field[at(q), :] - mine)
        acc[0, at(p), :] += ti

    def section_row(c, q, mine):
        other = hs[FIELD, c, pl.ds(q, 1), :]
        return lambda a, index: (store[CO, index] * (other - mine[a]),)

    def drag_dirs(n, carry):
        d = lax.div(n, 8)
        p0 = lax.rem(n, 8) * 2
        g = [gfac[at(p0 + a), :] for a in range(2)]
        v = [[own[VX + c, at(p0 + a), :] for c in range(3)] for a in range(2)]
        total = [[zero] * 3 for _ in range(2)]
        for q in range(SLOTS):
            gj = gfar[d, q]
            vj = [far[d, VX + c, q] for c in range(3)]
            back = [None] * 3
            for a in range(2):
                w = store[KE, d * 256 + (p0 + a) * 16 + q] * (g[a] * gj)
                for c in range(3):
                    e = w * (vj[c] - v[a][c])
                    total[a][c] = total[a][c] + e
                    back[c] = e if back[c] is None else back[c] + e
            for c in range(3):
                kaccj[d, c, q] = kaccj[d, c, q] - back[c]
        for a in range(2):
            for c in range(3):
                kacc[c, at(p0 + a), :] += total[a][c]
        return carry

    def drag_self(p):
        g = gfac[at(p), :]
        v = [own[VX + c, at(p), :] for c in range(3)]
        total = [zero] * 3
        for q, index, _ in self_partners(p):
            w = store[KE, index] * (g * gfac[at(q), :])
            for c in range(3):
                total[c] = total[c] + w * (own[VX + c, at(q), :] - v[c])
        for c in range(3):
            kacc[c, at(p), :] += total[c]

    def drag_row(c, q, mine):
        g, v = mine
        gj = hs[DRAG, c, pl.ds(q, 1), :]
        vj = [rowfar[c, VX + x, pl.ds(q, 1), :] for x in range(3)]

        def terms(a, index):
            w = store[KE, index] * (g[a] * gj)
            return [w * (vj[x] - v[a][x]) for x in range(3)]

        return terms

    def drag_column(c, mine, index):
        g, v = mine
        w = store[KE, index] * (g * cf[DRAG, c])
        return [w * (colfar[c, VX + x] - v[x]) for x in range(3)]

    def drag_rim():
        rim(
            kacc,
            3,
            lambda side: (
                [rsend[0, side, DRAG, half(a), :] for a in range(2)],
                [[rowsend0[side, VX + x, half(a), :] for x in range(3)] for a in range(2)],
            ),
            drag_row,
            lambda side: (oc[DRAG, side], [colown[side, VX + x] for x in range(3)]),
            drag_column,
        )

    def push_dirs(n, carry):
        d = lax.div(n, 8)
        p0 = lax.rem(n, 8) * 2
        pi = [field[at(p0 + a), :] for a in range(2)]
        total = [[zero] * 3 for _ in range(2)]
        for q in range(SLOTS):
            pj = sfar[d, q]
            back = [None] * 3
            for a in range(2):
                both = pi[a] + pj
                for c in range(3):
                    e = both * store[WX + c, d * 256 + (p0 + a) * 16 + q]
                    total[a][c] = total[a][c] + e
                    back[c] = e if back[c] is None else back[c] + e
            for c in range(3):
                kaccj[d, c, q] = kaccj[d, c, q] - back[c]
        for a in range(2):
            for c in range(3):
                kacc[c, at(p0 + a), :] += total[a][c]
        return carry

    def push_self(p):
        pi = field[at(p), :]
        total = [zero] * 3
        for q, index, reverse in self_partners(p):
            both = pi + field[at(q), :]
            for c in range(3):
                e = both * store[WX + c, index]
                total[c] = total[c] - e if reverse else total[c] + e
        for c in range(3):
            kacc[c, at(p), :] += total[c]

    def push_row(c, q, mine):
        pj = hs[FIELD, c, pl.ds(q, 1), :]

        def terms(a, index):
            both = mine[a] + pj
            return [both * store[WX + x, index] for x in range(3)]

        return terms

    def push_column(c, mine, index):
        both = mine + cf[FIELD, c]
        return [both * store[WX + x, index] for x in range(3)]

    for side in range(2):
        packed = gfac[edge_row(side), :]
        for e in range(ROUNDS):
            rsend[e, side, DRAG] = packed
    packed = packed_columns(lambda p: gfac[at(p), :])
    for e in range(ROUNDS):
        vsend[e, DRAG] = packed

    polynomial = section_polynomial(SECTIONS)

    def spread(e, kind):
        for side in range(2):
            h = rrecv[e, side, kind]
            hl, hr = drecv[e, side * 2, kind], drecv[e, side * 2 + 1, kind]
            hs[kind, side * 3] = pltpu.roll(jnp.where(lane16 == COLS - 1, hl, h), 1, 1)
            hs[kind, side * 3 + 1] = h
            hs[kind, side * 3 + 2] = pltpu.roll(jnp.where(lane16 == 0, hr, h), COLS - 1, 1)
            oc[kind, side] = gather(vsend[e, kind], own_index[side])
            for h in range(2):
                v = gather(vrecv[e, side, kind], far_index[side][h])
                for number, value in enumerate((pltpu.roll(v, 1, 0), v, pltpu.roll(v, ROWS - 1, 0))):
                    cf[kind, side * 6 + number * 2 + h] = value

    def one_round(e):
        for side in range(2):
            rsend[e, side, FIELD] = field[edge_row(side), :]
        vsend[e, FIELD] = packed_columns(lambda p: field[at(p), :])
        for copy in round_copies(e):
            copy.start()

        @pl.when(e < 3)
        def _():
            lax.fori_loop(0, 16, section_dirs, 0)
            each(SLOTS, section_self)

        @pl.when(e == 0)
        def _():
            each(SLOTS, drag_self)

        @pl.when(e == 2)
        def _():
            drag_rim()

        lax.fori_loop(jnp.minimum(e * 11, 32), jnp.minimum(e * 11 + 11, 32), drag_dirs, 0)

        @pl.when(e == 3)
        def _():
            lax.fori_loop(0, 32, push_dirs, 0)
            each(SLOTS, push_self)

        for copy in round_copies(e):
            copy.wait_recv()
        each(jnp.where(e == 0, 2, 1), lambda kind: spread(e, kind))

        @pl.when(e < 3)
        def _():
            rim(
                acc,
                1,
                lambda side: [rsend[e, side, FIELD, half(a), :] for a in range(2)],
                section_row,
                lambda side: oc[FIELD, side],
                lambda c, mine, index: (store[CO, index] * (cf[FIELD, c] - mine),),
            )

        def power(p):
            return jnp.where(p < pop[...], total_of(acc, accj, 0, p) / cap[p], 0.0)

        @pl.when(e < 2)
        def _():
            def update(p):
                u = power(p)
                powers[e + 1, p] = u
                set_field(p, u)

            each(SLOTS, update)

        @pl.when(e == 2)
        def _():
            stage_finish(2)
            best = msrc[3]
            for shift in (4, 2, 1):
                best = jnp.maximum(best, pltpu.roll(best, shift, 0))
            for shift in (64, 32, 16, 8, 4, 2, 1):
                best = jnp.maximum(best, pltpu.roll(best, shift, 1))
            step_dt = COURANT / best
            msrc[4] = step_dt

            def update(p):
                y = step_dt * (polynomial[4] * power(p))
                for k in (3, 2, 1):
                    y = step_dt * (polynomial[k] * powers[k - 1, p] + y)
                y = polynomial[0] * own[F, at(p), :] + y
                heated[p] = y
                set_field(p, pfac[p] * y)

            each(SLOTS, update)

        @pl.when(e == 3)
        def _():
            rim(
                kacc,
                3,
                lambda side: [rsend[e, side, FIELD, half(a), :] for a in range(2)],
                push_row,
                lambda side: oc[FIELD, side],
                push_column,
            )

    each(ROUNDS, one_round)

    def finish(p):
        live = p < pop[...]
        scale = jnp.where(live, msrc[4] / own[M, at(p), :], 0.0)
        for c in range(3):
            moved[c, p] = own[VX + c, at(p), :] + scale * total_of(kacc, kaccj, c, p)

    each(SLOTS, finish)

    for copy in opening_copies():
        copy.wait_send()

    def sent(e):
        for copy in round_copies(e):
            copy.wait_send()

    each(ROUNDS, sent)
    for stage in range(3):
        each(stage_size[stage], lambda k, stage=stage: stage_copy(stage, k).wait_send())


def body(sizes, *args):
    f32 = jnp.float32
    messages = sum(sizes) - 3
    tile = (SLOTS, ROWS, COLS)
    vmem = pl.BlockSpec(memory_space=pltpu.VMEM)
    scratch = [pltpu.VMEM(a.shape, a.dtype) for a in args] + [
        pltpu.VMEM((QUANTITIES, FLAT, COLS), f32),
        pltpu.VMEM((4, QUANTITIES) + tile, f32),
        pltpu.VMEM((FLAT, COLS), f32),
        pltpu.VMEM((3,) + tile, f32),
        pltpu.VMEM((FLAT, COLS), f32),
        pltpu.VMEM(tile, f32),
        pltpu.VMEM((4,) + tile, f32),
        pltpu.VMEM((4,) + tile, f32),
        pltpu.VMEM((2, FLAT, COLS), f32),
        pltpu.VMEM((4, 2) + tile, f32),
        pltpu.VMEM((3, FLAT, COLS), f32),
        pltpu.VMEM((4, 3) + tile, f32),
        pltpu.VMEM((5, PAIRS, ROWS, COLS), f32),
        pltpu.VMEM((2, QUANTITIES, SLOTS, COLS), f32),
        pltpu.VMEM((2, QUANTITIES, SLOTS, COLS), f32),
        pltpu.VMEM((QUANTITIES, ROWS, COLS), f32),
        pltpu.VMEM((2, QUANTITIES, ROWS, COLS), f32),
        pltpu.VMEM((2, SLOTS, COLS), f32),
        pltpu.VMEM((4, SLOTS, COLS), f32),
        pltpu.VMEM((6, QUANTITIES, SLOTS, COLS), f32),
        pltpu.VMEM((12, QUANTITIES, ROWS, COLS), f32),
        pltpu.VMEM((2, QUANTITIES, ROWS, COLS), f32),
        pltpu.VMEM((2, 3, ROWS, COLS), f32),
        pltpu.VMEM((ROUNDS, 2, 2, SLOTS, COLS), f32),
        pltpu.VMEM((ROUNDS, 2, 2, SLOTS, COLS), f32),
        pltpu.VMEM((ROUNDS, 2, ROWS, COLS), f32),
        pltpu.VMEM((ROUNDS, 2, 2, ROWS, COLS), f32),
        pltpu.VMEM((ROUNDS, 4, 2, SLOTS, COLS), f32),
        pltpu.VMEM((2, 6, SLOTS, COLS), f32),
        pltpu.VMEM((2, 12, ROWS, COLS), f32),
        pltpu.VMEM((2, 2, ROWS, COLS), f32),
        pltpu.VMEM((5, ROWS, COLS), f32),
        pltpu.VMEM((messages, ROWS, COLS), f32),
        pltpu.SemaphoreType.DMA((ROUNDS + 1, 8)),
        pltpu.SemaphoreType.DMA((ROUNDS + 1, 8)),
        pltpu.SemaphoreType.DMA((messages,)),
        pltpu.SemaphoreType.DMA((messages,)),
        pltpu.SemaphoreType.DMA((8,)),
    ]
    return pl.pallas_call(
        functools.partial(kernel, sizes),
        out_shape=(jax.ShapeDtypeStruct(tile, f32), jax.ShapeDtypeStruct((3,) + tile, f32)),
        in_specs=[pl.BlockSpec(memory_space=pl.ANY)] * 8,
        out_specs=(vmem, vmem),
        scratch_shapes=scratch,
        compiler_params=pltpu.CompilerParams(
            collective_id=0, has_side_effects=True, vmem_limit_bytes=60 * 1024 * 1024
        ),
        name="sections_and_kick",
    )(*args)


def solution(mesh):
    n_gx, n_gy = mesh.shape["gx"], mesh.shape["gy"]
    n_hi = 4 if n_gy % 4 == 0 and n_gy > 4 else 2
    sizes = (n_gx, n_gy // n_hi, n_hi)
    cells = P("gy", "gx")
    one = P(None, "gy", "gx")
    many = P(None, None, "gy", "gx")
    return jax.shard_map(
        functools.partial(body, sizes),
        mesh=mesh,
        in_specs=(cells, many, many, one, one, one, one, many),
        out_specs=(one, many),
        check_vma=False,
    )
```

```python
import functools

import jax
import jax.numpy as jnp
from jax import lax
from jax.experimental import pallas as pl
from jax.experimental.pallas import tpu as pltpu
from jax.sharding import PartitionSpec as P

SECTIONS = 4
ISO_PART = 0.1
HEAT_RATIO = 5.0 / 3.0
COURANT = 0.3
ROOT_HALF = 0.5**0.5
MESH = pl.DeviceIdType.MESH

SLOTS = 16
ROWS = 8
COLS = 128
FLAT = SLOTS * ROWS

X, Y, Z, BX, BY, BZ, KA, F, M, VX, VY, VZ = range(12)
QUANTITIES = 12

DIRS = ((0, 1), (1, -1), (1, 0), (1, 1))

CO, KE, WX, WY, WZ = range(5)
SELF_AT = len(DIRS) * SLOTS * SLOTS
ROW_AT = SELF_AT + SLOTS * 8
COL_AT = ROW_AT + 6 * SLOTS * 2
PAIRS = COL_AT + 12

ROUNDS = 4
FIELD, DRAG = range(2)

EMPTY_Z = 10.0
OUTSIDE_Z = 20.0
EDGE_Z = 40.0

SIN = (0.9999999957157406, -0.1666665796974384, 0.008333050613415454, -0.0001980904606136566, 2.605165590448684e-06)
COS = (
    0.9999999997798981,
    -0.4999999935694129,
    0.04166663620835954,
    -0.001388836083517328,
    2.476013513307355e-05,
    -2.605106944029617e-07,
)


def section_polynomial(section_total):
    weight = 4.0 / (section_total * section_total + section_total - 2)
    series = [1.0 / 3.0, 1.0 / 3.0, 1.0 / 3.0]
    for j in range(3, section_total + 1):
        series.append((j * j + j - 2) / (2.0 * j * (j + 1)))

    def padded(values):
        return values + [0.0] * (section_total + 1 - len(values))

    before, now = padded([1.0]), padded([1.0, series[1] * weight])
    for j in range(2, section_total + 1):
        m = (2 * j - 1) / j * series[j] / series[j - 1]
        n = -(j - 1) / j * series[j] / series[j - 2]
        after = [m * a + n * b for a, b in zip(now, before)]
        after[0] += 1.0 - m - n
        after[1] -= (1.0 - series[j - 1]) * m * weight
        for k in range(section_total):
            after[k + 1] += m * weight * now[k]
        before, now = now, after
    return now


def horner(coefs, t):
    total = jnp.full_like(t, coefs[-1])
    for c in coefs[-2::-1]:
        total = total * t + c
    return total


def sin_cos(angle):
    half = 0.5 * angle
    t = half * half
    s = half * horner(SIN, t)
    c = horner(COS, t)
    return 2.0 * s * c, 1.0 - 2.0 * s * s


def pair_terms(i, j):
    dx, dy, dz = i[X] - j[X], i[Y] - j[Y], i[Z] - j[Z]
    s = jnp.maximum(1.0 - (dx * dx + dy * dy + dz * dz), 0.0)
    s2 = s * s
    own = i[BX] * dx + i[BY] * dy + i[BZ] * dz
    far = j[BX] * dx + j[BY] * dy + j[BZ] * dz
    co = (s2 * s) * (ISO_PART + (own * own + far * far)) * (i[KA] + j[KA])
    w = s2 * (i[M] * j[M])
    return co, w * s, w * dx, w * dy, w * dz


def kernel(
    sizes,
    pop_in,
    loc_in,
    tilt_in,
    mass_in,
    kappa_in,
    cap_in,
    temp_in,
    mot_in,
    heated,
    moved,
    pop,
    loc,
    tilt,
    mass,
    kappa,
    cap,
    temp,
    mot,
    own,
    far,
    field,
    powers,
    gfac,
    pfac,
    sfar,
    gfar,
    acc,
    accj,
    kacc,
    kaccj,
    store,
    rowsend0,
    rowrecv0,
    colsend0,
    colrecv0,
    cbsend,
    cbrecv,
    rowfar,
    colfar,
    colown,
    coltot,
    rsend,
    rrecv,
    vsend,
    vrecv,
    drecv,
    hs,
    cf,
    oc,
    msrc,
    mrecv,
    send_sem,
    recv_sem,
    msend_sem,
    mrecv_sem,
    load_sem,
):
    loads = [
        pltpu.make_async_copy(src, dst, load_sem.at[number])
        for number, (src, dst) in enumerate(
            (
                (pop_in, pop),
                (loc_in, loc),
                (tilt_in, tilt),
                (mass_in, mass),
                (kappa_in, kappa),
                (cap_in, cap),
                (temp_in, temp),
                (mot_in, mot),
            )
        )
    ]
    for load in loads:
        load.start()

    n_gx, n_lo, n_hi = sizes
    n_gy = n_lo * n_hi
    gx = lax.axis_index("gx")
    gy = lax.axis_index("gy")
    left, right = lax.rem(gx + n_gx - 1, n_gx), lax.rem(gx + 1, n_gx)
    up, down = lax.rem(gy + n_gy - 1, n_gy), lax.rem(gy + 1, n_gy)
    lo, hi = lax.rem(gy, n_lo), lax.div(gy, n_lo)

    around = ((gx, up), (gx, down), (left, gy), (right, gy), (left, up), (right, up), (left, down), (right, down))

    stage_size = (n_gx - 1, n_lo - 1, n_hi - 1)
    stage_at = (0, n_gx - 1, n_gx + n_lo - 2)

    def stage_device(stage, k):
        if stage == 0:
            return (lax.rem(gx + k + 1, n_gx), gy)
        if stage == 1:
            return (gx, hi * n_lo + lax.rem(lo + k + 1, n_lo))
        return (gx, lax.rem(hi + k + 1, n_hi) * n_lo + lo)

    def each(count, fn):
        def run(k, carry):
            fn(k)
            return carry

        lax.fori_loop(0, count, run, 0)

    def grouped(count, size, fn, carry):
        def run(k, carry):
            for a in range(size):
                carry = fn(k * size + a, carry)
            return carry

        return lax.fori_loop(0, count // size, run, carry)

    barrier = pltpu.get_barrier_semaphore()

    def greet(device):
        pl.semaphore_signal(barrier, inc=1, device_id=device, device_id_type=MESH)

    for device in around:
        greet(device)
    for stage in range(3):
        each(stage_size[stage], lambda k, stage=stage: greet(stage_device(stage, k)))

    lane = lax.broadcasted_iota(jnp.int32, (ROWS, COLS), 1)
    row = lax.broadcasted_iota(jnp.int32, (ROWS, COLS), 0)
    lane16 = lax.broadcasted_iota(jnp.int32, (SLOTS, COLS), 1)
    zero = jnp.zeros((ROWS, COLS), jnp.float32)

    def at(p):
        start = p * ROWS
        return pl.ds(start if isinstance(p, int) else pl.multiple_of(start, ROWS), ROWS)

    def edge_row(side):
        return pl.ds(side * (ROWS - 1), SLOTS, stride=ROWS)

    def half(a):
        return pl.ds(a * 8, 8)

    def shifted(v):
        low = pltpu.roll(v, ROWS - 1, 0)
        return (pltpu.roll(v, COLS - 1, 1), pltpu.roll(low, 1, 1), low, pltpu.roll(low, COLS - 1, 1))

    def unshifted(a, b, c, d):
        return pltpu.roll(a, 1, 1) + pltpu.roll(pltpu.roll(b, COLS - 1, 1) + c + pltpu.roll(d, 1, 1), 1, 0)

    def gather(v, index):
        return jnp.take_along_axis(v, index, axis=1)

    def packed_columns(tile_of):
        v = tile_of(0)
        for p in range(1, SLOTS):
            mask = (lane == 8 * p) | (lane == 8 * p - 1)
            v = jnp.where(mask, pltpu.roll(tile_of(p), 8 * p, 1), v)
        return v

    group = lane & ~7
    within = (lane & 7) * 8
    own_index = (group, (group + (COLS - 1)) & (COLS - 1))
    far_index = (
        ((within + (COLS - 1)) & (COLS - 1), (within + 63) & (COLS - 1)),
        (within, within + 64),
    )

    def prepare(p, fastest):
        live = p < pop[...]
        sin_p, cos_p = sin_cos(tilt[0, p])
        sin_a, cos_a = sin_cos(tilt[1, p])
        t = temp[p]
        v = [mot[c, p] for c in range(3)]
        values = [
            loc[0, p],
            loc[1, p],
            jnp.where(live, loc[2, p], EMPTY_Z),
            ROOT_HALF * (sin_p * cos_a),
            ROOT_HALF * (sin_p * sin_a),
            ROOT_HALF * cos_p,
            0.5 * kappa[p],
            t,
            mass[p],
        ] + v
        for k in range(QUANTITIES):
            own[k, at(p), :] = values[k]
        for c in range(2):
            acc[c, at(p), :] = zero
        for c in range(3):
            kacc[c, at(p), :] = zero
        speed = jnp.sqrt(HEAT_RATIO * (HEAT_RATIO - 1.0) * t) + jnp.sqrt(v[0] * v[0] + v[1] * v[1] + v[2] * v[2])
        return jnp.maximum(fastest, jnp.where(live, speed, 0.0))

    for load in loads:
        load.wait()
    msrc[0] = grouped(SLOTS, 4, prepare, zero)

    def pack(k, cb):
        cb = list(cb)
        for side in range(2):
            packed = own[k, edge_row(side), :]
            rowsend0[side, k] = packed
            mask = (lane16 == 2 * k) | (lane16 == 2 * k + 1)
            cb[side] = jnp.where(mask, pltpu.roll(packed, 2 * k + 1, 1), cb[side])
        colsend0[k] = packed_columns(lambda p: own[k, at(p), :])
        return tuple(cb)

    blank = jnp.zeros((SLOTS, COLS), jnp.float32)
    cbsend[0], cbsend[1] = grouped(QUANTITIES, 3, pack, (blank, blank))

    def remote(src, dst, s, r, device):
        return pltpu.make_async_remote_copy(
            src_ref=src, dst_ref=dst, send_sem=s, recv_sem=r, device_id=device, device_id_type=MESH
        )

    def stage_copy(stage, k):
        slot = stage_at[stage] + k
        return remote(
            msrc.at[stage], mrecv.at[slot], msend_sem.at[slot], mrecv_sem.at[slot], stage_device(stage, k)
        )

    def stage_start(stage):
        each(stage_size[stage], lambda k: stage_copy(stage, k).start())

    def stage_finish(stage):
        def take(k, best):
            stage_copy(stage, k).wait_recv()
            return jnp.maximum(best, mrecv[stage_at[stage] + k])

        msrc[stage + 1] = lax.fori_loop(0, stage_size[stage], take, msrc[stage])

    def opening_copies():
        plan = (
            (rowsend0.at[0], rowrecv0.at[1]),
            (rowsend0.at[1], rowrecv0.at[0]),
            (colsend0, colrecv0.at[1]),
            (colsend0, colrecv0.at[0]),
            (cbsend.at[0], cbrecv.at[3]),
            (cbsend.at[0], cbrecv.at[2]),
            (cbsend.at[1], cbrecv.at[1]),
            (cbsend.at[1], cbrecv.at[0]),
        )
        return [
            remote(src, dst, send_sem.at[ROUNDS, c], recv_sem.at[ROUNDS, c], around[c])
            for c, (src, dst) in enumerate(plan)
        ]

    def round_copies(e):
        plan = (
            (rsend.at[e, 0], rrecv.at[e, 1]),
            (rsend.at[e, 1], rrecv.at[e, 0]),
            (vsend.at[e], vrecv.at[e, 1]),
            (vsend.at[e], vrecv.at[e, 0]),
            (rsend.at[e, 0], drecv.at[e, 3]),
            (rsend.at[e, 0], drecv.at[e, 2]),
            (rsend.at[e, 1], drecv.at[e, 1]),
            (rsend.at[e, 1], drecv.at[e, 0]),
        )
        return [
            remote(src, dst, send_sem.at[e, c], recv_sem.at[e, c], around[c]) for c, (src, dst) in enumerate(plan)
        ]

    pl.semaphore_wait(barrier, len(around) + sum(stage_size))
    for copy in opening_copies():
        copy.start()
    stage_start(0)

    PASS1 = range(9)

    def put(index, terms):
        for c in range(5):
            store[c, index] = terms[c]

    def first_self(p, carry):
        mine = [own[k, at(p), :] for k in PASS1]
        ti, ri = zero, zero
        for step in range(1, 9):
            q = lax.rem(p + step, SLOTS)
            other = [own[k, at(q), :] for k in PASS1]
            terms = pair_terms(mine, other)
            put(SELF_AT + p * 8 + (step - 1), terms)
            t = terms[CO] * (other[F] - mine[F])
            ti = ti + t
            ri = ri + terms[KE]
            if step < 8:
                acc[0, at(q), :] += -t
                acc[1, at(q), :] += terms[KE]
        acc[0, at(p), :] += ti
        acc[1, at(p), :] += ri
        for k in range(QUANTITIES):
            for d, v in enumerate(shifted(own[k, at(p), :])):
                if k == X and DIRS[d][1]:
                    v = v + float(DIRS[d][1])
                if k == Y and DIRS[d][0]:
                    v = v + float(DIRS[d][0])
                if k == Z:
                    out = None
                    for step, index, last in ((DIRS[d][0], row, ROWS - 1), (DIRS[d][1], lane, COLS - 1)):
                        if step:
                            hit = index == (last if step > 0 else 0)
                            out = hit if out is None else out | hit
                    v = jnp.where(out, OUTSIDE_Z, v)
                far[d, k, p] = v
        for d in range(4):
            for c in range(2):
                accj[d, c, p] = zero
            for c in range(3):
                kaccj[d, c, p] = zero
        return carry

    def first_dirs(n, carry):
        d = lax.div(n, 8)
        p0 = lax.rem(n, 8) * 2
        mine = [[own[k, at(p0 + a), :] for k in PASS1] for a in range(2)]
        ti = [zero, zero]
        ri = [zero, zero]
        for q in range(SLOTS):
            other = [far[d, k, q] for k in PASS1]
            tj, rj = None, None
            for a in range(2):
                terms = pair_terms(mine[a], other)
                put(d * 256 + (p0 + a) * 16 + q, terms)
                t, r = terms[CO] * (other[F] - mine[a][F]), terms[KE]
                ti[a] = ti[a] + t
                ri[a] = ri[a] + r
                tj = t if tj is None else tj + t
                rj = r if rj is None else rj + r
            accj[d, 0, q] = accj[d, 0, q] - tj
            accj[d, 1, q] = accj[d, 1, q] + rj
        for a in range(2):
            acc[0, at(p0 + a), :] += ti[a]
            acc[1, at(p0 + a), :] += ri[a]
        return carry

    lax.fori_loop(0, SLOTS, first_self, 0)
    lax.fori_loop(0, 32, first_dirs, 0)
    stage_finish(0)
    stage_start(1)

    for copy in opening_copies():
        copy.wait_recv()

    def rows_around(k, carry):
        for side in range(2):
            h = rowrecv0[side, k]
            cl = pltpu.roll(cbrecv[side * 2], lax.rem(COLS - 2 * k, COLS), 1)
            cr = pltpu.roll(cbrecv[side * 2 + 1], COLS - 2 - 2 * k, 1)
            rowfar[side * 3, k] = jnp.where(lane16 == 0, cl, pltpu.roll(h, 1, 1))
            rowfar[side * 3 + 1, k] = h
            rowfar[side * 3 + 2, k] = jnp.where(lane16 == COLS - 1, cr, pltpu.roll(h, COLS - 1, 1))
            colown[side, k] = gather(colsend0[k], own_index[side])
            for h in range(2):
                v = gather(colrecv0[side, k], far_index[side][h])
                for number, value in enumerate((pltpu.roll(v, 1, 0), v, pltpu.roll(v, ROWS - 1, 0))):
                    colfar[side * 6 + number * 2 + h, k] = value
        return carry

    grouped(QUANTITIES, 4, rows_around, 0)

    z_side = (jnp.where(gy == 0, EDGE_Z, 0.0), jnp.where(gy == n_gy - 1, EDGE_Z, 0.0))
    z_end = (jnp.where(gx == 0, EDGE_Z, 0.0), jnp.where(gx == n_gx - 1, EDGE_Z, 0.0))
    z_lane = (
        jnp.where(lane16 == 0, z_end[0], 0.0),
        jnp.zeros((SLOTS, COLS), jnp.float32),
        jnp.where(lane16 == COLS - 1, z_end[1], 0.0),
    )
    for side in range(2):
        for number in range(3):
            c = side * 3 + number
            if number != 1:
                rowfar[c, X] = rowfar[c, X] + float(number - 1)
            rowfar[c, Y] = rowfar[c, Y] + (-1.0 if side == 0 else 1.0)
            rowfar[c, Z] = rowfar[c, Z] + (z_lane[number] + z_side[side])
            for h in range(2):
                c = side * 6 + number * 2 + h
                colfar[c, X] = colfar[c, X] + (-1.0 if side == 0 else 1.0)
                z = colfar[c, Z] + z_end[side]
                if number != 1:
                    colfar[c, Y] = colfar[c, Y] + float(number - 1)
                    z = jnp.where(row == (0 if number == 0 else ROWS - 1), OUTSIDE_Z, z)
                colfar[c, Z] = z

    def scatter_rows(target, c, side, halves):
        target[c, edge_row(side), :] = target[c, edge_row(side), :] + jnp.concatenate(halves, axis=0)

    def group_sum(v):
        v = v + pltpu.roll(v, COLS - 1, 1)
        v = v + pltpu.roll(v, COLS - 2, 1)
        return v + pltpu.roll(v, COLS - 4, 1)

    ends = (lane == 0) | (lane == COLS - 1)

    def scatter_columns(target, count):
        combined = []
        for c in range(count):
            u = jnp.where((lane & 7) == 0, group_sum(coltot[0, c]), 0.0)
            combined.append(jnp.where((lane & 7) == 7, pltpu.roll(group_sum(coltot[1, c]), COLS - 1, 1), u))

        def add(p):
            for c in range(count):
                v = pltpu.roll(combined[c], (COLS - 8 * p) % COLS, 1) if p else combined[c]
                target[c, at(p), :] += jnp.where(ends, v, 0.0)

        for p in range(SLOTS):
            add(p)

    def rim(target, count, row_mine, row_terms, col_mine, col_terms):
        def one_side(side):
            mine = row_mine(side)

            def one_row(number, totals):
                total = list(totals)
                c = side * 3 + number
                for q in range(SLOTS):
                    add = row_terms(c, q, mine)
                    for a in range(2):
                        for x, e in enumerate(add(a, ROW_AT + (c * 16 + q) * 2 + a)):
                            total[a * count + x] = total[a * count + x] + e
                return tuple(total)

            total = (zero,) * (2 * count)
            if count == 1:
                for number in range(3):
                    total = one_row(number, total)
            else:
                total = lax.fori_loop(0, 3, one_row, total)
            for x in range(count):
                scatter_rows(target, x, side, [total[x], total[count + x]])

            mine_col = col_mine(side)

            def one_column(number, totals):
                c = side * 6 + number
                return tuple(t + e for t, e in zip(totals, col_terms(c, mine_col, COL_AT + c)))

            total = (zero,) * count
            for number in range(6):
                total = one_column(number, total)
            for x in range(count):
                coltot[side, x] = total[x]

        for side in range(2):
            one_side(side)
        scatter_columns(target, count)

    def first_terms(mine, other, index):
        terms = pair_terms(mine, other)
        put(index, terms)
        return terms[CO] * (other[F] - mine[F]), terms[KE]

    def first_row(c, q, mine):
        other = [rowfar[c, k, pl.ds(q, 1), :] for k in PASS1]
        return lambda a, index: first_terms(mine[a], other, index)

    rim(
        acc,
        2,
        lambda side: [[rowsend0[side, k, half(a), :] for k in PASS1] for a in range(2)],
        first_row,
        lambda side: [colown[side, k] for k in PASS1],
        lambda c, mine, index: first_terms(mine, [colfar[c, k] for k in PASS1], index),
    )
    stage_finish(1)
    stage_start(2)

    def total_of(target, per_dir, c, p):
        return target[c, at(p), :] + unshifted(*(per_dir[d, c, p] for d in range(4)))

    def set_field(p, value):
        field[at(p), :] = value
        for d, v in enumerate(shifted(value)):
            sfar[d, p] = v
        acc[0, at(p), :] = zero
        for d in range(4):
            accj[d, 0, p] = zero

    def first_update(p):
        live = p < pop[...]
        m = own[M, at(p), :]
        density = jnp.where(live, m + total_of(acc, accj, 1, p) / m, 1.0)
        inverse = 1.0 / density
        g = ROOT_HALF * inverse
        gfac[at(p), :] = g
        for d, v in enumerate(shifted(g)):
            gfar[d, p] = v
        pfac[p] = 6.0 * (HEAT_RATIO - 1.0) * inverse
        u = jnp.where(live, total_of(acc, accj, 0, p) / cap[p], 0.0)
        powers[0, p] = u
        set_field(p, u)

    for p in range(SLOTS):
        first_update(p)

    def section_dirs(n, carry):
        d = lax.div(n, 4)
        p0 = lax.rem(n, 4) * 4
        mine = [field[at(p0 + a), :] for a in range(4)]
        ti = [zero] * 4
        for q in range(SLOTS):
            other = sfar[d, q]
            tj = None
            for a in range(4):
                t = store[CO, d * 256 + (p0 + a) * 16 + q] * (other - mine[a])
                ti[a] = ti[a] + t
                tj = t if tj is None else tj + t
            accj[d, 0, q] = accj[d, 0, q] - tj
        for a in range(4):
            acc[0, at(p0 + a), :] += ti[a]
        return carry

    def self_partners(p):
        for step in range(1, 9):
            yield lax.rem(p + step, SLOTS), SELF_AT + p * 8 + (step - 1), False
        for step in range(1, 8):
            q = lax.rem(p + SLOTS - step, SLOTS)
            yield q, SELF_AT + q * 8 + (step - 1), True

    def section_self(p):
        mine = field[at(p), :]
        ti = zero
        for q, index, _ in self_partners(p):
            ti = ti + store[CO, index] * (field[at(q), :] - mine)
        acc[0, at(p), :] += ti

    def section_row(c, q, mine):
        other = hs[FIELD, c, pl.ds(q, 1), :]
        return lambda a, index: (store[CO, index] * (other - mine[a]),)

    def drag_dirs(n, carry):
        d = lax.div(n, 8)
        p0 = lax.rem(n, 8) * 2
        g = [gfac[at(p0 + a), :] for a in range(2)]
        v = [[own[VX + c, at(p0 + a), :] for c in range(3)] for a in range(2)]
        total = [[zero] * 3 for _ in range(2)]
        for q in range(SLOTS):
            gj = gfar[d, q]
            vj = [far[d, VX + c, q] for c in range(3)]
            back = [None] * 3
            for a in range(2):
                w = store[KE, d * 256 + (p0 + a) * 16 + q] * (g[a] * gj)
                for c in range(3):
                    e = w * (vj[c] - v[a][c])
                    total[a][c] = total[a][c] + e
                    back[c] = e if back[c] is None else back[c] + e
            for c in range(3):
                kaccj[d, c, q] = kaccj[d, c, q] - back[c]
        for a in range(2):
            for c in range(3):
                kacc[c, at(p0 + a), :] += total[a][c]
        return carry

    def drag_self(p):
        g = gfac[at(p), :]
        v = [own[VX + c, at(p), :] for c in range(3)]
        total = [zero] * 3
        for q, index, _ in self_partners(p):
            w = store[KE, index] * (g * gfac[at(q), :])
            for c in range(3):
                total[c] = total[c] + w * (own[VX + c, at(q), :] - v[c])
        for c in range(3):
            kacc[c, at(p), :] += total[c]

    def drag_row(c, q, mine):
        g, v = mine
        gj = hs[DRAG, c, pl.ds(q, 1), :]
        vj = [rowfar[c, VX + x, pl.ds(q, 1), :] for x in range(3)]

        def terms(a, index):
            w = store[KE, index] * (g[a] * gj)
            return [w * (vj[x] - v[a][x]) for x in range(3)]

        return terms

    def drag_column(c, mine, index):
        g, v = mine
        w = store[KE, index] * (g * cf[DRAG, c])
        return [w * (colfar[c, VX + x] - v[x]) for x in range(3)]

    def drag_rim():
        rim(
            kacc,
            3,
            lambda side: (
                [rsend[0, side, DRAG, half(a), :] for a in range(2)],
                [[rowsend0[side, VX + x, half(a), :] for x in range(3)] for a in range(2)],
            ),
            drag_row,
            lambda side: (oc[DRAG, side], [colown[side, VX + x] for x in range(3)]),
            drag_column,
        )

    def push_dirs(n, carry):
        d = lax.div(n, 8)
        p0 = lax.rem(n, 8) * 2
        pi = [field[at(p0 + a), :] for a in range(2)]
        total = [[zero] * 3 for _ in range(2)]
        for q in range(SLOTS):
            pj = sfar[d, q]
            back = [None] * 3
            for a in range(2):
                both = pi[a] + pj
                for c in range(3):
                    e = both * store[WX + c, d * 256 + (p0 + a) * 16 + q]
                    total[a][c] = total[a][c] + e
                    back[c] = e if back[c] is None else back[c] + e
            for c in range(3):
                kaccj[d, c, q] = kaccj[d, c, q] - back[c]
        for a in range(2):
            for c in range(3):
                kacc[c, at(p0 + a), :] += total[a][c]
        return carry

    def push_self(p):
        pi = field[at(p), :]
        total = [zero] * 3
        for q, index, reverse in self_partners(p):
            both = pi + field[at(q), :]
            for c in range(3):
                e = both * store[WX + c, index]
                total[c] = total[c] - e if reverse else total[c] + e
        for c in range(3):
            kacc[c, at(p), :] += total[c]

    def push_row(c, q, mine):
        pj = hs[FIELD, c, pl.ds(q, 1), :]

        def terms(a, index):
            both = mine[a] + pj
            return [both * store[WX + x, index] for x in range(3)]

        return terms

    def push_column(c, mine, index):
        both = mine + cf[FIELD, c]
        return [both * store[WX + x, index] for x in range(3)]

    for side in range(2):
        packed = gfac[edge_row(side), :]
        for e in range(ROUNDS):
            rsend[e, side, DRAG] = packed
    packed = packed_columns(lambda p: gfac[at(p), :])
    for e in range(ROUNDS):
        vsend[e, DRAG] = packed

    polynomial = section_polynomial(SECTIONS)

    def spread(e, kind):
        for side in range(2):
            h = rrecv[e, side, kind]
            hl, hr = drecv[e, side * 2, kind], drecv[e, side * 2 + 1, kind]
            hs[kind, side * 3] = pltpu.roll(jnp.where(lane16 == COLS - 1, hl, h), 1, 1)
            hs[kind, side * 3 + 1] = h
            hs[kind, side * 3 + 2] = pltpu.roll(jnp.where(lane16 == 0, hr, h), COLS - 1, 1)
            oc[kind, side] = gather(vsend[e, kind], own_index[side])
            for h in range(2):
                v = gather(vrecv[e, side, kind], far_index[side][h])
                for number, value in enumerate((pltpu.roll(v, 1, 0), v, pltpu.roll(v, ROWS - 1, 0))):
                    cf[kind, side * 6 + number * 2 + h] = value

    def one_round(e):
        for side in range(2):
            rsend[e, side, FIELD] = field[edge_row(side), :]
        vsend[e, FIELD] = packed_columns(lambda p: field[at(p), :])
        for copy in round_copies(e):
            copy.start()

        if e < 3:
            lax.fori_loop(0, 16, section_dirs, 0)
            each(SLOTS, section_self)

        if e == 0:
            each(SLOTS, drag_self)

        if e == 2:
            drag_rim()

        lax.fori_loop(min(e * 11, 32), min(e * 11 + 11, 32), drag_dirs, 0)

        if e == 3:
            lax.fori_loop(0, 32, push_dirs, 0)
            each(SLOTS, push_self)

        for copy in round_copies(e):
            copy.wait_recv()
        for kind in range(2 if e == 0 else 1):
            spread(e, kind)

        if e < 3:
            rim(
                acc,
                1,
                lambda side: [rsend[e, side, FIELD, half(a), :] for a in range(2)],
                section_row,
                lambda side: oc[FIELD, side],
                lambda c, mine, index: (store[CO, index] * (cf[FIELD, c] - mine),),
            )

        def power(p):
            return jnp.where(p < pop[...], total_of(acc, accj, 0, p) / cap[p], 0.0)

        if e == 1:
            stage_finish(2)
            best = msrc[3]
            for shift in (4, 2, 1):
                best = jnp.maximum(best, pltpu.roll(best, shift, 0))
            for shift in (64, 32, 16, 8, 4, 2, 1):
                best = jnp.maximum(best, pltpu.roll(best, shift, 1))
            msrc[4] = COURANT / best

        if e < 2:

            def update(p):
                u = power(p)
                powers[e + 1, p] = u
                set_field(p, u)

            for p in range(SLOTS):
                update(p)

        if e == 2:
            step_dt = msrc[4]

            def update(p):
                y = step_dt * (polynomial[4] * power(p))
                for k in (3, 2, 1):
                    y = step_dt * (polynomial[k] * powers[k - 1, p] + y)
                y = polynomial[0] * own[F, at(p), :] + y
                heated[p] = y
                set_field(p, pfac[p] * y)

            for p in range(SLOTS):
                update(p)

        if e == 3:
            rim(
                kacc,
                3,
                lambda side: [rsend[e, side, FIELD, half(a), :] for a in range(2)],
                push_row,
                lambda side: oc[FIELD, side],
                push_column,
            )

    for e in range(ROUNDS):
        one_round(e)

    def finish(p):
        live = p < pop[...]
        scale = jnp.where(live, msrc[4] / own[M, at(p), :], 0.0)
        for c in range(3):
            moved[c, p] = own[VX + c, at(p), :] + scale * total_of(kacc, kaccj, c, p)

    for p in range(SLOTS):
        finish(p)

    for copy in opening_copies():
        copy.wait_send()

    def sent(e):
        for copy in round_copies(e):
            copy.wait_send()

    each(ROUNDS, sent)
    for stage in range(3):
        each(stage_size[stage], lambda k, stage=stage: stage_copy(stage, k).wait_send())


def body(sizes, *args):
    f32 = jnp.float32
    messages = sum(sizes) - 3
    tile = (SLOTS, ROWS, COLS)
    vmem = pl.BlockSpec(memory_space=pltpu.VMEM)
    scratch = [pltpu.VMEM(a.shape, a.dtype) for a in args] + [
        pltpu.VMEM((QUANTITIES, FLAT, COLS), f32),
        pltpu.VMEM((4, QUANTITIES) + tile, f32),
        pltpu.VMEM((FLAT, COLS), f32),
        pltpu.VMEM((3,) + tile, f32),
        pltpu.VMEM((FLAT, COLS), f32),
        pltpu.VMEM(tile, f32),
        pltpu.VMEM((4,) + tile, f32),
        pltpu.VMEM((4,) + tile, f32),
        pltpu.VMEM((2, FLAT, COLS), f32),
        pltpu.VMEM((4, 2) + tile, f32),
        pltpu.VMEM((3, FLAT, COLS), f32),
        pltpu.VMEM((4, 3) + tile, f32),
        pltpu.VMEM((5, PAIRS, ROWS, COLS), f32),
        pltpu.VMEM((2, QUANTITIES, SLOTS, COLS), f32),
        pltpu.VMEM((2, QUANTITIES, SLOTS, COLS), f32),
        pltpu.VMEM((QUANTITIES, ROWS, COLS), f32),
        pltpu.VMEM((2, QUANTITIES, ROWS, COLS), f32),
        pltpu.VMEM((2, SLOTS, COLS), f32),
        pltpu.VMEM((4, SLOTS, COLS), f32),
        pltpu.VMEM((6, QUANTITIES, SLOTS, COLS), f32),
        pltpu.VMEM((12, QUANTITIES, ROWS, COLS), f32),
        pltpu.VMEM((2, QUANTITIES, ROWS, COLS), f32),
        pltpu.VMEM((2, 3, ROWS, COLS), f32),
        pltpu.VMEM((ROUNDS, 2, 2, SLOTS, COLS), f32),
        pltpu.VMEM((ROUNDS, 2, 2, SLOTS, COLS), f32),
        pltpu.VMEM((ROUNDS, 2, ROWS, COLS), f32),
        pltpu.VMEM((ROUNDS, 2, 2, ROWS, COLS), f32),
        pltpu.VMEM((ROUNDS, 4, 2, SLOTS, COLS), f32),
        pltpu.VMEM((2, 6, SLOTS, COLS), f32),
        pltpu.VMEM((2, 12, ROWS, COLS), f32),
        pltpu.VMEM((2, 2, ROWS, COLS), f32),
        pltpu.VMEM((5, ROWS, COLS), f32),
        pltpu.VMEM((messages, ROWS, COLS), f32),
        pltpu.SemaphoreType.DMA((ROUNDS + 1, 8)),
        pltpu.SemaphoreType.DMA((ROUNDS + 1, 8)),
        pltpu.SemaphoreType.DMA((messages,)),
        pltpu.SemaphoreType.DMA((messages,)),
        pltpu.SemaphoreType.DMA((8,)),
    ]
    return pl.pallas_call(
        functools.partial(kernel, sizes),
        out_shape=(jax.ShapeDtypeStruct(tile, f32), jax.ShapeDtypeStruct((3,) + tile, f32)),
        in_specs=[pl.BlockSpec(memory_space=pl.ANY)] * 8,
        out_specs=(vmem, vmem),
        scratch_shapes=scratch,
        compiler_params=pltpu.CompilerParams(
            collective_id=0, has_side_effects=True, vmem_limit_bytes=60 * 1024 * 1024
        ),
        name="sections_and_kick",
    )(*args)


def solution(mesh):
    n_gx, n_gy = mesh.shape["gx"], mesh.shape["gy"]
    n_hi = 4 if n_gy % 4 == 0 and n_gy > 4 else 2
    sizes = (n_gx, n_gy // n_hi, n_hi)
    cells = P("gy", "gx")
    one = P(None, "gy", "gx")
    many = P(None, None, "gy", "gx")
    return jax.shard_map(
        functools.partial(body, sizes),
        mesh=mesh,
        in_specs=(cells, many, many, one, one, one, one, many),
        out_specs=(one, many),
        check_vma=False,
    )
```

```python
import functools

import jax
import jax.numpy as jnp
from jax import lax
from jax.experimental import pallas as pl
from jax.experimental.pallas import tpu as pltpu
from jax.sharding import PartitionSpec as P

SECTIONS = 4
ISO_PART = 0.1
HEAT_RATIO = 5.0 / 3.0
COURANT = 0.3
ROOT_HALF = 0.5**0.5
MESH = pl.DeviceIdType.MESH

SLOTS = 16
ROWS = 8
COLS = 128
FLAT = SLOTS * ROWS

X, Y, Z, BX, BY, BZ, KA, F, M, VX, VY, VZ = range(12)
QUANTITIES = 12

DIRECTIONS = 4

CO, KE, WX, WY, WZ = range(5)
SELF_AT = DIRECTIONS * SLOTS * SLOTS
ROW_AT = SELF_AT + SLOTS * 8
COL_AT = ROW_AT + 6 * SLOTS * 2
PAIRS = COL_AT + 12

ROUNDS = 4
FIELD, DRAG = range(2)

EMPTY_Z = 10.0
OUTSIDE_X = 20.0
EDGE_Z = 40.0
PAD = 8

SIN = (0.9999999957157406, -0.1666665796974384, 0.008333050613415454, -0.0001980904606136566, 2.605165590448684e-06)
COS = (
    0.9999999997798981,
    -0.4999999935694129,
    0.04166663620835954,
    -0.001388836083517328,
    2.476013513307355e-05,
    -2.605106944029617e-07,
)


def section_polynomial(section_total):
    weight = 4.0 / (section_total * section_total + section_total - 2)
    series = [1.0 / 3.0, 1.0 / 3.0, 1.0 / 3.0]
    for j in range(3, section_total + 1):
        series.append((j * j + j - 2) / (2.0 * j * (j + 1)))

    def padded(values):
        return values + [0.0] * (section_total + 1 - len(values))

    before, now = padded([1.0]), padded([1.0, series[1] * weight])
    for j in range(2, section_total + 1):
        m = (2 * j - 1) / j * series[j] / series[j - 1]
        n = -(j - 1) / j * series[j] / series[j - 2]
        after = [m * a + n * b for a, b in zip(now, before)]
        after[0] += 1.0 - m - n
        after[1] -= (1.0 - series[j - 1]) * m * weight
        for k in range(section_total):
            after[k + 1] += m * weight * now[k]
        before, now = now, after
    return now


def horner(coefs, t):
    total = jnp.full_like(t, coefs[-1])
    for c in coefs[-2::-1]:
        total = total * t + c
    return total


def sin_cos(angle):
    half = 0.5 * angle
    t = half * half
    s = half * horner(SIN, t)
    c = horner(COS, t)
    return 2.0 * s * c, 1.0 - 2.0 * s * s


def pair_terms(i, j):
    dx, dy, dz = i[X] - j[X], i[Y] - j[Y], i[Z] - j[Z]
    s = jnp.maximum(1.0 - (dx * dx + dy * dy + dz * dz), 0.0)
    s2 = s * s
    own = i[BX] * dx + i[BY] * dy + i[BZ] * dz
    far = j[BX] * dx + j[BY] * dy + j[BZ] * dz
    co = (s2 * s) * (ISO_PART + (own * own + far * far)) * (i[KA] + j[KA])
    w = s2 * (i[M] * j[M])
    return co, w * s, w * dx, w * dy, w * dz


def kernel(
    sizes,
    pop_in,
    loc_in,
    tilt_in,
    mass_in,
    kappa_in,
    cap_in,
    temp_in,
    mot_in,
    heated,
    moved,
    pop,
    loc,
    tilt,
    mass,
    kappa,
    cap,
    temp,
    mot,
    far,
    powers,
    pfac,
    sfar,
    gfar,
    acc,
    accj,
    kacc,
    kaccj,
    store,
    rowsend0,
    rowrecv0,
    colsend0,
    colrecv0,
    cbsend,
    cbrecv,
    rowfar,
    colfar,
    colown,
    coltot,
    rsend,
    rrecv,
    vsend,
    vrecv,
    drecv,
    hs,
    cf,
    oc,
    msrc,
    mrecv,
    send_sem,
    recv_sem,
    msend_sem,
    mrecv_sem,
    load_sem,
):
    own, field, gfac = far.at[2], sfar.at[2], gfar.at[2]
    loads = [
        pltpu.make_async_copy(src, dst, load_sem.at[number])
        for number, (src, dst) in enumerate(
            (
                (pop_in, pop),
                (loc_in, loc),
                (tilt_in, tilt),
                (mass_in, mass),
                (kappa_in, kappa),
                (cap_in, cap),
                (temp_in, temp),
                (mot_in, mot),
            )
        )
    ]
    for load in loads:
        load.start()

    n_gx, n_lo, n_hi = sizes
    n_gy = n_lo * n_hi
    gx = lax.axis_index("gx")
    gy = lax.axis_index("gy")
    left, right = lax.rem(gx + n_gx - 1, n_gx), lax.rem(gx + 1, n_gx)
    up, down = lax.rem(gy + n_gy - 1, n_gy), lax.rem(gy + 1, n_gy)
    lo, hi = lax.rem(gy, n_lo), lax.div(gy, n_lo)

    around = ((gx, up), (gx, down), (left, gy), (right, gy), (left, up), (right, up), (left, down), (right, down))

    stage_size = (n_gx - 1, n_lo - 1, n_hi - 1)
    stage_at = (0, n_gx - 1, n_gx + n_lo - 2)

    def stage_device(stage, k):
        if stage == 0:
            return (lax.rem(gx + k + 1, n_gx), gy)
        if stage == 1:
            return (gx, hi * n_lo + lax.rem(lo + k + 1, n_lo))
        return (gx, lax.rem(hi + k + 1, n_hi) * n_lo + lo)

    def each(count, fn):
        def run(k, carry):
            fn(k)
            return carry

        lax.fori_loop(0, count, run, 0)

    def grouped(count, size, fn, carry):
        def run(k, carry):
            for a in range(size):
                carry = fn(k * size + a, carry)
            return carry

        return lax.fori_loop(0, count // size, run, carry)

    def over(fn, first, last, split):
        if first < split:
            lax.fori_loop(first, split, functools.partial(fn, 0), 0)
        if last > split:
            lax.fori_loop(max(first, split), last, functools.partial(fn, 1), 0)

    def paired(fn):
        def both(p):
            fn(2 * p)
            fn(2 * p + 1)

        each(SLOTS // 2, both)

    barrier = pltpu.get_barrier_semaphore()

    def greet(device):
        pl.semaphore_signal(barrier, inc=1, device_id=device, device_id_type=MESH)

    for device in around:
        greet(device)
    for stage in range(3):
        each(stage_size[stage], lambda k, stage=stage: greet(stage_device(stage, k)))

    lane = lax.broadcasted_iota(jnp.int32, (ROWS, COLS), 1)
    row = lax.broadcasted_iota(jnp.int32, (ROWS, COLS), 0)
    lane16 = lax.broadcasted_iota(jnp.int32, (SLOTS, COLS), 1)
    zero = jnp.zeros((ROWS, COLS), jnp.float32)
    rows_down = row.astype(jnp.float32)

    def at(p):
        start = p * ROWS
        return pl.ds(start if isinstance(p, int) else pl.multiple_of(start, ROWS), ROWS)

    def edge_row(side):
        return pl.ds(side * (ROWS - 1), SLOTS, stride=ROWS)

    def half(a):
        return pl.ds(a * 8, 8)

    def partner(q, off):
        return pl.ds(q * ROWS + off, ROWS)

    def slot_sum(q):
        start = PAD + q * ROWS
        return pl.ds(start if isinstance(q, int) else pl.multiple_of(start, ROWS), ROWS)

    def put_copies(target, k, p, value):
        target[(0, *k, at(p))] = pltpu.roll(value, COLS - 1, 1)
        target[(1, *k, at(p))] = pltpu.roll(value, 1, 1)
        target[(2, *k, at(p))] = value

    def gather(v, index):
        return jnp.take_along_axis(v, index, axis=1)

    def packed_columns(tile_of):
        v = tile_of(0)
        for p in range(1, SLOTS):
            mask = (lane == 8 * p) | (lane == 8 * p - 1)
            v = jnp.where(mask, pltpu.roll(tile_of(p), 8 * p, 1), v)
        return v

    group = lane & ~7
    within = (lane & 7) * 8
    own_index = (group, (group + (COLS - 1)) & (COLS - 1))
    far_index = (
        ((within + (COLS - 1)) & (COLS - 1), (within + 63) & (COLS - 1)),
        (within, within + 64),
    )

    def prepare(p, fastest):
        live = p < pop[...]
        sin_p, cos_p = sin_cos(tilt[0, p])
        sin_a, cos_a = sin_cos(tilt[1, p])
        t = temp[p]
        v = [mot[c, p] for c in range(3)]
        values = [
            loc[0, p],
            loc[1, p] + rows_down,
            jnp.where(live, loc[2, p], EMPTY_Z),
            ROOT_HALF * (sin_p * cos_a),
            ROOT_HALF * (sin_p * sin_a),
            ROOT_HALF * cos_p,
            0.5 * kappa[p],
            t,
            mass[p],
        ] + v
        for k in range(QUANTITIES):
            own[k, at(p), :] = values[k]
        for c in range(2):
            acc[c, at(p), :] = zero
        for c in range(3):
            kacc[c, at(p), :] = zero
        speed = jnp.sqrt(HEAT_RATIO * (HEAT_RATIO - 1.0) * t) + jnp.sqrt(v[0] * v[0] + v[1] * v[1] + v[2] * v[2])
        return jnp.maximum(fastest, jnp.where(live, speed, 0.0))

    after = pl.ds(FLAT, PAD)
    for copy in range(3):
        for k in range(QUANTITIES):
            far[copy, k, after, :] = zero
        sfar[copy, after, :] = zero
        gfar[copy, after, :] = zero
    for d in range(DIRECTIONS):
        for c in range(2):
            accj[d, c, pl.ds(0, PAD), :] = zero
        for c in range(3):
            kaccj[d, c, pl.ds(0, PAD), :] = zero
    for load in loads:
        load.wait()
    msrc[0] = grouped(SLOTS, 4, prepare, zero)

    def pack(k, cb):
        cb = list(cb)
        for side in range(2):
            packed = own[k, edge_row(side), :]
            rowsend0[side, k] = packed
            mask = (lane16 == 2 * k) | (lane16 == 2 * k + 1)
            cb[side] = jnp.where(mask, pltpu.roll(packed, 2 * k + 1, 1), cb[side])
        colsend0[k] = packed_columns(lambda p: own[k, at(p), :])
        return tuple(cb)

    blank = jnp.zeros((SLOTS, COLS), jnp.float32)
    cbsend[0], cbsend[1] = grouped(QUANTITIES, 3, pack, (blank, blank))

    def remote(src, dst, s, r, device):
        return pltpu.make_async_remote_copy(
            src_ref=src, dst_ref=dst, send_sem=s, recv_sem=r, device_id=device, device_id_type=MESH
        )

    def stage_copy(stage, k):
        slot = stage_at[stage] + k
        return remote(
            msrc.at[stage], mrecv.at[slot], msend_sem.at[slot], mrecv_sem.at[slot], stage_device(stage, k)
        )

    def stage_start(stage):
        each(stage_size[stage], lambda k: stage_copy(stage, k).start())

    def stage_finish(stage):
        def take(k, best):
            stage_copy(stage, k).wait_recv()
            return jnp.maximum(best, mrecv[stage_at[stage] + k])

        msrc[stage + 1] = lax.fori_loop(0, stage_size[stage], take, msrc[stage])

    def opening_copies():
        plan = (
            (rowsend0.at[0], rowrecv0.at[1]),
            (rowsend0.at[1], rowrecv0.at[0]),
            (colsend0, colrecv0.at[1]),
            (colsend0, colrecv0.at[0]),
            (cbsend.at[0], cbrecv.at[3]),
            (cbsend.at[0], cbrecv.at[2]),
            (cbsend.at[1], cbrecv.at[1]),
            (cbsend.at[1], cbrecv.at[0]),
        )
        return [
            remote(src, dst, send_sem.at[c], recv_sem.at[1, c], around[c])
            for c, (src, dst) in enumerate(plan)
        ]

    def round_copies(e):
        plan = (
            (rsend.at[e, 0], rrecv.at[e, 1]),
            (rsend.at[e, 1], rrecv.at[e, 0]),
            (vsend.at[e], vrecv.at[e, 1]),
            (vsend.at[e], vrecv.at[e, 0]),
            (rsend.at[e, 0], drecv.at[e, 3]),
            (rsend.at[e, 0], drecv.at[e, 2]),
            (rsend.at[e, 1], drecv.at[e, 1]),
            (rsend.at[e, 1], drecv.at[e, 0]),
        )
        return [
            remote(src, dst, send_sem.at[c], recv_sem.at[e % 2, c], around[c]) for c, (src, dst) in enumerate(plan)
        ]

    pl.semaphore_wait(barrier, len(around) + sum(stage_size))
    for copy in opening_copies():
        copy.start()
    stage_start(0)

    PASS1 = range(9)

    def put(index, terms):
        for c in range(5):
            store[c, index] = terms[c]

    def first_self(p, carry):
        mine = [own[k, at(p), :] for k in PASS1]
        ti, ri = zero, zero
        for step in range(1, 9):
            q = lax.rem(p + step, SLOTS)
            other = [own[k, at(q), :] for k in PASS1]
            terms = pair_terms(mine, other)
            put(SELF_AT + p * 8 + (step - 1), terms)
            t = terms[CO] * (other[F] - mine[F])
            ti = ti + t
            ri = ri + terms[KE]
            if step < 8:
                acc[0, at(q), :] -= t
                acc[1, at(q), :] += terms[KE]
        acc[0, at(p), :] += ti
        acc[1, at(p), :] += ri
        for k in range(QUANTITIES):
            value = own[k, at(p), :]
            east, west = pltpu.roll(value, COLS - 1, 1), pltpu.roll(value, 1, 1)
            if k == X:
                east = jnp.where(lane == COLS - 1, OUTSIDE_X, east + 1.0)
                west = jnp.where(lane == 0, OUTSIDE_X, west - 1.0)
            far[0, k, at(p), :] = east
            far[1, k, at(p), :] = west
        for d in range(DIRECTIONS):
            for c in range(2):
                accj[d, c, slot_sum(p), :] = zero
            for c in range(3):
                kaccj[d, c, slot_sum(p), :] = zero
        return carry

    def first_dirs(off, n, carry):
        d = lax.div(n, 8)
        p0 = lax.rem(n, 8) * 2
        mine = [[own[k, at(p0 + a), :] for k in PASS1] for a in range(2)]
        ti = [zero, zero]
        ri = [zero, zero]
        for q in range(SLOTS):
            other = [far[lax.rem(d, 3), k, partner(q, off), :] for k in PASS1]
            tj, rj = None, None
            for a in range(2):
                terms = pair_terms(mine[a], other)
                put(d * 256 + (p0 + a) * 16 + q, terms)
                t, r = terms[CO] * (other[F] - mine[a][F]), terms[KE]
                ti[a] = ti[a] + t
                ri[a] = ri[a] + r
                tj = t if tj is None else tj + t
                rj = r if rj is None else rj + r
            accj[d, 0, slot_sum(q), :] -= tj
            accj[d, 1, slot_sum(q), :] += rj
        for a in range(2):
            acc[0, at(p0 + a), :] += ti[a]
            acc[1, at(p0 + a), :] += ri[a]
        return carry

    lax.fori_loop(0, SLOTS, first_self, 0)
    over(first_dirs, 0, 32, 8)
    stage_finish(0)
    stage_start(1)

    for copy in opening_copies():
        copy.wait_recv()

    def rows_around(k, carry):
        for side in range(2):
            h = rowrecv0[side, k]
            cl = pltpu.roll(cbrecv[side * 2], lax.rem(COLS - 2 * k, COLS), 1)
            cr = pltpu.roll(cbrecv[side * 2 + 1], COLS - 2 - 2 * k, 1)
            rowfar[side * 3, k] = jnp.where(lane16 == 0, cl, pltpu.roll(h, 1, 1))
            rowfar[side * 3 + 1, k] = h
            rowfar[side * 3 + 2, k] = jnp.where(lane16 == COLS - 1, cr, pltpu.roll(h, COLS - 1, 1))
            colown[side, k] = gather(colsend0[k], own_index[side])
            for h in range(2):
                v = gather(colrecv0[side, k], far_index[side][h])
                for number, value in enumerate((pltpu.roll(v, 1, 0), v, pltpu.roll(v, ROWS - 1, 0))):
                    colfar[side * 6 + number * 2 + h, k] = value
        return carry

    grouped(QUANTITIES, 4, rows_around, 0)

    z_side = (jnp.where(gy == 0, EDGE_Z, 0.0), jnp.where(gy == n_gy - 1, EDGE_Z, 0.0))
    z_end = (jnp.where(gx == 0, EDGE_Z, 0.0), jnp.where(gx == n_gx - 1, EDGE_Z, 0.0))
    z_lane = (
        jnp.where(lane16 == 0, z_end[0], 0.0),
        jnp.zeros((SLOTS, COLS), jnp.float32),
        jnp.where(lane16 == COLS - 1, z_end[1], 0.0),
    )
    for side in range(2):
        for number in range(3):
            c = side * 3 + number
            if number != 1:
                rowfar[c, X] = rowfar[c, X] + float(number - 1)
            rowfar[c, Y] = rowfar[c, Y] + float(-ROWS if side == 0 else ROWS)
            rowfar[c, Z] = rowfar[c, Z] + (z_lane[number] + z_side[side])
            for h in range(2):
                c = side * 6 + number * 2 + h
                colfar[c, X] = colfar[c, X] + (-1.0 if side == 0 else 1.0)
                colfar[c, Z] = colfar[c, Z] + z_end[side]

    def scatter_rows(target, c, side, halves):
        target[c, edge_row(side), :] = target[c, edge_row(side), :] + jnp.concatenate(halves, axis=0)

    def group_sum(v):
        v = v + pltpu.roll(v, COLS - 1, 1)
        v = v + pltpu.roll(v, COLS - 2, 1)
        return v + pltpu.roll(v, COLS - 4, 1)

    ends = (lane == 0) | (lane == COLS - 1)

    def scatter_columns(target, count):
        combined = []
        for c in range(count):
            u = jnp.where((lane & 7) == 0, group_sum(coltot[0, c]), 0.0)
            combined.append(jnp.where((lane & 7) == 7, pltpu.roll(group_sum(coltot[1, c]), COLS - 1, 1), u))

        def add(p):
            for c in range(count):
                v = pltpu.roll(combined[c], (COLS - 8 * p) % COLS, 1) if p else combined[c]
                target[c, at(p), :] += jnp.where(ends, v, 0.0)

        for p in range(SLOTS):
            add(p)

    def rim(target, count, row_mine, row_terms, col_mine, col_terms):
        def one_side(side):
            mine = row_mine(side)

            def one_row(number, totals):
                total = list(totals)
                c = side * 3 + number
                for q in range(SLOTS):
                    add = row_terms(c, q, mine)
                    for a in range(2):
                        for x, e in enumerate(add(a, ROW_AT + (c * 16 + q) * 2 + a)):
                            total[a * count + x] = total[a * count + x] + e
                return tuple(total)

            total = (zero,) * (2 * count)
            if count == 1:
                for number in range(3):
                    total = one_row(number, total)
            else:
                total = lax.fori_loop(0, 3, one_row, total)
            for x in range(count):
                scatter_rows(target, x, side, [total[x], total[count + x]])

            mine_col = col_mine(side)

            def one_column(number, totals):
                c = side * 6 + number
                return tuple(t + e for t, e in zip(totals, col_terms(c, mine_col, COL_AT + c)))

            total = (zero,) * count
            for number in range(6):
                total = one_column(number, total)
            for x in range(count):
                coltot[side, x] = total[x]

        for side in range(2):
            one_side(side)
        scatter_columns(target, count)

    def first_terms(mine, other, index):
        terms = pair_terms(mine, other)
        put(index, terms)
        return terms[CO] * (other[F] - mine[F]), terms[KE]

    def first_row(c, q, mine):
        other = [rowfar[c, k, pl.ds(q, 1), :] for k in PASS1]
        return lambda a, index: first_terms(mine[a], other, index)

    rim(
        acc,
        2,
        lambda side: [[rowsend0[side, k, half(a), :] for k in PASS1] for a in range(2)],
        first_row,
        lambda side: [colown[side, k] for k in PASS1],
        lambda c, mine, index: first_terms(mine, [colfar[c, k] for k in PASS1], index),
    )
    stage_finish(1)
    stage_start(2)

    def total_of(target, per_dir, c, p):
        below = pl.ds(PAD + p * ROWS - 1, ROWS)
        east = per_dir[0, c, slot_sum(p), :] + per_dir[3, c, below, :]
        west = per_dir[1, c, below, :]
        total = target[c, at(p), :] + per_dir[2, c, below, :]
        return total + pltpu.roll(east, 1, 1) + pltpu.roll(west, COLS - 1, 1)

    def clear(p):
        acc[0, at(p), :] = zero
        for d in range(DIRECTIONS):
            accj[d, 0, slot_sum(p), :] = zero

    def set_field(p, value):
        put_copies(sfar, (), p, value)

    def first_update(p):
        live = p < pop[...]
        m = own[M, at(p), :]
        density = jnp.where(live, m + total_of(acc, accj, 1, p) / m, 1.0)
        inverse = 1.0 / density
        g = ROOT_HALF * inverse
        put_copies(gfar, (), p, g)
        pfac[p] = 6.0 * (HEAT_RATIO - 1.0) * inverse
        u = jnp.where(live, total_of(acc, accj, 0, p) / cap[p], 0.0)
        powers[0, p] = u
        set_field(p, u)

    for p in range(SLOTS):
        first_update(p)
    for p in range(SLOTS):
        clear(p)

    def section_dirs(off, n, carry):
        d = lax.div(n, 4)
        p0 = lax.rem(n, 4) * 4
        mine = [field[at(p0 + a), :] for a in range(4)]
        ti = [zero] * 4
        for q in range(SLOTS):
            other = sfar[lax.rem(d, 3), partner(q, off), :]
            tj = None
            for a in range(4):
                t = store[CO, d * 256 + (p0 + a) * 16 + q] * (other - mine[a])
                ti[a] = ti[a] + t
                tj = t if tj is None else tj + t
            accj[d, 0, slot_sum(q), :] -= tj
        for a in range(4):
            acc[0, at(p0 + a), :] += ti[a]
        return carry

    def wrap(p):
        return p % SLOTS if isinstance(p, int) else lax.rem(p, SLOTS)

    def self_partners(p):
        for step in range(1, 9):
            yield wrap(p + step), SELF_AT + p * 8 + (step - 1), False
        for step in range(1, 8):
            q = wrap(p + SLOTS - step)
            yield q, SELF_AT + q * 8 + (step - 1), True

    def section_self(p):
        mine = field[at(p), :]
        ti = zero
        for q, index, _ in self_partners(p):
            ti = ti + store[CO, index] * (field[at(q), :] - mine)
        acc[0, at(p), :] += ti

    def section_row(c, q, mine):
        other = hs[FIELD, c, pl.ds(q, 1), :]
        return lambda a, index: (store[CO, index] * (other - mine[a]),)

    def drag_dirs(off, n, carry):
        d = lax.div(n, 8)
        p0 = lax.rem(n, 8) * 2
        g = [gfac[at(p0 + a), :] for a in range(2)]
        v = [[own[VX + c, at(p0 + a), :] for c in range(3)] for a in range(2)]
        total = [[zero] * 3 for _ in range(2)]
        for q in range(SLOTS):
            gj = gfar[lax.rem(d, 3), partner(q, off), :]
            vj = [far[lax.rem(d, 3), VX + c, partner(q, off), :] for c in range(3)]
            back = [None] * 3
            for a in range(2):
                w = store[KE, d * 256 + (p0 + a) * 16 + q] * (g[a] * gj)
                for c in range(3):
                    e = w * (vj[c] - v[a][c])
                    total[a][c] = total[a][c] + e
                    back[c] = e if back[c] is None else back[c] + e
            for c in range(3):
                kaccj[d, c, slot_sum(q), :] -= back[c]
        for a in range(2):
            for c in range(3):
                kacc[c, at(p0 + a), :] += total[a][c]
        return carry

    def drag_self(p):
        g = gfac[at(p), :]
        v = [own[VX + c, at(p), :] for c in range(3)]
        total = [zero] * 3
        for q, index, _ in self_partners(p):
            w = store[KE, index] * (g * gfac[at(q), :])
            for c in range(3):
                total[c] = total[c] + w * (own[VX + c, at(q), :] - v[c])
        for c in range(3):
            kacc[c, at(p), :] += total[c]

    def drag_row(c, q, mine):
        g, v = mine
        gj = hs[DRAG, c, pl.ds(q, 1), :]
        vj = [rowfar[c, VX + x, pl.ds(q, 1), :] for x in range(3)]

        def terms(a, index):
            w = store[KE, index] * (g[a] * gj)
            return [w * (vj[x] - v[a][x]) for x in range(3)]

        return terms

    def drag_column(c, mine, index):
        g, v = mine
        w = store[KE, index] * (g * cf[DRAG, c])
        return [w * (colfar[c, VX + x] - v[x]) for x in range(3)]

    def drag_rim():
        rim(
            kacc,
            3,
            lambda side: (
                [rsend[0, side, DRAG, half(a), :] for a in range(2)],
                [[rowsend0[side, VX + x, half(a), :] for x in range(3)] for a in range(2)],
            ),
            drag_row,
            lambda side: (oc[DRAG, side], [colown[side, VX + x] for x in range(3)]),
            drag_column,
        )

    def push_dirs(off, n, carry):
        d = lax.div(n, 8)
        p0 = lax.rem(n, 8) * 2
        pi = [field[at(p0 + a), :] for a in range(2)]
        total = [[zero] * 3 for _ in range(2)]
        for q in range(SLOTS):
            pj = sfar[lax.rem(d, 3), partner(q, off), :]
            back = [None] * 3
            for a in range(2):
                both = pi[a] + pj
                for c in range(3):
                    e = both * store[WX + c, d * 256 + (p0 + a) * 16 + q]
                    total[a][c] = total[a][c] + e
                    back[c] = e if back[c] is None else back[c] + e
            for c in range(3):
                kaccj[d, c, slot_sum(q), :] -= back[c]
        for a in range(2):
            for c in range(3):
                kacc[c, at(p0 + a), :] += total[a][c]
        return carry

    def push_self(p):
        pi = field[at(p), :]
        total = [zero] * 3
        for q, index, reverse in self_partners(p):
            both = pi + field[at(q), :]
            for c in range(3):
                e = both * store[WX + c, index]
                total[c] = total[c] - e if reverse else total[c] + e
        for c in range(3):
            kacc[c, at(p), :] += total[c]

    def push_row(c, q, mine):
        pj = hs[FIELD, c, pl.ds(q, 1), :]

        def terms(a, index):
            both = mine[a] + pj
            return [both * store[WX + x, index] for x in range(3)]

        return terms

    def push_column(c, mine, index):
        both = mine + cf[FIELD, c]
        return [both * store[WX + x, index] for x in range(3)]

    for side in range(2):
        packed = gfac[edge_row(side), :]
        for e in range(ROUNDS):
            rsend[e, side, DRAG] = packed
    packed = packed_columns(lambda p: gfac[at(p), :])
    for e in range(ROUNDS):
        vsend[e, DRAG] = packed

    polynomial = section_polynomial(SECTIONS)

    def spread(e, kind):
        for side in range(2):
            h = rrecv[e, side, kind]
            hl, hr = drecv[e, side * 2, kind], drecv[e, side * 2 + 1, kind]
            hs[kind, side * 3] = pltpu.roll(jnp.where(lane16 == COLS - 1, hl, h), 1, 1)
            hs[kind, side * 3 + 1] = h
            hs[kind, side * 3 + 2] = pltpu.roll(jnp.where(lane16 == 0, hr, h), COLS - 1, 1)
            oc[kind, side] = gather(vsend[e, kind], own_index[side])
            for h in range(2):
                v = gather(vrecv[e, side, kind], far_index[side][h])
                for number, value in enumerate((pltpu.roll(v, 1, 0), v, pltpu.roll(v, ROWS - 1, 0))):
                    cf[kind, side * 6 + number * 2 + h] = value

    def one_round(e):
        for side in range(2):
            rsend[e, side, FIELD] = field[edge_row(side), :]
        vsend[e, FIELD] = packed_columns(lambda p: field[at(p), :])
        for copy in round_copies(e - 1) if e else opening_copies():
            copy.wait_send()
        for copy in round_copies(e):
            copy.start()

        if e < 3:
            over(section_dirs, 0, 16, 4)
            for p in range(SLOTS):
                section_self(p)

        if e == 0:
            paired(drag_self)

        if e == 2:
            drag_rim()

        if e < 3:
            over(drag_dirs, (0, 8, 20)[e], (8, 20, 32)[e], 8)

        if e == 3:
            over(push_dirs, 0, 32, 8)
            for p in range(SLOTS):
                push_self(p)

        for copy in round_copies(e):
            copy.wait_recv()
        for kind in range(2 if e == 0 else 1):
            spread(e, kind)

        if e < 3:
            rim(
                acc,
                1,
                lambda side: [rsend[e, side, FIELD, half(a), :] for a in range(2)],
                section_row,
                lambda side: oc[FIELD, side],
                lambda c, mine, index: (store[CO, index] * (cf[FIELD, c] - mine),),
            )

        def power(p):
            return jnp.where(p < pop[...], total_of(acc, accj, 0, p) / cap[p], 0.0)

        if e == 1:
            stage_finish(2)
            best = msrc[3]
            for shift in (4, 2, 1):
                best = jnp.maximum(best, pltpu.roll(best, shift, 0))
            for shift in (64, 32, 16, 8, 4, 2, 1):
                best = jnp.maximum(best, pltpu.roll(best, shift, 1))
            msrc[4] = COURANT / best

        if e < 2:

            def update(p):
                u = power(p)
                powers[e + 1, p] = u
                set_field(p, u)

            for p in range(SLOTS):
                update(p)
            for p in range(SLOTS):
                clear(p)

        if e == 2:
            step_dt = msrc[4]

            def update(p):
                y = step_dt * (polynomial[4] * power(p))
                for k in (3, 2, 1):
                    y = step_dt * (polynomial[k] * powers[k - 1, p] + y)
                y = polynomial[0] * own[F, at(p), :] + y
                heated[p] = y
                set_field(p, pfac[p] * y)

            for p in range(SLOTS):
                update(p)

        if e == 3:
            rim(
                kacc,
                3,
                lambda side: [rsend[e, side, FIELD, half(a), :] for a in range(2)],
                push_row,
                lambda side: oc[FIELD, side],
                push_column,
            )

    for e in range(ROUNDS):
        one_round(e)

    def finish(p):
        live = p < pop[...]
        scale = jnp.where(live, msrc[4] / own[M, at(p), :], 0.0)
        for c in range(3):
            moved[c, p] = own[VX + c, at(p), :] + scale * total_of(kacc, kaccj, c, p)

    for p in range(SLOTS):
        finish(p)

    for copy in round_copies(ROUNDS - 1):
        copy.wait_send()
    for stage in range(3):
        each(stage_size[stage], lambda k, stage=stage: stage_copy(stage, k).wait_send())


def hand_over(heated_in, moved_in, heated, moved, sem):
    copies = [
        pltpu.make_async_copy(heated_in, heated, sem.at[0]),
        pltpu.make_async_copy(moved_in, moved, sem.at[1]),
    ]
    for copy in copies:
        copy.start()
    for copy in copies:
        copy.wait()


def body(sizes, *args):
    f32 = jnp.float32
    messages = sum(sizes) - 3
    tile = (SLOTS, ROWS, COLS)
    vmem = pl.BlockSpec(memory_space=pltpu.VMEM)
    scratch = [pltpu.VMEM(a.shape, a.dtype) for a in args] + [
        pltpu.VMEM((3, QUANTITIES, FLAT + PAD, COLS), f32),
        pltpu.VMEM((3,) + tile, f32),
        pltpu.VMEM(tile, f32),
        pltpu.VMEM((3, FLAT + PAD, COLS), f32),
        pltpu.VMEM((3, FLAT + PAD, COLS), f32),
        pltpu.VMEM((2, FLAT, COLS), f32),
        pltpu.VMEM((DIRECTIONS, 2, PAD + FLAT, COLS), f32),
        pltpu.VMEM((3, FLAT, COLS), f32),
        pltpu.VMEM((DIRECTIONS, 3, PAD + FLAT, COLS), f32),
        pltpu.VMEM((5, PAIRS, ROWS, COLS), f32),
        pltpu.VMEM((2, QUANTITIES, SLOTS, COLS), f32),
        pltpu.VMEM((2, QUANTITIES, SLOTS, COLS), f32),
        pltpu.VMEM((QUANTITIES, ROWS, COLS), f32),
        pltpu.VMEM((2, QUANTITIES, ROWS, COLS), f32),
        pltpu.VMEM((2, SLOTS, COLS), f32),
        pltpu.VMEM((4, SLOTS, COLS), f32),
        pltpu.VMEM((6, QUANTITIES, SLOTS, COLS), f32),
        pltpu.VMEM((12, QUANTITIES, ROWS, COLS), f32),
        pltpu.VMEM((2, QUANTITIES, ROWS, COLS), f32),
        pltpu.VMEM((2, 3, ROWS, COLS), f32),
        pltpu.VMEM((ROUNDS, 2, 2, SLOTS, COLS), f32),
        pltpu.VMEM((ROUNDS, 2, 2, SLOTS, COLS), f32),
        pltpu.VMEM((ROUNDS, 2, ROWS, COLS), f32),
        pltpu.VMEM((ROUNDS, 2, 2, ROWS, COLS), f32),
        pltpu.VMEM((ROUNDS, 4, 2, SLOTS, COLS), f32),
        pltpu.VMEM((2, 6, SLOTS, COLS), f32),
        pltpu.VMEM((2, 12, ROWS, COLS), f32),
        pltpu.VMEM((2, 2, ROWS, COLS), f32),
        pltpu.VMEM((5, ROWS, COLS), f32),
        pltpu.VMEM((messages, ROWS, COLS), f32),
        pltpu.SemaphoreType.DMA((8,)),
        pltpu.SemaphoreType.DMA((2, 8)),
        pltpu.SemaphoreType.DMA((messages,)),
        pltpu.SemaphoreType.DMA((messages,)),
        pltpu.SemaphoreType.DMA((8,)),
    ]
    shapes = (jax.ShapeDtypeStruct(tile, f32), jax.ShapeDtypeStruct((3,) + tile, f32))
    results = pl.pallas_call(
        functools.partial(kernel, sizes),
        out_shape=shapes,
        in_specs=[pl.BlockSpec(memory_space=pl.ANY)] * 8,
        out_specs=(vmem, vmem),
        scratch_shapes=scratch,
        compiler_params=pltpu.CompilerParams(
            collective_id=0, has_side_effects=True, vmem_limit_bytes=60 * 1024 * 1024
        ),
        name="sections_and_kick",
    )(*args)
    anywhere = pl.BlockSpec(memory_space=pl.ANY)
    return pl.pallas_call(
        hand_over,
        out_shape=shapes,
        in_specs=[anywhere] * 2,
        out_specs=(anywhere, anywhere),
        scratch_shapes=[pltpu.SemaphoreType.DMA((2,))],
        compiler_params=pltpu.CompilerParams(vmem_limit_bytes=60 * 1024 * 1024),
        name="hand_over",
    )(*results)


def solution(mesh):
    n_gx, n_gy = mesh.shape["gx"], mesh.shape["gy"]
    n_hi = 4 if n_gy % 4 == 0 and n_gy > 4 else 2
    sizes = (n_gx, n_gy // n_hi, n_hi)
    cells = P("gy", "gx")
    one = P(None, "gy", "gx")
    many = P(None, None, "gy", "gx")
    return jax.shard_map(
        functools.partial(body, sizes),
        mesh=mesh,
        in_specs=(cells, many, many, one, one, one, one, many),
        out_specs=(one, many),
        check_vma=False,
    )
```

```python
import functools

import jax
import jax.numpy as jnp
from jax import lax
from jax.experimental import pallas as pl
from jax.experimental.pallas import tpu as pltpu
from jax.sharding import PartitionSpec as P

SECTIONS = 4
ISO_PART = 0.1
HEAT_RATIO = 5.0 / 3.0
COURANT = 0.3
ROOT_HALF = 0.5**0.5
MESH = pl.DeviceIdType.MESH

SLOTS = 16
ROWS = 8
COLS = 128
FLAT = SLOTS * ROWS

X, Y, Z, BX, BY, BZ, KA, F, M, VX, VY, VZ = range(12)
QUANTITIES = 12

DIRECTIONS = 4

CO, KE, WX, WY, WZ = range(5)
SELF_AT = DIRECTIONS * SLOTS * SLOTS
ROW_AT = SELF_AT + SLOTS * 8
COL_AT = ROW_AT + 6 * SLOTS * 2
PAIRS = COL_AT + 12

ROUNDS = 4
FIELD, DRAG = range(2)

EMPTY_Z = 10.0
OUTSIDE_X = 20.0
EDGE_Z = 40.0
PAD = 8

SIN = (0.9999999957157406, -0.1666665796974384, 0.008333050613415454, -0.0001980904606136566, 2.605165590448684e-06)
COS = (
    0.9999999997798981,
    -0.4999999935694129,
    0.04166663620835954,
    -0.001388836083517328,
    2.476013513307355e-05,
    -2.605106944029617e-07,
)


def section_polynomial(section_total):
    weight = 4.0 / (section_total * section_total + section_total - 2)
    series = [1.0 / 3.0, 1.0 / 3.0, 1.0 / 3.0]
    for j in range(3, section_total + 1):
        series.append((j * j + j - 2) / (2.0 * j * (j + 1)))

    def padded(values):
        return values + [0.0] * (section_total + 1 - len(values))

    before, now = padded([1.0]), padded([1.0, series[1] * weight])
    for j in range(2, section_total + 1):
        m = (2 * j - 1) / j * series[j] / series[j - 1]
        n = -(j - 1) / j * series[j] / series[j - 2]
        after = [m * a + n * b for a, b in zip(now, before)]
        after[0] += 1.0 - m - n
        after[1] -= (1.0 - series[j - 1]) * m * weight
        for k in range(section_total):
            after[k + 1] += m * weight * now[k]
        before, now = now, after
    return now


def horner(coefs, t):
    total = jnp.full_like(t, coefs[-1])
    for c in coefs[-2::-1]:
        total = total * t + c
    return total


def sin_cos(angle):
    half = 0.5 * angle
    t = half * half
    s = half * horner(SIN, t)
    c = horner(COS, t)
    return 2.0 * s * c, 1.0 - 2.0 * s * s


def pair_terms(i, j):
    dx, dy, dz = i[X] - j[X], i[Y] - j[Y], i[Z] - j[Z]
    s = jnp.maximum(1.0 - (dx * dx + dy * dy + dz * dz), 0.0)
    s2 = s * s
    own = i[BX] * dx + i[BY] * dy + i[BZ] * dz
    far = j[BX] * dx + j[BY] * dy + j[BZ] * dz
    co = (s2 * s) * (ISO_PART + (own * own + far * far)) * (i[KA] + j[KA])
    w = s2 * (i[M] * j[M])
    return co, w * s, w * dx, w * dy, w * dz


def kernel(
    sizes,
    pop_in,
    loc_in,
    tilt_in,
    mass_in,
    kappa_in,
    cap_in,
    temp_in,
    mot_in,
    heated,
    moved,
    pop,
    loc,
    tilt,
    mass,
    kappa,
    cap,
    temp,
    mot,
    far,
    powers,
    pfac,
    sfar,
    gfar,
    acc,
    accj,
    kacc,
    kaccj,
    store,
    rowsend0,
    rowrecv0,
    colsend0,
    colrecv0,
    cbsend,
    cbrecv,
    rowfar,
    colfar,
    colown,
    coltot,
    rsend,
    rrecv,
    vsend,
    vrecv,
    drecv,
    hs,
    cf,
    oc,
    msrc,
    mrecv,
    send_sem,
    recv_sem,
    msend_sem,
    mrecv_sem,
    load_sem,
):
    own, field, gfac = far.at[2], sfar.at[2], gfar.at[2]
    loads = [
        pltpu.make_async_copy(src, dst, load_sem.at[number])
        for number, (src, dst) in enumerate(
            (
                (pop_in, pop),
                (loc_in, loc),
                (tilt_in, tilt),
                (mass_in, mass),
                (kappa_in, kappa),
                (cap_in, cap),
                (temp_in, temp),
                (mot_in, mot),
            )
        )
    ]
    for load in loads:
        load.start()

    n_gx, n_lo, n_hi = sizes
    n_gy = n_lo * n_hi
    gx = lax.axis_index("gx")
    gy = lax.axis_index("gy")
    left, right = lax.rem(gx + n_gx - 1, n_gx), lax.rem(gx + 1, n_gx)
    up, down = lax.rem(gy + n_gy - 1, n_gy), lax.rem(gy + 1, n_gy)
    lo, hi = lax.rem(gy, n_lo), lax.div(gy, n_lo)

    around = ((gx, up), (gx, down), (left, gy), (right, gy), (left, up), (right, up), (left, down), (right, down))

    stage_size = (n_gx - 1, n_lo - 1, n_hi - 1)
    stage_at = (0, n_gx - 1, n_gx + n_lo - 2)

    def stage_device(stage, k):
        if stage == 0:
            return (lax.rem(gx + k + 1, n_gx), gy)
        if stage == 1:
            return (gx, hi * n_lo + lax.rem(lo + k + 1, n_lo))
        return (gx, lax.rem(hi + k + 1, n_hi) * n_lo + lo)

    def each(count, fn):
        def run(k, carry):
            fn(k)
            return carry

        lax.fori_loop(0, count, run, 0)

    def grouped(count, size, fn, carry):
        def run(k, carry):
            for a in range(size):
                carry = fn(k * size + a, carry)
            return carry

        return lax.fori_loop(0, count // size, run, carry)

    def over(fn, first, last, split):
        if first < split:
            lax.fori_loop(first, split, functools.partial(fn, 0), 0)
        if last > split:
            lax.fori_loop(max(first, split), last, functools.partial(fn, 1), 0)

    def paired(fn):
        def both(p):
            fn(2 * p)
            fn(2 * p + 1)

        each(SLOTS // 2, both)

    barrier = pltpu.get_barrier_semaphore()

    def greet(device):
        pl.semaphore_signal(barrier, inc=1, device_id=device, device_id_type=MESH)

    for device in around:
        greet(device)
    for stage in range(3):
        each(stage_size[stage], lambda k, stage=stage: greet(stage_device(stage, k)))

    lane = lax.broadcasted_iota(jnp.int32, (ROWS, COLS), 1)
    row = lax.broadcasted_iota(jnp.int32, (ROWS, COLS), 0)
    lane16 = lax.broadcasted_iota(jnp.int32, (SLOTS, COLS), 1)
    zero = jnp.zeros((ROWS, COLS), jnp.float32)
    rows_down = row.astype(jnp.float32)

    def at(p):
        start = p * ROWS
        return pl.ds(start if isinstance(p, int) else pl.multiple_of(start, ROWS), ROWS)

    def edge_row(side):
        return pl.ds(side * (ROWS - 1), SLOTS, stride=ROWS)

    def half(a):
        return pl.ds(a * 8, 8)

    def partner(q, off):
        return pl.ds(q * ROWS + off, ROWS)

    def slot_sum(q):
        start = PAD + q * ROWS
        return pl.ds(start if isinstance(q, int) else pl.multiple_of(start, ROWS), ROWS)

    def put_copies(target, k, p, value):
        target[(0, *k, at(p))] = pltpu.roll(value, COLS - 1, 1)
        target[(1, *k, at(p))] = pltpu.roll(value, 1, 1)
        target[(2, *k, at(p))] = value

    def gather(v, index):
        return jnp.take_along_axis(v, index, axis=1)

    def packed_columns(tile_of):
        v = tile_of(0)
        for p in range(1, SLOTS):
            mask = (lane == 8 * p) | (lane == 8 * p - 1)
            v = jnp.where(mask, pltpu.roll(tile_of(p), 8 * p, 1), v)
        return v

    group = lane & ~7
    within = (lane & 7) * 8
    own_index = (group, (group + (COLS - 1)) & (COLS - 1))
    far_index = (
        ((within + (COLS - 1)) & (COLS - 1), (within + 63) & (COLS - 1)),
        (within, within + 64),
    )

    def prepare(p, fastest):
        live = p < pop[...]
        sin_p, cos_p = sin_cos(tilt[0, p])
        sin_a, cos_a = sin_cos(tilt[1, p])
        t = temp[p]
        v = [mot[c, p] for c in range(3)]
        values = [
            loc[0, p],
            loc[1, p] + rows_down,
            jnp.where(live, loc[2, p], EMPTY_Z),
            ROOT_HALF * (sin_p * cos_a),
            ROOT_HALF * (sin_p * sin_a),
            ROOT_HALF * cos_p,
            0.5 * kappa[p],
            t,
            mass[p],
        ] + v
        for k in range(QUANTITIES):
            own[k, at(p), :] = values[k]
        for c in range(2):
            acc[c, at(p), :] = zero
        for c in range(3):
            kacc[c, at(p), :] = zero
        speed = jnp.sqrt(HEAT_RATIO * (HEAT_RATIO - 1.0) * t) + jnp.sqrt(v[0] * v[0] + v[1] * v[1] + v[2] * v[2])
        return jnp.maximum(fastest, jnp.where(live, speed, 0.0))

    after = pl.ds(FLAT, PAD)
    for copy in range(3):
        for k in range(QUANTITIES):
            far[copy, k, after, :] = zero
        sfar[copy, after, :] = zero
        gfar[copy, after, :] = zero
    for d in range(DIRECTIONS):
        for c in range(2):
            accj[d, c, pl.ds(0, PAD), :] = zero
        for c in range(3):
            kaccj[d, c, pl.ds(0, PAD), :] = zero
    for load in loads:
        load.wait()
    msrc[0] = grouped(SLOTS, 4, prepare, zero)

    def pack(k, cb):
        cb = list(cb)
        for side in range(2):
            packed = own[k, edge_row(side), :]
            rowsend0[side, k] = packed
            mask = (lane16 == 2 * k) | (lane16 == 2 * k + 1)
            cb[side] = jnp.where(mask, pltpu.roll(packed, 2 * k + 1, 1), cb[side])
        colsend0[k] = packed_columns(lambda p: own[k, at(p), :])
        return tuple(cb)

    blank = jnp.zeros((SLOTS, COLS), jnp.float32)
    cbsend[0], cbsend[1] = grouped(QUANTITIES, 3, pack, (blank, blank))

    def remote(src, dst, s, r, device):
        return pltpu.make_async_remote_copy(
            src_ref=src, dst_ref=dst, send_sem=s, recv_sem=r, device_id=device, device_id_type=MESH
        )

    def stage_copy(stage, k):
        slot = stage_at[stage] + k
        return remote(
            msrc.at[stage], mrecv.at[slot], msend_sem.at[slot], mrecv_sem.at[slot], stage_device(stage, k)
        )

    def stage_start(stage):
        each(stage_size[stage], lambda k: stage_copy(stage, k).start())

    def stage_finish(stage):
        def take(k, best):
            stage_copy(stage, k).wait_recv()
            return jnp.maximum(best, mrecv[stage_at[stage] + k])

        msrc[stage + 1] = lax.fori_loop(0, stage_size[stage], take, msrc[stage])

    def opening_copies():
        plan = (
            (rowsend0.at[0], rowrecv0.at[1]),
            (rowsend0.at[1], rowrecv0.at[0]),
            (colsend0, colrecv0.at[1]),
            (colsend0, colrecv0.at[0]),
            (cbsend.at[0], cbrecv.at[3]),
            (cbsend.at[0], cbrecv.at[2]),
            (cbsend.at[1], cbrecv.at[1]),
            (cbsend.at[1], cbrecv.at[0]),
        )
        return [
            remote(src, dst, send_sem.at[c], recv_sem.at[1, c], around[c])
            for c, (src, dst) in enumerate(plan)
        ]

    def round_copies(e):
        kinds = pl.ds(0, 2 if e == 0 else 1)
        plan = (
            (rsend.at[e, 0, kinds], rrecv.at[e, 1, kinds]),
            (rsend.at[e, 1, kinds], rrecv.at[e, 0, kinds]),
            (vsend.at[e, kinds], vrecv.at[e, 1, kinds]),
            (vsend.at[e, kinds], vrecv.at[e, 0, kinds]),
            (rsend.at[e, 0, kinds], drecv.at[e, 3, kinds]),
            (rsend.at[e, 0, kinds], drecv.at[e, 2, kinds]),
            (rsend.at[e, 1, kinds], drecv.at[e, 1, kinds]),
            (rsend.at[e, 1, kinds], drecv.at[e, 0, kinds]),
        )
        return [
            remote(src, dst, send_sem.at[c], recv_sem.at[e % 2, c], around[c]) for c, (src, dst) in enumerate(plan)
        ]

    pl.semaphore_wait(barrier, len(around) + sum(stage_size))
    for copy in opening_copies():
        copy.start()
    stage_start(0)

    PASS1 = range(9)

    def put(index, terms):
        for c in range(5):
            store[c, index] = terms[c]

    def first_self(p, carry):
        mine = [own[k, at(p), :] for k in PASS1]
        ti, ri = zero, zero
        for step in range(1, 9):
            q = lax.rem(p + step, SLOTS)
            other = [own[k, at(q), :] for k in PASS1]
            terms = pair_terms(mine, other)
            put(SELF_AT + p * 8 + (step - 1), terms)
            t = terms[CO] * (other[F] - mine[F])
            ti = ti + t
            ri = ri + terms[KE]
            if step < 8:
                acc[0, at(q), :] -= t
                acc[1, at(q), :] += terms[KE]
        acc[0, at(p), :] += ti
        acc[1, at(p), :] += ri
        for k in range(QUANTITIES):
            value = own[k, at(p), :]
            east, west = pltpu.roll(value, COLS - 1, 1), pltpu.roll(value, 1, 1)
            if k == X:
                east = jnp.where(lane == COLS - 1, OUTSIDE_X, east + 1.0)
                west = jnp.where(lane == 0, OUTSIDE_X, west - 1.0)
            far[0, k, at(p), :] = east
            far[1, k, at(p), :] = west
        for d in range(DIRECTIONS):
            for c in range(2):
                accj[d, c, slot_sum(p), :] = zero
            for c in range(3):
                kaccj[d, c, slot_sum(p), :] = zero
        return carry

    def first_dirs(off, n, carry):
        d = lax.div(n, 8)
        p0 = lax.rem(n, 8) * 2
        mine = [[own[k, at(p0 + a), :] for k in PASS1] for a in range(2)]
        ti = [zero, zero]
        ri = [zero, zero]
        for q in range(SLOTS):
            other = [far[lax.rem(d, 3), k, partner(q, off), :] for k in PASS1]
            tj, rj = None, None
            for a in range(2):
                terms = pair_terms(mine[a], other)
                put(d * 256 + (p0 + a) * 16 + q, terms)
                t, r = terms[CO] * (other[F] - mine[a][F]), terms[KE]
                ti[a] = ti[a] + t
                ri[a] = ri[a] + r
                tj = t if tj is None else tj + t
                rj = r if rj is None else rj + r
            accj[d, 0, slot_sum(q), :] -= tj
            accj[d, 1, slot_sum(q), :] += rj
        for a in range(2):
            acc[0, at(p0 + a), :] += ti[a]
            acc[1, at(p0 + a), :] += ri[a]
        return carry

    lax.fori_loop(0, SLOTS, first_self, 0)
    over(first_dirs, 0, 32, 8)
    stage_finish(0)
    stage_start(1)

    for copy in opening_copies():
        copy.wait_recv()

    def rows_around(k, carry):
        for side in range(2):
            h = rowrecv0[side, k]
            cl = pltpu.roll(cbrecv[side * 2], lax.rem(COLS - 2 * k, COLS), 1)
            cr = pltpu.roll(cbrecv[side * 2 + 1], COLS - 2 - 2 * k, 1)
            rowfar[side * 3, k] = jnp.where(lane16 == 0, cl, pltpu.roll(h, 1, 1))
            rowfar[side * 3 + 1, k] = h
            rowfar[side * 3 + 2, k] = jnp.where(lane16 == COLS - 1, cr, pltpu.roll(h, COLS - 1, 1))
            colown[side, k] = gather(colsend0[k], own_index[side])
            for h in range(2):
                v = gather(colrecv0[side, k], far_index[side][h])
                for number, value in enumerate((pltpu.roll(v, 1, 0), v, pltpu.roll(v, ROWS - 1, 0))):
                    colfar[side * 6 + number * 2 + h, k] = value
        return carry

    grouped(QUANTITIES, 4, rows_around, 0)

    z_side = (jnp.where(gy == 0, EDGE_Z, 0.0), jnp.where(gy == n_gy - 1, EDGE_Z, 0.0))
    z_end = (jnp.where(gx == 0, EDGE_Z, 0.0), jnp.where(gx == n_gx - 1, EDGE_Z, 0.0))
    z_lane = (
        jnp.where(lane16 == 0, z_end[0], 0.0),
        jnp.zeros((SLOTS, COLS), jnp.float32),
        jnp.where(lane16 == COLS - 1, z_end[1], 0.0),
    )
    for side in range(2):
        for number in range(3):
            c = side * 3 + number
            if number != 1:
                rowfar[c, X] = rowfar[c, X] + float(number - 1)
            rowfar[c, Y] = rowfar[c, Y] + float(-ROWS if side == 0 else ROWS)
            rowfar[c, Z] = rowfar[c, Z] + (z_lane[number] + z_side[side])
            for h in range(2):
                c = side * 6 + number * 2 + h
                colfar[c, X] = colfar[c, X] + (-1.0 if side == 0 else 1.0)
                colfar[c, Z] = colfar[c, Z] + z_end[side]

    def scatter_rows(target, c, side, halves):
        target[c, edge_row(side), :] = target[c, edge_row(side), :] + jnp.concatenate(halves, axis=0)

    def group_sum(v):
        v = v + pltpu.roll(v, COLS - 1, 1)
        v = v + pltpu.roll(v, COLS - 2, 1)
        return v + pltpu.roll(v, COLS - 4, 1)

    ends = (lane == 0) | (lane == COLS - 1)

    def scatter_columns(target, count):
        combined = []
        for c in range(count):
            u = jnp.where((lane & 7) == 0, group_sum(coltot[0, c]), 0.0)
            combined.append(jnp.where((lane & 7) == 7, pltpu.roll(group_sum(coltot[1, c]), COLS - 1, 1), u))

        def add(p):
            for c in range(count):
                v = pltpu.roll(combined[c], (COLS - 8 * p) % COLS, 1) if p else combined[c]
                target[c, at(p), :] += jnp.where(ends, v, 0.0)

        for p in range(SLOTS):
            add(p)

    def rim(target, count, row_mine, row_terms, col_mine, col_terms):
        def one_side(side):
            mine = row_mine(side)

            def one_row(number, totals):
                total = list(totals)
                c = side * 3 + number
                for q in range(SLOTS):
                    add = row_terms(c, q, mine)
                    for a in range(2):
                        for x, e in enumerate(add(a, ROW_AT + (c * 16 + q) * 2 + a)):
                            total[a * count + x] = total[a * count + x] + e
                return tuple(total)

            total = (zero,) * (2 * count)
            if count == 1:
                for number in range(3):
                    total = one_row(number, total)
            else:
                total = lax.fori_loop(0, 3, one_row, total)
            for x in range(count):
                scatter_rows(target, x, side, [total[x], total[count + x]])

            mine_col = col_mine(side)

            def one_column(number, totals):
                c = side * 6 + number
                return tuple(t + e for t, e in zip(totals, col_terms(c, mine_col, COL_AT + c)))

            total = (zero,) * count
            for number in range(6):
                total = one_column(number, total)
            for x in range(count):
                coltot[side, x] = total[x]

        for side in range(2):
            one_side(side)
        scatter_columns(target, count)

    def first_terms(mine, other, index):
        terms = pair_terms(mine, other)
        put(index, terms)
        return terms[CO] * (other[F] - mine[F]), terms[KE]

    def first_row(c, q, mine):
        other = [rowfar[c, k, pl.ds(q, 1), :] for k in PASS1]
        return lambda a, index: first_terms(mine[a], other, index)

    rim(
        acc,
        2,
        lambda side: [[rowsend0[side, k, half(a), :] for k in PASS1] for a in range(2)],
        first_row,
        lambda side: [colown[side, k] for k in PASS1],
        lambda c, mine, index: first_terms(mine, [colfar[c, k] for k in PASS1], index),
    )
    def total_of(target, per_dir, c, p):
        below = pl.ds(PAD + p * ROWS - 1, ROWS)
        east = per_dir[0, c, slot_sum(p), :] + per_dir[3, c, below, :]
        west = per_dir[1, c, below, :]
        total = target[c, at(p), :] + per_dir[2, c, below, :]
        return total + pltpu.roll(east, 1, 1) + pltpu.roll(west, COLS - 1, 1)

    def clear(p):
        acc[0, at(p), :] = zero
        for d in range(DIRECTIONS):
            accj[d, 0, slot_sum(p), :] = zero

    def set_field(p, value):
        put_copies(sfar, (), p, value)

    def first_update(p):
        live = p < pop[...]
        m = own[M, at(p), :]
        density = jnp.where(live, m + total_of(acc, accj, 1, p) / m, 1.0)
        inverse = 1.0 / density
        g = ROOT_HALF * inverse
        put_copies(gfar, (), p, g)
        pfac[p] = 6.0 * (HEAT_RATIO - 1.0) * inverse
        u = jnp.where(live, total_of(acc, accj, 0, p) / cap[p], 0.0)
        powers[0, p] = u
        set_field(p, u)

    for p in range(SLOTS):
        first_update(p)
    for p in range(SLOTS):
        clear(p)

    def section_dirs(off, n, carry):
        d = lax.div(n, 4)
        p0 = lax.rem(n, 4) * 4
        mine = [field[at(p0 + a), :] for a in range(4)]
        ti = [zero] * 4
        for q in range(SLOTS):
            other = sfar[lax.rem(d, 3), partner(q, off), :]
            tj = None
            for a in range(4):
                t = store[CO, d * 256 + (p0 + a) * 16 + q] * (other - mine[a])
                ti[a] = ti[a] + t
                tj = t if tj is None else tj + t
            accj[d, 0, slot_sum(q), :] -= tj
        for a in range(4):
            acc[0, at(p0 + a), :] += ti[a]
        return carry

    def wrap(p):
        return p % SLOTS if isinstance(p, int) else lax.rem(p, SLOTS)

    def self_partners(p):
        for step in range(1, 9):
            yield wrap(p + step), SELF_AT + p * 8 + (step - 1), False
        for step in range(1, 8):
            q = wrap(p + SLOTS - step)
            yield q, SELF_AT + q * 8 + (step - 1), True

    def section_self(p):
        mine = field[at(p), :]
        ti = zero
        for q, index, _ in self_partners(p):
            ti = ti + store[CO, index] * (field[at(q), :] - mine)
        acc[0, at(p), :] += ti

    def section_row(c, q, mine):
        other = hs[FIELD, c, pl.ds(q, 1), :]
        return lambda a, index: (store[CO, index] * (other - mine[a]),)

    def drag_dirs(off, n, carry):
        d = lax.div(n, 8)
        p0 = lax.rem(n, 8) * 2
        g = [gfac[at(p0 + a), :] for a in range(2)]
        v = [[own[VX + c, at(p0 + a), :] for c in range(3)] for a in range(2)]
        total = [[zero] * 3 for _ in range(2)]
        for q in range(SLOTS):
            gj = gfar[lax.rem(d, 3), partner(q, off), :]
            vj = [far[lax.rem(d, 3), VX + c, partner(q, off), :] for c in range(3)]
            back = [None] * 3
            for a in range(2):
                w = store[KE, d * 256 + (p0 + a) * 16 + q] * (g[a] * gj)
                for c in range(3):
                    e = w * (vj[c] - v[a][c])
                    total[a][c] = total[a][c] + e
                    back[c] = e if back[c] is None else back[c] + e
            for c in range(3):
                kaccj[d, c, slot_sum(q), :] -= back[c]
        for a in range(2):
            for c in range(3):
                kacc[c, at(p0 + a), :] += total[a][c]
        return carry

    def drag_self(p):
        g = gfac[at(p), :]
        v = [own[VX + c, at(p), :] for c in range(3)]
        total = [zero] * 3
        for q, index, _ in self_partners(p):
            w = store[KE, index] * (g * gfac[at(q), :])
            for c in range(3):
                total[c] = total[c] + w * (own[VX + c, at(q), :] - v[c])
        for c in range(3):
            kacc[c, at(p), :] += total[c]

    def drag_row(c, q, mine):
        g, v = mine
        gj = hs[DRAG, c, pl.ds(q, 1), :]
        vj = [rowfar[c, VX + x, pl.ds(q, 1), :] for x in range(3)]

        def terms(a, index):
            w = store[KE, index] * (g[a] * gj)
            return [w * (vj[x] - v[a][x]) for x in range(3)]

        return terms

    def drag_column(c, mine, index):
        g, v = mine
        w = store[KE, index] * (g * cf[DRAG, c])
        return [w * (colfar[c, VX + x] - v[x]) for x in range(3)]

    def drag_rim():
        rim(
            kacc,
            3,
            lambda side: (
                [rsend[0, side, DRAG, half(a), :] for a in range(2)],
                [[rowsend0[side, VX + x, half(a), :] for x in range(3)] for a in range(2)],
            ),
            drag_row,
            lambda side: (oc[DRAG, side], [colown[side, VX + x] for x in range(3)]),
            drag_column,
        )

    def push_dirs(off, n, carry):
        d = lax.div(n, 8)
        p0 = lax.rem(n, 8) * 2
        pi = [field[at(p0 + a), :] for a in range(2)]
        total = [[zero] * 3 for _ in range(2)]
        for q in range(SLOTS):
            pj = sfar[lax.rem(d, 3), partner(q, off), :]
            back = [None] * 3
            for a in range(2):
                both = pi[a] + pj
                for c in range(3):
                    e = both * store[WX + c, d * 256 + (p0 + a) * 16 + q]
                    total[a][c] = total[a][c] + e
                    back[c] = e if back[c] is None else back[c] + e
            for c in range(3):
                kaccj[d, c, slot_sum(q), :] -= back[c]
        for a in range(2):
            for c in range(3):
                kacc[c, at(p0 + a), :] += total[a][c]
        return carry

    def push_self(p):
        pi = field[at(p), :]
        total = [zero] * 3
        for q, index, reverse in self_partners(p):
            both = pi + field[at(q), :]
            for c in range(3):
                e = both * store[WX + c, index]
                total[c] = total[c] - e if reverse else total[c] + e
        for c in range(3):
            kacc[c, at(p), :] += total[c]

    def push_row(c, q, mine):
        pj = hs[FIELD, c, pl.ds(q, 1), :]

        def terms(a, index):
            both = mine[a] + pj
            return [both * store[WX + x, index] for x in range(3)]

        return terms

    def push_column(c, mine, index):
        both = mine + cf[FIELD, c]
        return [both * store[WX + x, index] for x in range(3)]

    for side in range(2):
        packed = gfac[edge_row(side), :]
        rsend[0, side, DRAG] = packed
    packed = packed_columns(lambda p: gfac[at(p), :])
    vsend[0, DRAG] = packed

    polynomial = section_polynomial(SECTIONS)

    def spread(e, kind):
        for side in range(2):
            h = rrecv[e, side, kind]
            hl, hr = drecv[e, side * 2, kind], drecv[e, side * 2 + 1, kind]
            hs[kind, side * 3] = pltpu.roll(jnp.where(lane16 == COLS - 1, hl, h), 1, 1)
            hs[kind, side * 3 + 1] = h
            hs[kind, side * 3 + 2] = pltpu.roll(jnp.where(lane16 == 0, hr, h), COLS - 1, 1)
            oc[kind, side] = gather(vsend[e, kind], own_index[side])
            for h in range(2):
                v = gather(vrecv[e, side, kind], far_index[side][h])
                for number, value in enumerate((pltpu.roll(v, 1, 0), v, pltpu.roll(v, ROWS - 1, 0))):
                    cf[kind, side * 6 + number * 2 + h] = value

    def one_round(e):
        for side in range(2):
            rsend[e, side, FIELD] = field[edge_row(side), :]
        vsend[e, FIELD] = packed_columns(lambda p: field[at(p), :])
        for copy in round_copies(e - 1) if e else opening_copies():
            copy.wait_send()
        for copy in round_copies(e):
            copy.start()

        if e < 3:
            over(section_dirs, 0, 16, 4)
            for p in range(SLOTS):
                section_self(p)

        if e == 0:
            paired(drag_self)

        if e == 2:
            drag_rim()

        if e < 3:
            over(drag_dirs, (0, 8, 20)[e], (8, 20, 32)[e], 8)

        if e == 3:
            over(push_dirs, 0, 32, 8)
            for p in range(SLOTS):
                push_self(p)

        if e == 0:
            stage_finish(1)
            stage_start(2)
        if e == 2:
            stage_finish(2)
            best = msrc[3]
            for shift in (4, 2, 1):
                best = jnp.maximum(best, pltpu.roll(best, shift, 0))
            for shift in (64, 32, 16, 8, 4, 2, 1):
                best = jnp.maximum(best, pltpu.roll(best, shift, 1))
            msrc[4] = COURANT / best

        for copy in round_copies(e):
            copy.wait_recv()
        for kind in range(2 if e == 0 else 1):
            spread(e, kind)

        if e < 3:
            rim(
                acc,
                1,
                lambda side: [rsend[e, side, FIELD, half(a), :] for a in range(2)],
                section_row,
                lambda side: oc[FIELD, side],
                lambda c, mine, index: (store[CO, index] * (cf[FIELD, c] - mine),),
            )

        def power(p):
            return jnp.where(p < pop[...], total_of(acc, accj, 0, p) / cap[p], 0.0)

        if e < 2:

            def update(p):
                u = power(p)
                powers[e + 1, p] = u
                set_field(p, u)

            for p in range(SLOTS):
                update(p)
            for p in range(SLOTS):
                clear(p)

        if e == 2:
            step_dt = msrc[4]

            def update(p):
                y = step_dt * (polynomial[4] * power(p))
                for k in (3, 2, 1):
                    y = step_dt * (polynomial[k] * powers[k - 1, p] + y)
                y = polynomial[0] * own[F, at(p), :] + y
                heated[p] = y
                set_field(p, pfac[p] * y)

            for p in range(SLOTS):
                update(p)

        if e == 3:
            rim(
                kacc,
                3,
                lambda side: [rsend[e, side, FIELD, half(a), :] for a in range(2)],
                push_row,
                lambda side: oc[FIELD, side],
                push_column,
            )

    for e in range(ROUNDS):
        one_round(e)

    def finish(p):
        live = p < pop[...]
        scale = jnp.where(live, msrc[4] / own[M, at(p), :], 0.0)
        for c in range(3):
            moved[c, p] = own[VX + c, at(p), :] + scale * total_of(kacc, kaccj, c, p)

    for p in range(SLOTS):
        finish(p)

    for copy in round_copies(ROUNDS - 1):
        copy.wait_send()
    for stage in range(3):
        each(stage_size[stage], lambda k, stage=stage: stage_copy(stage, k).wait_send())


def hand_over(heated_in, moved_in, heated, moved, heated_here, moved_here, in_sem, out_sem):
    ways = ((heated_in, heated_here, heated), (moved_in, moved_here, moved))
    loads = [pltpu.make_async_copy(src, here, in_sem.at[k]) for k, (src, here, _) in enumerate(ways)]
    stores = [pltpu.make_async_copy(here, dst, out_sem.at[k]) for k, (_, here, dst) in enumerate(ways)]
    for load in loads:
        load.start()
    for load, store in zip(loads, stores):
        load.wait()
        store.start()
    for store in stores:
        store.wait()


def body(sizes, *args):
    f32 = jnp.float32
    messages = sum(sizes) - 3
    tile = (SLOTS, ROWS, COLS)
    vmem = pl.BlockSpec(memory_space=pltpu.VMEM)
    scratch = [pltpu.VMEM(a.shape, a.dtype) for a in args] + [
        pltpu.VMEM((3, QUANTITIES, FLAT + PAD, COLS), f32),
        pltpu.VMEM((3,) + tile, f32),
        pltpu.VMEM(tile, f32),
        pltpu.VMEM((3, FLAT + PAD, COLS), f32),
        pltpu.VMEM((3, FLAT + PAD, COLS), f32),
        pltpu.VMEM((2, FLAT, COLS), f32),
        pltpu.VMEM((DIRECTIONS, 2, PAD + FLAT, COLS), f32),
        pltpu.VMEM((3, FLAT, COLS), f32),
        pltpu.VMEM((DIRECTIONS, 3, PAD + FLAT, COLS), f32),
        pltpu.VMEM((5, PAIRS, ROWS, COLS), f32),
        pltpu.VMEM((2, QUANTITIES, SLOTS, COLS), f32),
        pltpu.VMEM((2, QUANTITIES, SLOTS, COLS), f32),
        pltpu.VMEM((QUANTITIES, ROWS, COLS), f32),
        pltpu.VMEM((2, QUANTITIES, ROWS, COLS), f32),
        pltpu.VMEM((2, SLOTS, COLS), f32),
        pltpu.VMEM((4, SLOTS, COLS), f32),
        pltpu.VMEM((6, QUANTITIES, SLOTS, COLS), f32),
        pltpu.VMEM((12, QUANTITIES, ROWS, COLS), f32),
        pltpu.VMEM((2, QUANTITIES, ROWS, COLS), f32),
        pltpu.VMEM((2, 3, ROWS, COLS), f32),
        pltpu.VMEM((ROUNDS, 2, 2, SLOTS, COLS), f32),
        pltpu.VMEM((ROUNDS, 2, 2, SLOTS, COLS), f32),
        pltpu.VMEM((ROUNDS, 2, ROWS, COLS), f32),
        pltpu.VMEM((ROUNDS, 2, 2, ROWS, COLS), f32),
        pltpu.VMEM((ROUNDS, 4, 2, SLOTS, COLS), f32),
        pltpu.VMEM((2, 6, SLOTS, COLS), f32),
        pltpu.VMEM((2, 12, ROWS, COLS), f32),
        pltpu.VMEM((2, 2, ROWS, COLS), f32),
        pltpu.VMEM((5, ROWS, COLS), f32),
        pltpu.VMEM((messages, ROWS, COLS), f32),
        pltpu.SemaphoreType.DMA((8,)),
        pltpu.SemaphoreType.DMA((2, 8)),
        pltpu.SemaphoreType.DMA((messages,)),
        pltpu.SemaphoreType.DMA((messages,)),
        pltpu.SemaphoreType.DMA((8,)),
    ]
    shapes = (jax.ShapeDtypeStruct(tile, f32), jax.ShapeDtypeStruct((3,) + tile, f32))
    results = pl.pallas_call(
        functools.partial(kernel, sizes),
        out_shape=shapes,
        in_specs=[pl.BlockSpec(memory_space=pl.ANY)] * 8,
        out_specs=(vmem, vmem),
        scratch_shapes=scratch,
        compiler_params=pltpu.CompilerParams(
            collective_id=0, has_side_effects=True, vmem_limit_bytes=60 * 1024 * 1024
        ),
        name="sections_and_kick",
    )(*args)
    anywhere = pl.BlockSpec(memory_space=pl.ANY)
    return pl.pallas_call(
        hand_over,
        out_shape=shapes,
        in_specs=[anywhere] * 2,
        out_specs=(anywhere, anywhere),
        scratch_shapes=[
            pltpu.VMEM(tile, f32),
            pltpu.VMEM((3,) + tile, f32),
            pltpu.SemaphoreType.DMA((2,)),
            pltpu.SemaphoreType.DMA((2,)),
        ],
        compiler_params=pltpu.CompilerParams(vmem_limit_bytes=60 * 1024 * 1024),
        name="hand_over",
    )(*results)


def solution(mesh):
    n_gx, n_gy = mesh.shape["gx"], mesh.shape["gy"]
    n_hi = 4 if n_gy % 4 == 0 and n_gy > 4 else 2
    sizes = (n_gx, n_gy // n_hi, n_hi)
    cells = P("gy", "gx")
    one = P(None, "gy", "gx")
    many = P(None, None, "gy", "gx")
    return jax.shard_map(
        functools.partial(body, sizes),
        mesh=mesh,
        in_specs=(cells, many, many, one, one, one, one, many),
        out_specs=(one, many),
        check_vma=False,
    )
```

```python
import functools

import jax
import jax.numpy as jnp
from jax import lax
from jax.experimental import pallas as pl
from jax.experimental.pallas import tpu as pltpu
from jax.sharding import PartitionSpec as P

SECTIONS = 4
ISO_PART = 0.1
HEAT_RATIO = 5.0 / 3.0
COURANT = 0.3
ROOT_HALF = 0.5**0.5
MESH = pl.DeviceIdType.MESH

SLOTS = 16
ROWS = 8
COLS = 128
FLAT = SLOTS * ROWS

X, Y, Z, BX, BY, BZ, KA, F, M, VX, VY, VZ = range(12)
QUANTITIES = 12

DIRECTIONS = 4

CO, KE, WX, WY, WZ = range(5)
SELF_AT = DIRECTIONS * SLOTS * SLOTS
ROW_AT = SELF_AT + SLOTS * 8
COL_AT = ROW_AT + 6 * SLOTS * 2
PAIRS = COL_AT + 12

ROUNDS = 4
FIELD, DRAG = range(2)

EMPTY_Z = 10.0
OUTSIDE_X = 20.0
EDGE_Z = 40.0
PAD = 8

SIN = (0.9999999957157406, -0.1666665796974384, 0.008333050613415454, -0.0001980904606136566, 2.605165590448684e-06)
COS = (
    0.9999999997798981,
    -0.4999999935694129,
    0.04166663620835954,
    -0.001388836083517328,
    2.476013513307355e-05,
    -2.605106944029617e-07,
)


def section_polynomial(section_total):
    weight = 4.0 / (section_total * section_total + section_total - 2)
    series = [1.0 / 3.0, 1.0 / 3.0, 1.0 / 3.0]
    for j in range(3, section_total + 1):
        series.append((j * j + j - 2) / (2.0 * j * (j + 1)))

    def padded(values):
        return values + [0.0] * (section_total + 1 - len(values))

    before, now = padded([1.0]), padded([1.0, series[1] * weight])
    for j in range(2, section_total + 1):
        m = (2 * j - 1) / j * series[j] / series[j - 1]
        n = -(j - 1) / j * series[j] / series[j - 2]
        after = [m * a + n * b for a, b in zip(now, before)]
        after[0] += 1.0 - m - n
        after[1] -= (1.0 - series[j - 1]) * m * weight
        for k in range(section_total):
            after[k + 1] += m * weight * now[k]
        before, now = now, after
    return now


def horner(coefs, t):
    total = jnp.full_like(t, coefs[-1])
    for c in coefs[-2::-1]:
        total = total * t + c
    return total


def sin_cos(angle):
    half = 0.5 * angle
    t = half * half
    s = half * horner(SIN, t)
    c = horner(COS, t)
    return 2.0 * s * c, 1.0 - 2.0 * s * s


def pair_terms(i, j):
    dx, dy, dz = i[X] - j[X], i[Y] - j[Y], i[Z] - j[Z]
    s = jnp.maximum(1.0 - (dx * dx + dy * dy + dz * dz), 0.0)
    s2 = s * s
    own = i[BX] * dx + i[BY] * dy + i[BZ] * dz
    far = j[BX] * dx + j[BY] * dy + j[BZ] * dz
    co = (s2 * s) * (ISO_PART + (own * own + far * far)) * (i[KA] + j[KA])
    w = s2 * (i[M] * j[M])
    return co, w * s, w * dx, w * dy, w * dz


def kernel(
    sizes,
    pop_in,
    loc_in,
    tilt_in,
    mass_in,
    kappa_in,
    cap_in,
    temp_in,
    mot_in,
    heated,
    moved,
    pop,
    loc,
    tilt,
    mass,
    kappa,
    cap,
    temp,
    mot,
    far,
    powers,
    pfac,
    sfar,
    gfar,
    acc,
    accj,
    kacc,
    kaccj,
    store,
    rowsend0,
    rowrecv0,
    colsend0,
    colrecv0,
    cbsend,
    cbrecv,
    rowfar,
    colfar,
    colown,
    coltot,
    rsend,
    rrecv,
    vsend,
    vrecv,
    drecv,
    hs,
    cf,
    oc,
    msrc,
    mrecv,
    send_sem,
    recv_sem,
    msend_sem,
    mrecv_sem,
    load_sem,
):
    own, field, gfac = far.at[2], sfar.at[2], gfar.at[2]
    loads = [
        pltpu.make_async_copy(src, dst, load_sem.at[number])
        for number, (src, dst) in enumerate(
            (
                (pop_in, pop),
                (loc_in, loc),
                (tilt_in, tilt),
                (mass_in, mass),
                (kappa_in, kappa),
                (cap_in, cap),
                (temp_in, temp),
                (mot_in, mot),
            )
        )
    ]
    for load in loads:
        load.start()

    n_gx, n_lo, n_hi = sizes
    n_gy = n_lo * n_hi
    gx = lax.axis_index("gx")
    gy = lax.axis_index("gy")
    left, right = lax.rem(gx + n_gx - 1, n_gx), lax.rem(gx + 1, n_gx)
    up, down = lax.rem(gy + n_gy - 1, n_gy), lax.rem(gy + 1, n_gy)
    lo, hi = lax.rem(gy, n_lo), lax.div(gy, n_lo)

    around = ((gx, up), (gx, down), (left, gy), (right, gy), (left, up), (right, up), (left, down), (right, down))

    stage_size = (n_gx - 1, n_lo - 1, n_hi - 1)
    stage_at = (0, n_gx - 1, n_gx + n_lo - 2)

    def stage_device(stage, k):
        if stage == 0:
            return (lax.rem(gx + k + 1, n_gx), gy)
        if stage == 1:
            return (gx, hi * n_lo + lax.rem(lo + k + 1, n_lo))
        return (gx, lax.rem(hi + k + 1, n_hi) * n_lo + lo)

    def each(count, fn):
        def run(k, carry):
            fn(k)
            return carry

        lax.fori_loop(0, count, run, 0)

    def grouped(count, size, fn, carry):
        def run(k, carry):
            for a in range(size):
                carry = fn(k * size + a, carry)
            return carry

        return lax.fori_loop(0, count // size, run, carry)

    def over(fn, first, last, split):
        if first < split:
            lax.fori_loop(first, split, functools.partial(fn, 0), 0)
        if last > split:
            lax.fori_loop(max(first, split), last, functools.partial(fn, 1), 0)

    def paired(fn):
        def both(p):
            fn(2 * p)
            fn(2 * p + 1)

        each(SLOTS // 2, both)

    barrier = pltpu.get_barrier_semaphore()

    def greet(device):
        pl.semaphore_signal(barrier, inc=1, device_id=device, device_id_type=MESH)

    for device in around:
        greet(device)
    for stage in range(3):
        each(stage_size[stage], lambda k, stage=stage: greet(stage_device(stage, k)))

    lane = lax.broadcasted_iota(jnp.int32, (ROWS, COLS), 1)
    row = lax.broadcasted_iota(jnp.int32, (ROWS, COLS), 0)
    lane16 = lax.broadcasted_iota(jnp.int32, (SLOTS, COLS), 1)
    zero = jnp.zeros((ROWS, COLS), jnp.float32)
    rows_down = row.astype(jnp.float32)

    def at(p):
        start = p * ROWS
        return pl.ds(start if isinstance(p, int) else pl.multiple_of(start, ROWS), ROWS)

    def edge_row(side):
        return pl.ds(side * (ROWS - 1), SLOTS, stride=ROWS)

    def half(a):
        return pl.ds(a * 8, 8)

    def partner(q, off):
        return pl.ds(q * ROWS + off, ROWS)

    def slot_sum(q):
        start = PAD + q * ROWS
        return pl.ds(start if isinstance(q, int) else pl.multiple_of(start, ROWS), ROWS)

    def put_copies(target, k, p, value):
        target[(0, *k, at(p))] = pltpu.roll(value, COLS - 1, 1)
        target[(1, *k, at(p))] = pltpu.roll(value, 1, 1)
        target[(2, *k, at(p))] = value

    def gather(v, index):
        return jnp.take_along_axis(v, index, axis=1)

    def packed_columns(tile_of):
        v = tile_of(0)
        for p in range(1, SLOTS):
            mask = (lane == 8 * p) | (lane == 8 * p - 1)
            v = jnp.where(mask, pltpu.roll(tile_of(p), 8 * p, 1), v)
        return v

    group = lane & ~7
    within = (lane & 7) * 8
    own_index = (group, (group + (COLS - 1)) & (COLS - 1))
    far_index = (
        ((within + (COLS - 1)) & (COLS - 1), (within + 63) & (COLS - 1)),
        (within, within + 64),
    )

    def prepare(p, fastest):
        live = p < pop[...]
        sin_p, cos_p = sin_cos(tilt[0, p])
        sin_a, cos_a = sin_cos(tilt[1, p])
        t = temp[p]
        v = [mot[c, p] for c in range(3)]
        values = [
            loc[0, p],
            loc[1, p] + rows_down,
            jnp.where(live, loc[2, p], EMPTY_Z),
            ROOT_HALF * (sin_p * cos_a),
            ROOT_HALF * (sin_p * sin_a),
            ROOT_HALF * cos_p,
            0.5 * kappa[p],
            t,
            mass[p],
        ] + v
        for k in range(QUANTITIES):
            own[k, at(p), :] = values[k]
        for c in range(2):
            acc[c, at(p), :] = zero
        for c in range(3):
            kacc[c, at(p), :] = zero
        speed = jnp.sqrt(HEAT_RATIO * (HEAT_RATIO - 1.0) * t) + jnp.sqrt(v[0] * v[0] + v[1] * v[1] + v[2] * v[2])
        return jnp.maximum(fastest, jnp.where(live, speed, 0.0))

    after = pl.ds(FLAT, PAD)
    for copy in range(3):
        for k in range(QUANTITIES):
            far[copy, k, after, :] = zero
        sfar[copy, after, :] = zero
        gfar[copy, after, :] = zero
    for d in range(DIRECTIONS):
        for c in range(2):
            accj[d, c, pl.ds(0, PAD), :] = zero
        for c in range(3):
            kaccj[d, c, pl.ds(0, PAD), :] = zero
    for load in loads:
        load.wait()
    msrc[0] = grouped(SLOTS, 4, prepare, zero)

    def pack(k, cb):
        cb = list(cb)
        for side in range(2):
            packed = own[k, edge_row(side), :]
            rowsend0[side, k] = packed
            mask = (lane16 == 2 * k) | (lane16 == 2 * k + 1)
            cb[side] = jnp.where(mask, pltpu.roll(packed, 2 * k + 1, 1), cb[side])
        colsend0[k] = packed_columns(lambda p: own[k, at(p), :])
        return tuple(cb)

    blank = jnp.zeros((SLOTS, COLS), jnp.float32)
    cbsend[0], cbsend[1] = grouped(QUANTITIES, 3, pack, (blank, blank))

    def remote(src, dst, s, r, device):
        return pltpu.make_async_remote_copy(
            src_ref=src, dst_ref=dst, send_sem=s, recv_sem=r, device_id=device, device_id_type=MESH
        )

    def stage_copy(stage, k):
        slot = stage_at[stage] + k
        return remote(
            msrc.at[stage], mrecv.at[slot], msend_sem.at[slot], mrecv_sem.at[slot], stage_device(stage, k)
        )

    def stage_start(stage):
        each(stage_size[stage], lambda k: stage_copy(stage, k).start())

    def stage_finish(stage):
        def take(k, best):
            stage_copy(stage, k).wait_recv()
            return jnp.maximum(best, mrecv[stage_at[stage] + k])

        msrc[stage + 1] = lax.fori_loop(0, stage_size[stage], take, msrc[stage])

    def opening_copies():
        plan = (
            (rowsend0.at[0], rowrecv0.at[1]),
            (rowsend0.at[1], rowrecv0.at[0]),
            (colsend0, colrecv0.at[1]),
            (colsend0, colrecv0.at[0]),
            (cbsend.at[0], cbrecv.at[3]),
            (cbsend.at[0], cbrecv.at[2]),
            (cbsend.at[1], cbrecv.at[1]),
            (cbsend.at[1], cbrecv.at[0]),
        )
        return [
            remote(src, dst, send_sem.at[c], recv_sem.at[1, c], around[c])
            for c, (src, dst) in enumerate(plan)
        ]

    def round_copies(e):
        kinds = pl.ds(0, 2 if e == 0 else 1)
        plan = (
            (rsend.at[e, 0, kinds], rrecv.at[e, 1, kinds]),
            (rsend.at[e, 1, kinds], rrecv.at[e, 0, kinds]),
            (vsend.at[e, kinds], vrecv.at[e, 1, kinds]),
            (vsend.at[e, kinds], vrecv.at[e, 0, kinds]),
            (rsend.at[e, 0, kinds], drecv.at[e, 3, kinds]),
            (rsend.at[e, 0, kinds], drecv.at[e, 2, kinds]),
            (rsend.at[e, 1, kinds], drecv.at[e, 1, kinds]),
            (rsend.at[e, 1, kinds], drecv.at[e, 0, kinds]),
        )
        return [
            remote(src, dst, send_sem.at[c], recv_sem.at[e % 2, c], around[c]) for c, (src, dst) in enumerate(plan)
        ]

    pl.semaphore_wait(barrier, len(around) + sum(stage_size))
    for copy in opening_copies():
        copy.start()
    stage_start(0)

    PASS1 = range(9)

    def put(index, terms):
        for c in range(5):
            store[c, index] = terms[c]

    def first_self(p, carry):
        mine = [own[k, at(p), :] for k in PASS1]
        ti, ri = zero, zero
        for step in range(1, 9):
            q = lax.rem(p + step, SLOTS)
            other = [own[k, at(q), :] for k in PASS1]
            terms = pair_terms(mine, other)
            put(SELF_AT + p * 8 + (step - 1), terms)
            t = terms[CO] * (other[F] - mine[F])
            ti = ti + t
            ri = ri + terms[KE]
            if step < 8:
                acc[0, at(q), :] -= t
                acc[1, at(q), :] += terms[KE]
        acc[0, at(p), :] += ti
        acc[1, at(p), :] += ri
        for k in range(QUANTITIES):
            value = own[k, at(p), :]
            east, west = pltpu.roll(value, COLS - 1, 1), pltpu.roll(value, 1, 1)
            if k == X:
                east = jnp.where(lane == COLS - 1, OUTSIDE_X, east + 1.0)
                west = jnp.where(lane == 0, OUTSIDE_X, west - 1.0)
            far[0, k, at(p), :] = east
            far[1, k, at(p), :] = west
        for d in range(DIRECTIONS):
            for c in range(2):
                accj[d, c, slot_sum(p), :] = zero
            for c in range(3):
                kaccj[d, c, slot_sum(p), :] = zero
        return carry

    def first_dirs(off, n, carry):
        d = lax.div(n, 8)
        p0 = lax.rem(n, 8) * 2
        mine = [[own[k, at(p0 + a), :] for k in PASS1] for a in range(2)]
        ti = [zero, zero]
        ri = [zero, zero]
        for q in range(SLOTS):
            other = [far[lax.rem(d, 3), k, partner(q, off), :] for k in PASS1]
            tj, rj = None, None
            for a in range(2):
                terms = pair_terms(mine[a], other)
                put(d * 256 + (p0 + a) * 16 + q, terms)
                t, r = terms[CO] * (other[F] - mine[a][F]), terms[KE]
                ti[a] = ti[a] + t
                ri[a] = ri[a] + r
                tj = t if tj is None else tj + t
                rj = r if rj is None else rj + r
            accj[d, 0, slot_sum(q), :] -= tj
            accj[d, 1, slot_sum(q), :] += rj
        for a in range(2):
            acc[0, at(p0 + a), :] += ti[a]
            acc[1, at(p0 + a), :] += ri[a]
        return carry

    lax.fori_loop(0, SLOTS, first_self, 0)
    over(first_dirs, 0, 32, 8)
    stage_finish(0)
    stage_start(1)

    for copy in opening_copies():
        copy.wait_recv()

    def rows_around(k, carry):
        for side in range(2):
            h = rowrecv0[side, k]
            cl = pltpu.roll(cbrecv[side * 2], lax.rem(COLS - 2 * k, COLS), 1)
            cr = pltpu.roll(cbrecv[side * 2 + 1], COLS - 2 - 2 * k, 1)
            rowfar[side * 3, k] = jnp.where(lane16 == 0, cl, pltpu.roll(h, 1, 1))
            rowfar[side * 3 + 1, k] = h
            rowfar[side * 3 + 2, k] = jnp.where(lane16 == COLS - 1, cr, pltpu.roll(h, COLS - 1, 1))
            colown[side, k] = gather(colsend0[k], own_index[side])
            for h in range(2):
                v = gather(colrecv0[side, k], far_index[side][h])
                for number, value in enumerate((pltpu.roll(v, 1, 0), v, pltpu.roll(v, ROWS - 1, 0))):
                    colfar[side * 6 + number * 2 + h, k] = value
        return carry

    grouped(QUANTITIES, 4, rows_around, 0)

    z_side = (jnp.where(gy == 0, EDGE_Z, 0.0), jnp.where(gy == n_gy - 1, EDGE_Z, 0.0))
    z_end = (jnp.where(gx == 0, EDGE_Z, 0.0), jnp.where(gx == n_gx - 1, EDGE_Z, 0.0))
    z_lane = (
        jnp.where(lane16 == 0, z_end[0], 0.0),
        jnp.zeros((SLOTS, COLS), jnp.float32),
        jnp.where(lane16 == COLS - 1, z_end[1], 0.0),
    )
    for side in range(2):
        for number in range(3):
            c = side * 3 + number
            if number != 1:
                rowfar[c, X] = rowfar[c, X] + float(number - 1)
            rowfar[c, Y] = rowfar[c, Y] + float(-ROWS if side == 0 else ROWS)
            rowfar[c, Z] = rowfar[c, Z] + (z_lane[number] + z_side[side])
            for h in range(2):
                c = side * 6 + number * 2 + h
                colfar[c, X] = colfar[c, X] + (-1.0 if side == 0 else 1.0)
                colfar[c, Z] = colfar[c, Z] + z_end[side]

    def scatter_rows(target, c, side, halves):
        target[c, edge_row(side), :] = target[c, edge_row(side), :] + jnp.concatenate(halves, axis=0)

    def group_sum(v):
        v = v + pltpu.roll(v, COLS - 1, 1)
        v = v + pltpu.roll(v, COLS - 2, 1)
        return v + pltpu.roll(v, COLS - 4, 1)

    ends = (lane == 0) | (lane == COLS - 1)

    def scatter_columns(target, count):
        combined = []
        for c in range(count):
            u = jnp.where((lane & 7) == 0, group_sum(coltot[0, c]), 0.0)
            combined.append(jnp.where((lane & 7) == 7, pltpu.roll(group_sum(coltot[1, c]), COLS - 1, 1), u))

        def add(p):
            for c in range(count):
                v = pltpu.roll(combined[c], (COLS - 8 * p) % COLS, 1) if p else combined[c]
                target[c, at(p), :] += jnp.where(ends, v, 0.0)

        for p in range(SLOTS):
            add(p)

    def rim(target, count, row_mine, row_terms, col_mine, col_terms):
        def one_side(side):
            mine = row_mine(side)

            def one_row(number, totals):
                total = list(totals)
                c = side * 3 + number
                for q in range(SLOTS):
                    add = row_terms(c, q, mine)
                    for a in range(2):
                        for x, e in enumerate(add(a, ROW_AT + (c * 16 + q) * 2 + a)):
                            total[a * count + x] = total[a * count + x] + e
                return tuple(total)

            total = (zero,) * (2 * count)
            if count == 1:
                for number in range(3):
                    total = one_row(number, total)
            else:
                total = lax.fori_loop(0, 3, one_row, total)
            for x in range(count):
                scatter_rows(target, x, side, [total[x], total[count + x]])

            mine_col = col_mine(side)

            def one_column(number, totals):
                c = side * 6 + number
                return tuple(t + e for t, e in zip(totals, col_terms(c, mine_col, COL_AT + c)))

            total = (zero,) * count
            for number in range(6):
                total = one_column(number, total)
            for x in range(count):
                coltot[side, x] = total[x]

        for side in range(2):
            one_side(side)
        scatter_columns(target, count)

    def first_terms(mine, other, index):
        terms = pair_terms(mine, other)
        put(index, terms)
        return terms[CO] * (other[F] - mine[F]), terms[KE]

    def first_row(c, q, mine):
        other = [rowfar[c, k, pl.ds(q, 1), :] for k in PASS1]
        return lambda a, index: first_terms(mine[a], other, index)

    rim(
        acc,
        2,
        lambda side: [[rowsend0[side, k, half(a), :] for k in PASS1] for a in range(2)],
        first_row,
        lambda side: [colown[side, k] for k in PASS1],
        lambda c, mine, index: first_terms(mine, [colfar[c, k] for k in PASS1], index),
    )
    def total_of(target, per_dir, c, p):
        below = pl.ds(PAD + p * ROWS - 1, ROWS)
        east = per_dir[0, c, slot_sum(p), :] + per_dir[3, c, below, :]
        west = per_dir[1, c, below, :]
        total = target[c, at(p), :] + per_dir[2, c, below, :]
        return total + pltpu.roll(east, 1, 1) + pltpu.roll(west, COLS - 1, 1)

    def clear(p):
        acc[0, at(p), :] = zero
        for d in range(DIRECTIONS):
            accj[d, 0, slot_sum(p), :] = zero

    def set_field(p, value):
        put_copies(sfar, (), p, value)

    def first_update(p):
        live = p < pop[...]
        m = own[M, at(p), :]
        density = jnp.where(live, m + total_of(acc, accj, 1, p) / m, 1.0)
        inverse = 1.0 / density
        g = ROOT_HALF * inverse
        put_copies(gfar, (), p, g)
        pfac[p] = 6.0 * (HEAT_RATIO - 1.0) * inverse
        u = jnp.where(live, total_of(acc, accj, 0, p) / cap[p], 0.0)
        powers[0, p] = u
        set_field(p, u)

    for p in range(SLOTS):
        first_update(p)
    for p in range(SLOTS):
        clear(p)

    def section_dirs(off, n, carry):
        d = lax.div(n, 2)
        p0 = lax.rem(n, 2) * 8
        mine = [field[at(p0 + a), :] for a in range(8)]
        ti = [zero] * 8
        for q in range(SLOTS):
            other = sfar[lax.rem(d, 3), partner(q, off), :]
            tj = None
            for a in range(8):
                t = store[CO, d * 256 + (p0 + a) * 16 + q] * (other - mine[a])
                ti[a] = ti[a] + t
                tj = t if tj is None else tj + t
            accj[d, 0, slot_sum(q), :] -= tj
        for a in range(8):
            acc[0, at(p0 + a), :] += ti[a]
        return carry

    def wrap(p):
        return p % SLOTS if isinstance(p, int) else lax.rem(p, SLOTS)

    def self_partners(p):
        for step in range(1, 9):
            yield wrap(p + step), SELF_AT + p * 8 + (step - 1), False
        for step in range(1, 8):
            q = wrap(p + SLOTS - step)
            yield q, SELF_AT + q * 8 + (step - 1), True

    def section_self(p):
        mine = field[at(p), :]
        ti = zero
        for q, index, _ in self_partners(p):
            ti = ti + store[CO, index] * (field[at(q), :] - mine)
        acc[0, at(p), :] += ti

    def section_row(c, q, mine):
        other = hs[FIELD, c, pl.ds(q, 1), :]
        return lambda a, index: (store[CO, index] * (other - mine[a]),)

    def drag_dirs(off, n, carry):
        d = lax.div(n, 4)
        p0 = lax.rem(n, 4) * 4
        g = [gfac[at(p0 + a), :] for a in range(4)]
        v = [[own[VX + c, at(p0 + a), :] for c in range(3)] for a in range(4)]
        total = [[zero] * 3 for _ in range(4)]
        for q in range(SLOTS):
            gj = gfar[lax.rem(d, 3), partner(q, off), :]
            vj = [far[lax.rem(d, 3), VX + c, partner(q, off), :] for c in range(3)]
            back = [None] * 3
            for a in range(4):
                w = store[KE, d * 256 + (p0 + a) * 16 + q] * (g[a] * gj)
                for c in range(3):
                    e = w * (vj[c] - v[a][c])
                    total[a][c] = total[a][c] + e
                    back[c] = e if back[c] is None else back[c] + e
            for c in range(3):
                kaccj[d, c, slot_sum(q), :] -= back[c]
        for a in range(4):
            for c in range(3):
                kacc[c, at(p0 + a), :] += total[a][c]
        return carry

    def drag_self(p):
        g = gfac[at(p), :]
        v = [own[VX + c, at(p), :] for c in range(3)]
        total = [zero] * 3
        for q, index, _ in self_partners(p):
            w = store[KE, index] * (g * gfac[at(q), :])
            for c in range(3):
                total[c] = total[c] + w * (own[VX + c, at(q), :] - v[c])
        for c in range(3):
            kacc[c, at(p), :] += total[c]

    def drag_row(c, q, mine):
        g, v = mine
        gj = hs[DRAG, c, pl.ds(q, 1), :]
        vj = [rowfar[c, VX + x, pl.ds(q, 1), :] for x in range(3)]

        def terms(a, index):
            w = store[KE, index] * (g[a] * gj)
            return [w * (vj[x] - v[a][x]) for x in range(3)]

        return terms

    def drag_column(c, mine, index):
        g, v = mine
        w = store[KE, index] * (g * cf[DRAG, c])
        return [w * (colfar[c, VX + x] - v[x]) for x in range(3)]

    def drag_rim():
        rim(
            kacc,
            3,
            lambda side: (
                [rsend[0, side, DRAG, half(a), :] for a in range(2)],
                [[rowsend0[side, VX + x, half(a), :] for x in range(3)] for a in range(2)],
            ),
            drag_row,
            lambda side: (oc[DRAG, side], [colown[side, VX + x] for x in range(3)]),
            drag_column,
        )

    def push_dirs(off, n, carry):
        d = lax.div(n, 4)
        p0 = lax.rem(n, 4) * 4
        pi = [field[at(p0 + a), :] for a in range(4)]
        total = [[zero] * 3 for _ in range(4)]
        for q in range(SLOTS):
            pj = sfar[lax.rem(d, 3), partner(q, off), :]
            back = [None] * 3
            for a in range(4):
                both = pi[a] + pj
                for c in range(3):
                    e = both * store[WX + c, d * 256 + (p0 + a) * 16 + q]
                    total[a][c] = total[a][c] + e
                    back[c] = e if back[c] is None else back[c] + e
            for c in range(3):
                kaccj[d, c, slot_sum(q), :] -= back[c]
        for a in range(4):
            for c in range(3):
                kacc[c, at(p0 + a), :] += total[a][c]
        return carry

    def push_self(p):
        pi = field[at(p), :]
        total = [zero] * 3
        for q, index, reverse in self_partners(p):
            both = pi + field[at(q), :]
            for c in range(3):
                e = both * store[WX + c, index]
                total[c] = total[c] - e if reverse else total[c] + e
        for c in range(3):
            kacc[c, at(p), :] += total[c]

    def push_row(c, q, mine):
        pj = hs[FIELD, c, pl.ds(q, 1), :]

        def terms(a, index):
            both = mine[a] + pj
            return [both * store[WX + x, index] for x in range(3)]

        return terms

    def push_column(c, mine, index):
        both = mine + cf[FIELD, c]
        return [both * store[WX + x, index] for x in range(3)]

    for side in range(2):
        packed = gfac[edge_row(side), :]
        rsend[0, side, DRAG] = packed
    packed = packed_columns(lambda p: gfac[at(p), :])
    vsend[0, DRAG] = packed

    polynomial = section_polynomial(SECTIONS)

    def spread(e, kind):
        for side in range(2):
            h = rrecv[e, side, kind]
            hl, hr = drecv[e, side * 2, kind], drecv[e, side * 2 + 1, kind]
            hs[kind, side * 3] = pltpu.roll(jnp.where(lane16 == COLS - 1, hl, h), 1, 1)
            hs[kind, side * 3 + 1] = h
            hs[kind, side * 3 + 2] = pltpu.roll(jnp.where(lane16 == 0, hr, h), COLS - 1, 1)
            oc[kind, side] = gather(vsend[e, kind], own_index[side])
            for h in range(2):
                v = gather(vrecv[e, side, kind], far_index[side][h])
                for number, value in enumerate((pltpu.roll(v, 1, 0), v, pltpu.roll(v, ROWS - 1, 0))):
                    cf[kind, side * 6 + number * 2 + h] = value

    def one_round(e):
        for side in range(2):
            rsend[e, side, FIELD] = field[edge_row(side), :]
        vsend[e, FIELD] = packed_columns(lambda p: field[at(p), :])
        for copy in round_copies(e - 1) if e else opening_copies():
            copy.wait_send()
        for copy in round_copies(e):
            copy.start()

        if e < 3:
            over(section_dirs, 0, 8, 2)
            for p in range(SLOTS):
                section_self(p)

        if e == 0:
            paired(drag_self)

        if e == 2:
            drag_rim()

        if e < 3:
            over(drag_dirs, (0, 4, 10)[e], (4, 10, 16)[e], 4)

        if e == 3:
            over(push_dirs, 0, 16, 4)
            for p in range(SLOTS):
                push_self(p)

        if e == 0:
            stage_finish(1)
            stage_start(2)
        if e == 2:
            stage_finish(2)
            best = msrc[3]
            for shift in (4, 2, 1):
                best = jnp.maximum(best, pltpu.roll(best, shift, 0))
            for shift in (64, 32, 16, 8, 4, 2, 1):
                best = jnp.maximum(best, pltpu.roll(best, shift, 1))
            msrc[4] = COURANT / best

        for copy in round_copies(e):
            copy.wait_recv()
        for kind in range(2 if e == 0 else 1):
            spread(e, kind)

        if e < 3:
            rim(
                acc,
                1,
                lambda side: [rsend[e, side, FIELD, half(a), :] for a in range(2)],
                section_row,
                lambda side: oc[FIELD, side],
                lambda c, mine, index: (store[CO, index] * (cf[FIELD, c] - mine),),
            )

        def power(p):
            return jnp.where(p < pop[...], total_of(acc, accj, 0, p) / cap[p], 0.0)

        if e < 2:

            def update(p):
                u = power(p)
                powers[e + 1, p] = u
                set_field(p, u)

            for p in range(SLOTS):
                update(p)
            for p in range(SLOTS):
                clear(p)

        if e == 2:
            step_dt = msrc[4]

            def update(p):
                y = step_dt * (polynomial[4] * power(p))
                for k in (3, 2, 1):
                    y = step_dt * (polynomial[k] * powers[k - 1, p] + y)
                y = polynomial[0] * own[F, at(p), :] + y
                heated[p] = y
                set_field(p, pfac[p] * y)

            for p in range(SLOTS):
                update(p)

        if e == 3:
            rim(
                kacc,
                3,
                lambda side: [rsend[e, side, FIELD, half(a), :] for a in range(2)],
                push_row,
                lambda side: oc[FIELD, side],
                push_column,
            )

    for e in range(ROUNDS):
        one_round(e)

    def finish(p):
        live = p < pop[...]
        scale = jnp.where(live, msrc[4] / own[M, at(p), :], 0.0)
        for c in range(3):
            moved[c, p] = own[VX + c, at(p), :] + scale * total_of(kacc, kaccj, c, p)

    for p in range(SLOTS):
        finish(p)

    for copy in round_copies(ROUNDS - 1):
        copy.wait_send()
    for stage in range(3):
        each(stage_size[stage], lambda k, stage=stage: stage_copy(stage, k).wait_send())


def hand_over(heated_in, moved_in, heated, moved, heated_here, moved_here, in_sem, out_sem):
    ways = ((heated_in, heated_here, heated), (moved_in, moved_here, moved))
    loads = [pltpu.make_async_copy(src, here, in_sem.at[k]) for k, (src, here, _) in enumerate(ways)]
    stores = [pltpu.make_async_copy(here, dst, out_sem.at[k]) for k, (_, here, dst) in enumerate(ways)]
    for load in loads:
        load.start()
    for load, store in zip(loads, stores):
        load.wait()
        store.start()
    for store in stores:
        store.wait()


def body(sizes, *args):
    f32 = jnp.float32
    messages = sum(sizes) - 3
    tile = (SLOTS, ROWS, COLS)
    vmem = pl.BlockSpec(memory_space=pltpu.VMEM)
    scratch = [pltpu.VMEM(a.shape, a.dtype) for a in args] + [
        pltpu.VMEM((3, QUANTITIES, FLAT + PAD, COLS), f32),
        pltpu.VMEM((3,) + tile, f32),
        pltpu.VMEM(tile, f32),
        pltpu.VMEM((3, FLAT + PAD, COLS), f32),
        pltpu.VMEM((3, FLAT + PAD, COLS), f32),
        pltpu.VMEM((2, FLAT, COLS), f32),
        pltpu.VMEM((DIRECTIONS, 2, PAD + FLAT, COLS), f32),
        pltpu.VMEM((3, FLAT, COLS), f32),
        pltpu.VMEM((DIRECTIONS, 3, PAD + FLAT, COLS), f32),
        pltpu.VMEM((5, PAIRS, ROWS, COLS), f32),
        pltpu.VMEM((2, QUANTITIES, SLOTS, COLS), f32),
        pltpu.VMEM((2, QUANTITIES, SLOTS, COLS), f32),
        pltpu.VMEM((QUANTITIES, ROWS, COLS), f32),
        pltpu.VMEM((2, QUANTITIES, ROWS, COLS), f32),
        pltpu.VMEM((2, SLOTS, COLS), f32),
        pltpu.VMEM((4, SLOTS, COLS), f32),
        pltpu.VMEM((6, QUANTITIES, SLOTS, COLS), f32),
        pltpu.VMEM((12, QUANTITIES, ROWS, COLS), f32),
        pltpu.VMEM((2, QUANTITIES, ROWS, COLS), f32),
        pltpu.VMEM((2, 3, ROWS, COLS), f32),
        pltpu.VMEM((ROUNDS, 2, 2, SLOTS, COLS), f32),
        pltpu.VMEM((ROUNDS, 2, 2, SLOTS, COLS), f32),
        pltpu.VMEM((ROUNDS, 2, ROWS, COLS), f32),
        pltpu.VMEM((ROUNDS, 2, 2, ROWS, COLS), f32),
        pltpu.VMEM((ROUNDS, 4, 2, SLOTS, COLS), f32),
        pltpu.VMEM((2, 6, SLOTS, COLS), f32),
        pltpu.VMEM((2, 12, ROWS, COLS), f32),
        pltpu.VMEM((2, 2, ROWS, COLS), f32),
        pltpu.VMEM((5, ROWS, COLS), f32),
        pltpu.VMEM((messages, ROWS, COLS), f32),
        pltpu.SemaphoreType.DMA((8,)),
        pltpu.SemaphoreType.DMA((2, 8)),
        pltpu.SemaphoreType.DMA((messages,)),
        pltpu.SemaphoreType.DMA((messages,)),
        pltpu.SemaphoreType.DMA((8,)),
    ]
    shapes = (jax.ShapeDtypeStruct(tile, f32), jax.ShapeDtypeStruct((3,) + tile, f32))
    results = pl.pallas_call(
        functools.partial(kernel, sizes),
        out_shape=shapes,
        in_specs=[pl.BlockSpec(memory_space=pl.ANY)] * 8,
        out_specs=(vmem, vmem),
        scratch_shapes=scratch,
        compiler_params=pltpu.CompilerParams(
            collective_id=0, has_side_effects=True, vmem_limit_bytes=60 * 1024 * 1024
        ),
        name="sections_and_kick",
    )(*args)
    anywhere = pl.BlockSpec(memory_space=pl.ANY)
    return pl.pallas_call(
        hand_over,
        out_shape=shapes,
        in_specs=[anywhere] * 2,
        out_specs=(anywhere, anywhere),
        scratch_shapes=[
            pltpu.VMEM(tile, f32),
            pltpu.VMEM((3,) + tile, f32),
            pltpu.SemaphoreType.DMA((2,)),
            pltpu.SemaphoreType.DMA((2,)),
        ],
        compiler_params=pltpu.CompilerParams(vmem_limit_bytes=60 * 1024 * 1024),
        name="hand_over",
    )(*results)


def solution(mesh):
    n_gx, n_gy = mesh.shape["gx"], mesh.shape["gy"]
    n_hi = 4 if n_gy % 4 == 0 and n_gy > 4 else 2
    sizes = (n_gx, n_gy // n_hi, n_hi)
    cells = P("gy", "gx")
    one = P(None, "gy", "gx")
    many = P(None, None, "gy", "gx")
    return jax.shard_map(
        functools.partial(body, sizes),
        mesh=mesh,
        in_specs=(cells, many, many, one, one, one, one, many),
        out_specs=(one, many),
        check_vma=False,
    )
```
